32 devices in a mesh: clip: 8 (over z, y), frame: 4 (over x, core).
Axes of the slice: x: 2, y: 2, z: 4, core: 2. Of those that a mesh axis runs over, the one named last changes fastest.
Arguments:
- clips_in: bfloat16 [8, 8, 20, 20, 320], P('clip', 'frame'), may hold values from -6 to 6
- out_grad: bfloat16 [8, 8, 20, 20, 320], P('clip', 'frame'), may hold values from -6 to 6
- clip_side: int32 [8], P('clip'), may hold values from 14 to 20, as said below
- qkv_weight: float32 [960, 320], P('frame'), may hold values from -0.3125 to 0.3125
- proj_weight: float32 [320, 320], P('frame'), may hold values from -6 to 6
- up_weight: float32 [1280, 320], P('frame'), may hold values from -0.3125 to 0.3125
- down_weight: float32 [1280, 320], P('frame'), may hold values from -0.15625 to 0.15625
- qkv_moment: float32 [960, 320], P('frame'), may hold values from -512 to 512
- proj_moment: float32 [320, 320], P('frame'), may hold values from -512 to 512
- up_moment: float32 [1280, 320], P('frame'), may hold values from -512 to 512
- down_moment: float32 [1280, 320], P('frame'), may hold values from -512 to 512
- vectors: float32 [9, 320], replicated
- vector_mean: float32 [9, 320], replicated, may hold values from -48 to 48
- vector_square: float32 [9, 320], replicated, may hold values from 5.12 to 51.2
- up_bias: float32 [1280], replicated, may hold values from -3 to 3
- up_bias_mean: float32 [1280], replicated, may hold values from -48 to 48
- up_bias_square: float32 [1280], replicated, may hold values from 5.12 to 51.2
- conv_kernel: float32 [27, 320], replicated, may hold values from -1.25 to 1.25
- kernel_mean: float32 [27, 320], replicated, may hold values from -48 to 48
- kernel_square: float32 [27, 320], replicated, may hold values from 5.12 to 51.2
Outputs:
- block_out: bfloat16 [8, 8, 20, 20, 320], P('clip', 'frame')
- input_grad: float32 [8, 8, 20, 20, 320], P('clip', 'frame')
- qkv_moment_new: float32 [960, 320], P('frame')
- qkv_weight_new: float32 [960, 320], P('frame')
- proj_moment_new: float32 [320, 320], P('frame')
- proj_weight_new: float32 [320, 320], P('frame')
- up_moment_new: float32 [1280, 320], P('frame')
- up_weight_new: float32 [1280, 320], P('frame')
- down_moment_new: float32 [1280, 320], P('frame')
- down_weight_new: float32 [1280, 320], P('frame')
- vector_mean_new: float32 [9, 320], replicated
- vector_square_new: float32 [9, 320], replicated
- vectors_new: float32 [9, 320], replicated
- up_bias_mean_new: float32 [1280], replicated
- up_bias_square_new: float32 [1280], replicated
- up_bias_new: float32 [1280], replicated
- kernel_mean_new: float32 [27, 320], replicated
- kernel_square_new: float32 [27, 320], replicated
- kernel_new: float32 [27, 320], replicated
The draws below stay inside these ranges and needn't reach their ends.
Inputs may be any that keep to these rules, and one draw needn't show every extreme that they name: `clip_side`: each entry is 14 or 20; both occur in every draw.
All inputs are finite; a program needn't handle non-finite values.
Results may differ from the reference program's by a relative error of at most 0.009.
The reference program's roundings to bfloat16 on the way count: a program that leaves them out, or rounds other values in their place, can miss the bound.
Values may be sent and summed in bfloat16 or wider, within the bound.
A program may use at most 128 MiB of HBM per device.

```python
import math
import jax
import jax.numpy as jnp
from jax import lax

D = 320
HEADS = 5
HEAD_DIM = 64
FF = 1280
FRAMES = 8
SIDE = 20
SMALL_SIDE = 14
QBLOCKS = 5
NS_STEPS = 5
STEP = 10
CLIPS = 8
CLIP_TOK = 3200
TOKENS = 25600


def draw_clip_side(key, part):
    key = jax.random.fold_in(key, 11)
    pick_key, first_key, gap_key = jax.random.split(key, 3)
    large_pick = jax.random.randint(pick_key, (CLIPS,), 0, 8) == 0
    side_list = jnp.where(large_pick, SIDE, SMALL_SIDE).astype(jnp.int32)
    first_at = jax.random.randint(first_key, (), 0, CLIPS)
    gap_len = jax.random.randint(gap_key, (), 1, CLIPS)
    side_list = side_list.at[first_at].set(SIDE)
    side_list = side_list.at[(first_at + gap_len) % CLIPS].set(SMALL_SIDE)
    return side_list.astype(jnp.int32)


def draw_vectors(key, part):
    key = jax.random.fold_in(key, 37)
    noise_vals = jax.random.truncated_normal(key, -3.0, 3.0, (9, D), jnp.float32) * 0.2
    row_ids = jnp.arange(9, dtype=jnp.int32)[:, None]
    gain_rows = ((row_ids == 0) | (row_ids == 2)).astype(jnp.float32)
    return gain_rows + noise_vals


def level_of(key, extent, pieces, smallest, top_value):
    loudness = 1.0
    for dim, blocks in pieces:
        heights = jax.random.uniform(jax.random.fold_in(jax.random.fold_in(key, 6), dim), (blocks,), jnp.float32, smallest / len(pieces), top_value / len(pieces))
        loudness = loudness * jnp.repeat(jnp.exp(heights), extent[dim] // blocks).reshape((-1,) + (1,) * (len(extent) - 1 - dim))
    return loudness


def scatter_about(key, extent, spread, reach, shards=(), held_as=jnp.bfloat16):
    drawn = spread * jax.random.normal(key, extent, jnp.float32)
    if shards:
        drawn = drawn * level_of(key, extent, shards, -0.22, 0.18)
    return jnp.clip(drawn, -reach, reach).astype(held_as)


def setup_inputs(seed: int = 0) -> dict:
    arg_keys = jax.random.split(jax.random.key(seed), 21)
    clips_in = scatter_about(arg_keys[0], (CLIPS, FRAMES, SIDE, SIDE, D), 1.0, 6.0, ((0, 8), (1, 4)))
    out_grad = scatter_about(arg_keys[1], (CLIPS, FRAMES, SIDE, SIDE, D), 1.0, 6.0, ((0, 8), (1, 4)))
    clip_side = draw_clip_side(jax.random.fold_in(arg_keys[20], 71), 0)
    qkv_weight = scatter_about(arg_keys[3], (3 * D, D), D ** -0.5, 0.3125, ((0, 4),), jnp.float32)
    proj_weight = scatter_about(arg_keys[4], (D, D), (0.6 * CLIP_TOK ** 0.5 * D ** -0.5), 6.0, ((0, 4),), jnp.float32)
    up_weight = scatter_about(arg_keys[5], (FF, D), D ** -0.5, 0.3125, ((0, 4),), jnp.float32)
    down_weight = scatter_about(arg_keys[6], (FF, D), FF ** -0.5, 0.15625, ((0, 4),), jnp.float32)
    qkv_moment = scatter_about(arg_keys[7], (3 * D, D), (0.5 * TOKENS ** 0.5), 512.0, ((0, 4),), jnp.float32)
    proj_moment = scatter_about(arg_keys[8], (D, D), (0.5 * TOKENS ** 0.5), 512.0, ((0, 4),), jnp.float32)
    up_moment = scatter_about(arg_keys[9], (FF, D), (0.5 * TOKENS ** 0.5), 512.0, ((0, 4),), jnp.float32)
    down_moment = scatter_about(arg_keys[10], (FF, D), (0.5 * TOKENS ** 0.5), 512.0, ((0, 4),), jnp.float32)
    vectors = draw_vectors(jax.random.fold_in(arg_keys[20], 71), 0)
    vector_mean = scatter_about(arg_keys[12], (9, D), (0.05 * TOKENS ** 0.5), 48.0, (), jnp.float32)
    vector_square = jnp.clip(jnp.exp(jax.random.uniform(arg_keys[13], (9, D), jnp.float32, math.log(5.12), math.log(51.2))), 5.12, 51.2)
    up_bias = scatter_about(arg_keys[14], (FF,), 0.2, 3.0, (), jnp.float32)
    up_bias_mean = scatter_about(arg_keys[15], (FF,), (0.05 * TOKENS ** 0.5), 48.0, (), jnp.float32)
    up_bias_square = jnp.clip(jnp.exp(jax.random.uniform(arg_keys[16], (FF,), jnp.float32, math.log(5.12), math.log(51.2))), 5.12, 51.2)
    conv_kernel = scatter_about(arg_keys[17], (27, D), 27 ** -0.5, 1.25, (), jnp.float32)
    kernel_mean = scatter_about(arg_keys[18], (27, D), (0.05 * TOKENS ** 0.5), 48.0, (), jnp.float32)
    kernel_square = jnp.clip(jnp.exp(jax.random.uniform(arg_keys[19], (27, D), jnp.float32, math.log(5.12), math.log(51.2))), 5.12, 51.2)
    return {"clips_in": clips_in, "out_grad": out_grad, "clip_side": clip_side, "qkv_weight": qkv_weight, "proj_weight": proj_weight, "up_weight": up_weight, "down_weight": down_weight, "qkv_moment": qkv_moment, "proj_moment": proj_moment, "up_moment": up_moment, "down_moment": down_moment, "vectors": vectors, "vector_mean": vector_mean, "vector_square": vector_square, "up_bias": up_bias, "up_bias_mean": up_bias_mean, "up_bias_square": up_bias_square, "conv_kernel": conv_kernel, "kernel_mean": kernel_mean, "kernel_square": kernel_square}


@jax.custom_vjp
def low(v):
    return lax.optimization_barrier(v.astype(jnp.bfloat16)).astype(jnp.float32)

@jax.custom_vjp
def low_back(v):
    return v

def low_keep(v):
    return (low(v), None)

def low_pass(kept, grad):
    return (grad,)

def back_keep(v):
    return (v, None)

def back_low(kept, grad):
    return (low(grad),)
low.defvjp(low_keep, low_pass)
low_back.defvjp(back_keep, back_low)
HIGHEST = lax.Precision.HIGHEST
POLY_ONE = 3.4445
POLY_TWO = -4.775
POLY_THREE = 2.0315

def layer_norm(rows_in, gain_vec, shift_vec):
    average = lax.optimization_barrier(jnp.mean(rows_in, axis=-1, keepdims=True))
    centered = rows_in - average
    variance = lax.optimization_barrier(jnp.mean(centered * centered, axis=-1, keepdims=True))
    return centered * lax.rsqrt(variance + 1e-05) * gain_vec + shift_vec

def depthwise(padded, conv_kernel, frame_count, grid_side):
    summed = jnp.zeros(padded.shape[:-4] + (frame_count, grid_side, grid_side, padded.shape[-1]), jnp.float32)
    for offset in range(27):
        depth_at, remain = divmod(offset, 9)
        row_at, column_at = divmod(remain, 3)
        summed = summed + conv_kernel[offset] * padded[..., depth_at:depth_at + frame_count, row_at:row_at + grid_side, column_at:column_at + grid_side, :]
    return summed

def clip_forward(weights, vectors, up_bias, conv_kernel, clip_x, clip_limit):
    qkv_low, proj_low, up_low, down_low = weights
    grid_pos = jnp.arange(SIDE, dtype=jnp.int32)
    inside = (grid_pos[:, None] < clip_limit) & (grid_pos[None, :] < clip_limit)
    masked = clip_x * inside.astype(jnp.float32)[None, :, :, None]
    padded = jnp.pad(masked, ((1, 1), (1, 1), (1, 1), (0, 0)))
    first_res = clip_x + depthwise(padded, conv_kernel, FRAMES, SIDE) + vectors[4]
    tokens = first_res.reshape(CLIP_TOK, D)
    normed = low(layer_norm(tokens, vectors[0], vectors[1]))
    qkv_bias = jnp.concatenate([vectors[5], jnp.zeros((D,), jnp.float32), vectors[6]])
    joined = low_back(low(jnp.dot(normed, qkv_low.T, precision=HIGHEST) + qkv_bias))
    split_heads = joined.reshape(CLIP_TOK, 3, HEADS, HEAD_DIM)
    queries = split_heads[:, 0]
    key_rows = split_heads[:, 1]
    values = split_heads[:, 2]
    key_ok = jnp.broadcast_to(inside[None], (FRAMES, SIDE, SIDE)).reshape(CLIP_TOK)
    score_scale = HEAD_DIM ** (-0.5)

    def attend(query_block):
        scores = low_back(jnp.einsum('qhd,khd->hqk', query_block, key_rows, precision=HIGHEST) * score_scale)
        scores = jnp.where(key_ok[None, None, :], scores, -1e+30)
        row_peak = lax.optimization_barrier(jnp.max(scores, axis=-1, keepdims=True))
        exp_terms = jnp.exp(scores - row_peak)
        attn_probs = low(exp_terms / lax.optimization_barrier(jnp.sum(exp_terms, axis=-1, keepdims=True)))
        return low_back(low(jnp.einsum('hqk,khd->qhd', attn_probs, values, precision=HIGHEST)))
    blocks = queries.reshape(QBLOCKS, CLIP_TOK // QBLOCKS, HEADS, HEAD_DIM)
    attended = lax.map(jax.checkpoint(attend), blocks).reshape(CLIP_TOK, D)
    branch = low_back(jnp.dot(attended, proj_low.T, precision=HIGHEST) + vectors[7])
    second = tokens + branch
    normed_two = low(layer_norm(second, vectors[2], vectors[3]))
    hidden = low_back(jnp.dot(normed_two, up_low.T, precision=HIGHEST) + up_bias)
    activated = low(jax.nn.gelu(hidden, approximate=False))
    output = low_back(jnp.dot(activated, down_low, precision=HIGHEST) + vectors[8])
    return (second + output).reshape(FRAMES, SIDE, SIDE, D)

def orthogonal(moment):
    scaled = moment / (jnp.sqrt(jnp.sum(moment * moment)) + 1e-07)
    for rounds in range(NS_STEPS):
        gram_mat = jnp.dot(scaled.T, scaled, precision=HIGHEST)
        poly_mat = POLY_TWO * gram_mat + POLY_THREE * jnp.dot(gram_mat, gram_mat, precision=HIGHEST)
        scaled = POLY_ONE * scaled + jnp.dot(scaled, poly_mat, precision=HIGHEST)
    return scaled

def adamw(param, mean_old, square_old, gradient, rate_value, decay):
    mean_new = 0.9 * mean_old + 0.1 * gradient
    square_new = 0.999 * square_old + 0.001 * gradient * gradient
    mean_hat = mean_new / (1.0 - 0.9 ** STEP)
    square_hat = square_new / (1.0 - 0.999 ** STEP)
    return (mean_new, square_new, param - rate_value * (mean_hat / (jnp.sqrt(square_hat) + 1e-08) + decay * param))

def reference(clips_in, out_grad, clip_side, qkv_weight, proj_weight, up_weight, down_weight, qkv_moment, proj_moment, up_moment, down_moment, vectors, vector_mean, vector_square, up_bias, up_bias_mean, up_bias_square, conv_kernel, kernel_mean, kernel_square):

    def forward(qkv_master, proj_master, up_master, down_master, vector_vals, bias_vals, kernel_vals, inputs):
        weights = (low(qkv_master), low(proj_master), low(up_master), low(down_master))

        def one_clip(clip_pair):
            return clip_forward(weights, vector_vals, bias_vals, kernel_vals, clip_pair[0], clip_pair[1])
        return lax.map(one_clip, (inputs, clip_side))
    result, pullback = jax.vjp(forward, qkv_weight, proj_weight, up_weight, down_weight, vectors, up_bias, conv_kernel, clips_in.astype(jnp.float32))
    grid_pos = jnp.arange(SIDE, dtype=jnp.int32)
    limits = clip_side[:, None, None]
    inside = (grid_pos[None, :, None] < limits) & (grid_pos[None, None, :] < limits)
    cotangent = out_grad.astype(jnp.float32) * inside.astype(jnp.float32)[:, None, :, :, None]
    gradients = pullback(cotangent)
    qkv_new_moment = 0.95 * qkv_moment + gradients[0]
    proj_new_moment = 0.95 * proj_moment + gradients[1]
    up_new_moment = 0.95 * up_moment + gradients[2]
    down_new_moment = 0.95 * down_moment + gradients[3]
    qkv_new = 0.999 * qkv_weight - 0.2 * math.sqrt(3.0) * orthogonal(qkv_new_moment)
    proj_new = 0.999 * proj_weight - 0.12 * math.sqrt(CLIP_TOK) * orthogonal(proj_new_moment)
    up_new = 0.999 * up_weight - 0.2 * math.sqrt(FF / D) * orthogonal(up_new_moment)
    down_new = 0.999 * down_weight - 0.2 * orthogonal(down_new_moment)
    vec_mean, vec_square, vec_new = adamw(vectors, vector_mean, vector_square, gradients[4], 0.2, 0.0)
    bias_mean, bias_square, bias_new = adamw(up_bias, up_bias_mean, up_bias_square, gradients[5], 0.2, 0.0)
    kern_mean, kern_square, kern_new = adamw(conv_kernel, kernel_mean, kernel_square, gradients[6], 0.05, 0.01)
    return (result.astype(jnp.bfloat16), gradients[7], qkv_new_moment, qkv_new, proj_new_moment, proj_new, up_new_moment, up_new, down_new_moment, down_new, vec_mean, vec_square, vec_new, bias_mean, bias_square, bias_new, kern_mean, kern_square, kern_new)
```

```python
import functools
import math

import jax
import jax.numpy as jnp
import numpy as np
from jax import lax
from jax.experimental import pallas as pl
from jax.experimental.pallas import tpu as pltpu
from jax.sharding import PartitionSpec as P

D = 320
HEADS = 5
HEAD_DIM = 64
PAIR = 2 * HEAD_DIM
WIDE = HEADS * PAIR
FF = 1280
NS_STEPS = 5
STEP = 10
CLIP_TOK = 3200
SHARE = 320

POLY_ONE = 3.4445
POLY_TWO = -4.775
POLY_THREE = 2.0315
LOG2E = math.log2(math.e)
SCORE_SCALE = HEAD_DIM**-0.5
MASKED = -1e30
MESH = pl.DeviceIdType.MESH
BF = jnp.bfloat16
F32 = jnp.float32
NT = (((1,), (1,)), ((), ()))
VMEM_SPEC = pl.BlockSpec(memory_space=pltpu.VMEM)


def dot_nt(left, right):
    return lax.dot_general(left, right, NT, preferred_element_type=F32)


def dot_nn(left, right):
    return jnp.dot(left, right, preferred_element_type=F32)


def lanes_of(rows):
    return lax.broadcasted_iota(jnp.int32, (rows, PAIR), 1)


CELL_AT = np.stack([np.arange(400) // 20, np.arange(400) % 20], axis=1).astype(np.float32)


def select_lanes(upper):
    row = lax.broadcasted_iota(jnp.int32, (D, WIDE), 0)
    col = lax.broadcasted_iota(jnp.int32, (D, WIDE), 1)
    source = lax.shift_left(lax.shift_right_logical(col, 7), 6) + (col & (HEAD_DIM - 1))
    half = col & HEAD_DIM
    return (source == row) & (half == (HEAD_DIM if upper else 0))


def flatten_frame(read_row, dst, base):
    for row in range(20):
        dst[base + 20 * row : base + 20 * row + 20, :] = read_row(row).astype(F32)


def build_slabs(center, edged, slot, flat, cells):
    blank = jnp.zeros((20, D), F32)
    edged[1, slot, 0:20, :] = blank
    edged[1, slot, 420:440, :] = blank
    edged[1, slot, 20:420, :] = flat
    center[1, slot] = flat
    col = cells[:, 1:2]
    for e, keep in ((0, col > 0.5), (2, col < 18.5)):
        moved = jnp.where(keep, edged[1, slot, 19 + e : 419 + e, :], 0.0)
        center[e, slot] = moved
        edged[e, slot, 0:20, :] = blank
        edged[e, slot, 420:440, :] = blank
        edged[e, slot, 20:420, :] = moved


def slab(center, edged, slot, b, e, start, size):
    if b == 1:
        return center[e, slot, pl.ds(start, size), :]
    return edged[e, slot, pl.ds(start + 20 * b, size), :]


def inside_of(side_ref, cells):
    side = side_ref[0].astype(F32) - 0.5
    return (cells[:, 0:1] < side) & (cells[:, 1:2] < side)


def norm_parts(rows):
    average = jnp.sum(rows, axis=-1, keepdims=True) * (1.0 / D)
    centered = rows - average
    variance = jnp.sum(centered * centered, axis=-1, keepdims=True) * (1.0 / D)
    scale = lax.rsqrt(variance + 1e-05)
    return centered * scale, scale


def frame_peers():
    f = lax.axis_index("frame")
    near = f + 1 - 2 * lax.rem(f, 2)
    across = lax.rem(f + 2, 4)
    return f, near, across, lax.rem(near + 2, 4)


def share_rows(rows, clips):
    return 16 * (-(-rows // (16 * clips)))


def greet_all(clips):
    barrier = pltpu.get_barrier_semaphore()
    for peer in frame_peers()[1:]:
        pl.semaphore_signal(barrier, inc=1, device_id={"frame": peer}, device_id_type=MESH)
    c = lax.axis_index("clip")

    def greet(step, carry):
        pl.semaphore_signal(
            barrier, inc=1, device_id={"clip": lax.rem(c + step, clips)}, device_id_type=MESH
        )
        return carry

    lax.fori_loop(1, clips, greet, 0)


def await_greetings(count):
    pl.semaphore_wait(pltpu.get_barrier_semaphore(), count)


def send(src, dst, send_sem, recv_sem, peer):
    return pltpu.make_async_remote_copy(
        src_ref=src,
        dst_ref=dst,
        send_sem=send_sem,
        recv_sem=recv_sem,
        device_id={"frame": peer},
        device_id_type=MESH,
    )


def halo_copies(first, last, halo, sems):
    f = lax.axis_index("frame")
    down = send(first, halo.at[1], sems.at[0, 0], sems.at[1, 0], jnp.maximum(f - 1, 0))
    up = send(last, halo.at[0], sems.at[0, 1], sems.at[1, 1], jnp.minimum(f + 1, 3))
    return down, up


def start_halos(down, up, halo):
    f = lax.axis_index("frame")

    @pl.when(f > 0)
    def _():
        down.start()

    @pl.when(f < 3)
    def _():
        up.start()

    @pl.when(f == 0)
    def _():
        halo[0] = jnp.zeros(halo.shape[1:], halo.dtype)

    @pl.when(f == 3)
    def _():
        halo[1] = jnp.zeros(halo.shape[1:], halo.dtype)


def wait_halos(down, up):
    f = lax.axis_index("frame")

    @pl.when(f > 0)
    def _():
        down.wait_send()
        up.wait_recv()

    @pl.when(f < 3)
    def _():
        up.wait_send()
        down.wait_recv()


EXP_SCALE = SCORE_SCALE * LOG2E


def tail_lanes(inside, copies):
    lane = lax.broadcasted_iota(jnp.int32, (inside.shape[0], PAIR), 1)
    tail = jnp.where(
        lane == HEAD_DIM,
        jnp.where(inside, 0.0, MASKED),
        jnp.where((lane > HEAD_DIM) & (lane < HEAD_DIM + 4), 1.0, 0.0),
    )
    return jnp.concatenate([tail] * copies, axis=0).astype(BF)


def front_kernel(
    clips,
    x_ref,
    side_ref,
    cells_ref,
    qkv_ref,
    proj_ref,
    up_ref,
    down_ref,
    vec_ref,
    taps_ref,
    tok_out,
    nhome_out,
    ncross_out,
    q_out,
    home_out,
    cross_out,
    kept_out,
    att_out,
    wq_out,
    wkv_out,
    others_out,
    tok_ref,
    nhome_ref,
    ncross_ref,
    q_ref,
    home_ref,
    cross_ref,
    kept_ref,
    att_ref,
    wq_ref,
    wkv_ref,
    others_ref,
    halo_ref,
    raw,
    outer,
    center,
    edged,
    qkv_full,
    tail,
    halo_sems,
    qkv_sems,
    other_sems,
    spread_sems,
    near_sems,
    cross_sems,
    out_sems,
):
    leaving = []

    def leave(src, dst):
        copy = pltpu.make_async_copy(src, dst, out_sems.at[len(leaving)])
        copy.start()
        leaving.append(copy)

    f, near, across, far = frame_peers()
    c = lax.axis_index("clip")
    greet_all(clips)
    part_rows = qkv_ref.shape[1]

    def qkv_rows(owner):
        return qkv_full.at[pl.ds(pl.multiple_of(owner * part_rows, 16), part_rows), :]

    qkv_full[pl.ds(pl.multiple_of(f * part_rows, 16), part_rows), :] = qkv_ref[...].T.astype(BF)
    start = 0
    for shard in (proj_ref, up_ref, down_ref):
        size = shard.shape[0]
        others_ref[f, start : start + size, :] = shard[...].astype(BF)
        start += size
    spare = others_ref.shape[1] - start
    if spare:
        others_ref[f, start : start + spare, :] = jnp.zeros((spare, D), BF)
    cells = cells_ref[...]
    inside = inside_of(side_ref, cells)
    for t in range(2):
        flatten_frame(lambda row, t=t: x_ref[0, t, row], raw, 400 * t)

    await_greetings(3 + clips - 1)
    down, up = halo_copies(x_ref.at[0, 0], x_ref.at[0, 1], halo_ref, halo_sems)
    start_halos(down, up, halo_ref)
    qkv_cross = send(qkv_rows(f), qkv_rows(f), qkv_sems.at[0, 1], qkv_sems.at[1, 1], across)
    qkv_near = send(qkv_rows(f), qkv_rows(f), qkv_sems.at[0, 0], qkv_sems.at[1, 0], near)
    qkv_relay = send(
        qkv_rows(across), qkv_rows(across), qkv_sems.at[0, 2], qkv_sems.at[1, 2], near
    )
    qkv_cross.start()
    qkv_near.start()

    part = others_ref.shape[1] // clips

    def part_of(owner, clip):
        return others_ref.at[owner, pl.ds(pl.multiple_of(clip * part, 16), part), :]

    other_near = send(
        others_ref.at[f], others_ref.at[f], other_sems.at[0, 0], other_sems.at[1, 0], near
    )
    other_cross = send(
        part_of(f, c), part_of(f, c), other_sems.at[0, 1], other_sems.at[1, 1], across
    )
    other_relay = send(
        others_ref.at[across],
        others_ref.at[across],
        other_sems.at[0, 2],
        other_sems.at[1, 2],
        near,
    )

    def spread(clip, landing):
        return pltpu.make_async_remote_copy(
            src_ref=part_of(across, c),
            dst_ref=part_of(across, landing),
            send_sem=spread_sems.at[0, clip],
            recv_sem=spread_sems.at[1, landing],
            device_id={"clip": clip},
            device_id_type=MESH,
        )

    def other_clips(act):
        def body(step, carry):
            act(lax.rem(c + step, clips))
            return carry

        lax.fori_loop(1, clips, body, 0)

    other_cross.start()
    other_near.start()

    for t in range(2):
        build_slabs(
            center, edged, t + 1, jnp.where(inside, raw[400 * t : 400 * t + 400, :], 0.0), cells
        )

    def conv_part(t, depths, start, total):
        for a in depths:
            for b in range(3):
                for e in range(3):
                    offset = 9 * a + 3 * b + e
                    total = total + taps_ref[offset : offset + 1, :] * slab(
                        center, edged, t + a, b, e, start, 40
                    )
        return total

    for t, depths in ((0, (1, 2)), (1, (0, 1))):

        def own_part(step, carry, t=t, depths=depths):
            start = pl.multiple_of(step * 40, 8)
            at = pl.ds(pl.multiple_of(start + 400 * t, 8), 40)
            tok_ref[at, :] = conv_part(t, depths, start, raw[at, :] + vec_ref[4:5, :])
            return carry

        lax.fori_loop(0, 10, own_part, 0)
    other_cross.wait_recv()
    other_clips(lambda clip: spread(clip, c).start())
    qkv_cross.wait_recv()
    qkv_relay.start()
    wait_halos(down, up)
    for side, slot in ((0, 0), (1, 3)):
        flatten_frame(lambda row, side=side: halo_ref[side, row], outer, 0)
        build_slabs(center, edged, slot, jnp.where(inside, outer[...], 0.0), cells)
    for t, depths in ((0, (0,)), (1, (2,))):

        def rim_part(step, carry, t=t, depths=depths):
            start = pl.multiple_of(step * 40, 8)
            at = pl.ds(pl.multiple_of(start + 400 * t, 8), 40)
            rows = conv_part(t, depths, start, tok_ref[at, :])
            tok_ref[at, :] = rows
            raw[at, :] = norm_parts(rows)[0] * vec_ref[0:1, :] + vec_ref[1:2, :]
            return carry

        lax.fori_loop(0, 10, rim_part, 0)
    rows = tok_ref.shape[0]
    nhome_ref[0:rows, :] = raw[...].astype(BF)

    piece = rows // HEADS

    def cross_copy(k):
        at = pl.ds(pl.multiple_of(k * piece, 16), piece)
        return send(
            nhome_ref.at[at, :],
            ncross_ref.at[at, :],
            cross_sems.at[0, 0, k],
            cross_sems.at[1, 0, k],
            across,
        )

    def relay_copy(k):
        return send(
            ncross_ref.at[pl.ds(pl.multiple_of(k * piece, 16), piece), :],
            ncross_ref.at[pl.ds(pl.multiple_of(rows + k * piece, 16), piece), :],
            cross_sems.at[0, 1, k],
            cross_sems.at[1, 1, k],
            near,
        )

    near_copy = send(
        nhome_ref.at[pl.ds(0, rows), :],
        nhome_ref.at[pl.ds(rows, rows), :],
        near_sems.at[0],
        near_sems.at[1],
        near,
    )
    for k in range(HEADS):
        cross_copy(k).start()
    near_copy.start()

    blank = jnp.zeros((1, HEAD_DIM), F32)

    def head_bias(row, h):
        return vec_ref[row : row + 1, HEAD_DIM * h : HEAD_DIM * (h + 1)]

    qkv_near.wait_recv()
    qkv_relay.wait_recv()
    for h in range(HEADS):
        wq_ref[PAIR * h : PAIR * h + HEAD_DIM, :] = qkv_full[HEAD_DIM * h : HEAD_DIM * (h + 1), :]
        wq_ref[PAIR * h + HEAD_DIM : PAIR * (h + 1), :] = jnp.zeros((HEAD_DIM, D), BF)
        wkv_ref[PAIR * h : PAIR * h + HEAD_DIM, :] = qkv_full[
            D + HEAD_DIM * h : D + HEAD_DIM * (h + 1), :
        ]
        wkv_ref[PAIR * h + HEAD_DIM : PAIR * (h + 1), :] = qkv_full[
            2 * D + HEAD_DIM * h : 2 * D + HEAD_DIM * (h + 1), :
        ]
    leave(tok_ref, tok_out)
    leave(wq_ref, wq_out)
    leave(wkv_ref, wkv_out)
    wide_query = jnp.concatenate(
        [part for h in range(HEADS) for part in (head_bias(5, h), blank)], axis=1
    )
    wide_pair = jnp.concatenate(
        [part for h in range(HEADS) for part in (blank, head_bias(6, h))], axis=1
    )

    def project(normed, weight, bias, place):
        joined = (dot_nt(normed, weight[...]) + bias).astype(BF)
        for h in range(HEADS):
            place(h, joined[:, PAIR * h : PAIR * (h + 1)])

    def place_query(h, value):
        q_ref[h] = value

    def place_own(h, value):
        home_ref[h, 0:rows, :] = value

    def place_near(h, value):
        home_ref[h, rows : 2 * rows, :] = value

    def place_cross(h, value):
        cross_ref[h] = value

    project(nhome_ref[0:rows, :], wq_ref, wide_query, place_query)
    project(nhome_ref[0:rows, :], wkv_ref, wide_pair, place_own)
    leave(q_ref, q_out)
    tail[...] = tail_lanes(inside, 4)
    tile = rows // 2
    mask_lane = jnp.where(lanes_of(tile) == HEAD_DIM, 1.0, 0.0).astype(BF)

    def tile_pass(t, source, last):
        at = pl.ds(pl.multiple_of(t * tile, 16), tile)
        lane = lanes_of(tile)
        for h in range(HEADS):
            keys = jnp.concatenate([source[h], tail[...]], axis=1)
            score = dot_nt(jnp.concatenate([q_ref[h, at, :], mask_lane], axis=1), keys)
            peak = jnp.max(score, axis=-1, keepdims=True)
            if last:
                kept = kept_ref[h, at, :]
                old_peak = kept[:, 0:1]
                peak = jnp.maximum(peak, old_peak)
            terms = jnp.exp2((score - peak) * EXP_SCALE).astype(BF)
            mixed = dot_nn(terms, keys)
            total = mixed[:, PAIR + HEAD_DIM + 1 : PAIR + HEAD_DIM + 2]
            mixed = mixed[:, 0:PAIR]
            if last:
                fade = jnp.exp2((old_peak - peak) * EXP_SCALE)
                total = total + fade * kept[:, 32:33]
                mixed = (mixed + fade * kept) / total
                log_sum = peak + jnp.log2(total) * (1.0 / EXP_SCALE)
                kept_ref[h, at, :] = jnp.where(lane < HEAD_DIM, log_sum, mixed)
                att_ref[h, at, :] = jnp.where(lane < HEAD_DIM, 0.0, mixed).astype(BF)
            else:
                kept_ref[h, at, :] = jnp.where(
                    lane < 32, peak, jnp.where(lane < HEAD_DIM, total, mixed)
                )

    def pass_on(k):
        cross_copy(k).wait_recv()
        relay_copy(k).start()

    def first_pass(t, carry):
        tile_pass(t, home_ref, False)

        @pl.when(t == 0)
        def _():
            for k in (0, 1, 2):
                pass_on(k)

        return carry

    def second_pass(t, carry):
        tile_pass(t, cross_ref, True)

        @pl.when(t == 0)
        def _():
            other_clips(lambda clip: spread(clip, clip).wait_recv())
            other_relay.start()

        return carry

    near_copy.wait_recv()
    leave(nhome_ref, nhome_out)
    project(nhome_ref[rows : 2 * rows, :], wkv_ref, wide_pair, place_near)
    leave(home_ref, home_out)
    lax.fori_loop(0, 2, first_pass, 0)
    for k in (3, 4):
        pass_on(k)
    for k in range(HEADS):
        relay_copy(k).wait_recv()
    leave(ncross_ref, ncross_out)
    project(ncross_ref[...], wkv_ref, wide_pair, place_cross)
    leave(cross_ref, cross_out)
    lax.fori_loop(0, 2, second_pass, 0)
    leave(kept_ref, kept_out)
    leave(att_ref, att_out)
    other_near.wait()
    other_relay.wait()
    leave(others_ref, others_out)
    other_clips(lambda clip: spread(clip, c).wait_send())
    for copy in (other_cross, near_copy, qkv_cross, qkv_near, qkv_relay):
        copy.wait_send()
    for k in range(HEADS):
        cross_copy(k).wait_send()
        relay_copy(k).wait_send()
    for copy in leaving:
        copy.wait()


def front(clips_in, clip_side, qkv, proj, up, down, vectors, taps, clips, collective_id):
    rows = 800
    other_rows = clips * share_rows(proj.shape[0] + up.shape[0] + down.shape[0], clips)
    outs = (
        ((rows, D), F32),
        ((2 * rows, D), BF),
        ((2 * rows, D), BF),
        ((HEADS, rows, PAIR), BF),
        ((HEADS, 2 * rows, PAIR), BF),
        ((HEADS, 2 * rows, PAIR), BF),
        ((HEADS, rows, PAIR), F32),
        ((HEADS, rows, PAIR), BF),
        ((WIDE, D), BF),
        ((WIDE, D), BF),
        ((4, other_rows, D), BF),
    )
    return pl.pallas_call(
        functools.partial(front_kernel, clips),
        in_specs=[VMEM_SPEC, pl.BlockSpec(memory_space=pltpu.SMEM)] + [VMEM_SPEC] * 7,
        out_specs=[pl.BlockSpec(memory_space=pl.ANY)] * len(outs),
        out_shape=[jax.ShapeDtypeStruct(*out) for out in outs],
        scratch_shapes=[pltpu.VMEM(*out) for out in outs]
        + [
            pltpu.VMEM((2, 20, 20, D), BF),
            pltpu.VMEM((rows, D), F32),
            pltpu.VMEM((400, D), F32),
            pltpu.VMEM((3, 4, 400, D), F32),
            pltpu.VMEM((3, 4, 440, D), F32),
            pltpu.VMEM((3 * D, D), BF),
            pltpu.VMEM((2 * rows, PAIR), BF),
            pltpu.SemaphoreType.DMA((2, 2)),
            pltpu.SemaphoreType.DMA((2, 3)),
            pltpu.SemaphoreType.DMA((2, 3)),
            pltpu.SemaphoreType.DMA((2, clips)),
            pltpu.SemaphoreType.DMA((2,)),
            pltpu.SemaphoreType.DMA((2, 2, HEADS)),
            pltpu.SemaphoreType.DMA((len(outs),)),
        ],
        compiler_params=pltpu.CompilerParams(
            collective_id=collective_id, has_side_effects=True, vmem_limit_bytes=60 * 2**20
        ),
        cost_estimate=pl.CostEstimate(
            flops=2**34, bytes_accessed=16 * 2**20, transcendentals=2**23
        ),
    )(clips_in, clip_side, jnp.asarray(CELL_AT), qkv, proj, up, down, vectors, taps)


INV_SQRT2 = math.sqrt(0.5)
INV_SQRT_2PI = 1.0 / math.sqrt(2.0 * math.pi)


def dot_tn(left, right):
    return lax.dot_general(left, right, (((0,), (0,)), ((), ())), preferred_element_type=F32)


def norm_back(upstream, unit, scale, gain):
    through = upstream * gain
    mean_one = jnp.sum(through, axis=-1, keepdims=True) * (1.0 / D)
    mean_two = jnp.sum(through * unit, axis=-1, keepdims=True) * (1.0 / D)
    return scale * (through - mean_one - unit * mean_two)


def column_sum(rows):
    return jnp.sum(rows, axis=0, keepdims=True)


def mid_kernel(
    att_ref,
    tok_ref,
    og_ref,
    side_ref,
    cells_ref,
    vec_ref,
    ubias_ref,
    others_ref,
    out_ref,
    gsec_ref,
    dout_ref,
    grads_ref,
    vsum_ref,
    raw,
    wide,
    act,
    ghid,
    normed,
    top,
    branch_low,
    att_low,
    proj_ref,
    up_ref,
    down_ref,
):
    start = 0
    for full in (proj_ref, up_ref, down_ref):
        size = full.shape[0] // 4
        for owner in range(4):
            full[size * owner : size * (owner + 1), :] = others_ref[owner, start : start + size, :]
        start += size
    inside = inside_of(side_ref, cells_ref[...])
    pick = select_lanes(True).astype(F32).astype(BF)
    wide[...] = dot_nn(proj_ref[...], pick).astype(BF)
    vsum_ref[...] = jnp.zeros(vsum_ref.shape, F32)
    for t in range(2):
        at = slice(400 * t, 400 * t + 400)
        heads = jnp.concatenate([att_ref[h, at, :] for h in range(HEADS)], axis=1)
        att_low[at, :] = dot_nt(heads, pick).astype(BF)
        second = tok_ref[at, :] + (dot_nt(heads, wide[...]) + vec_ref[7:8, :])
        unit, scale = norm_parts(second)
        normed_two = (unit * vec_ref[2:3, :] + vec_ref[3:4, :]).astype(BF)
        normed[at, :] = normed_two
        flatten_frame(lambda row, t=t: og_ref[0, t, row], raw, 0)
        grad_top = jnp.where(inside, raw[...], 0.0)
        top_low = grad_top.astype(BF)
        top[at, :] = top_low
        hidden = dot_nt(normed_two, up_ref[...]) + ubias_ref[...]
        half = 0.5 + 0.5 * lax.erf(hidden * INV_SQRT2)
        activated = (hidden * half).astype(BF)
        act[at, :] = activated
        slope = half + hidden * (INV_SQRT_2PI * jnp.exp(-0.5 * hidden * hidden))
        grad_hidden = (dot_nt(top_low, down_ref[...]) * slope).astype(BF)
        ghid[at, :] = grad_hidden
        raw[...] = second + (dot_nn(activated, down_ref[...]) + vec_ref[8:9, :])
        for row in range(20):
            out_ref[0, t, row] = raw[20 * row : 20 * row + 20, :].astype(BF)
        upstream = dot_nn(grad_hidden, up_ref[...])
        grad_second = grad_top + norm_back(upstream, unit, scale, vec_ref[2:3, :])
        gsec_ref[at, :] = grad_second
        low = grad_second.astype(BF)
        branch_low[at, :] = low
        dout = dot_nn(low, wide[...]).astype(BF)
        for h in range(HEADS):
            dout_ref[h, at, :] = dout[:, PAIR * h : PAIR * (h + 1)]
        vsum_ref[0:1, :] += column_sum(upstream * unit)
        vsum_ref[1:2, :] += column_sum(upstream)
        vsum_ref[2:3, :] += column_sum(low.astype(F32))
        vsum_ref[3:4, :] += column_sum(grad_top)
        bias_sum = column_sum(grad_hidden.astype(F32))
        for part in range(4):
            vsum_ref[4 + part : 5 + part, :] += bias_sum[:, D * part : D * (part + 1)]
    rows = up_ref.shape[0] // 4
    proj_rows = D // 4
    grad = dot_tn(branch_low[...], att_low[...]).astype(BF)
    for owner in range(4):
        grads_ref[owner, 0:proj_rows, :] = grad[proj_rows * owner : proj_rows * (owner + 1), :]
    for owner in range(4):
        at = slice(rows * owner, rows * (owner + 1))
        start = proj_rows
        grads_ref[owner, start : start + rows, :] = dot_tn(ghid[:, at], normed[...]).astype(BF)
        start = proj_rows + rows
        grads_ref[owner, start : start + rows, :] = dot_tn(act[:, at], top[...]).astype(BF)


def middle(attended, tokens, out_grad, clip_side, vectors, up_bias, others):
    rows = 800
    low = lambda *shape: jax.ShapeDtypeStruct(shape, BF)
    wide = lambda *shape: jax.ShapeDtypeStruct(shape, F32)
    return pl.pallas_call(
        mid_kernel,
        in_specs=[VMEM_SPEC] * 3 + [pl.BlockSpec(memory_space=pltpu.SMEM)] + [VMEM_SPEC] * 4,
        out_specs=[VMEM_SPEC] * 5,
        out_shape=[
            low(*out_grad.shape),
            wide(rows, D),
            low(HEADS, rows, PAIR),
            low(4, (D + 2 * FF) // 4, D),
            wide(8, D),
        ],
        scratch_shapes=[
            pltpu.VMEM((400, D), F32),
            pltpu.VMEM((D, WIDE), BF),
            pltpu.VMEM((rows, FF), BF),
            pltpu.VMEM((rows, FF), BF),
            pltpu.VMEM((rows, D), BF),
            pltpu.VMEM((rows, D), BF),
            pltpu.VMEM((rows, D), BF),
            pltpu.VMEM((rows, D), BF),
            pltpu.VMEM((D, D), BF),
            pltpu.VMEM((FF, D), BF),
            pltpu.VMEM((FF, D), BF),
        ],
        compiler_params=pltpu.CompilerParams(vmem_limit_bytes=56 * 2**20),
        cost_estimate=pl.CostEstimate(
            flops=6 * 2**30, bytes_accessed=12 * 2**20, transcendentals=2**21
        ),
    )(attended, tokens, out_grad, clip_side, jnp.asarray(CELL_AT), vectors, up_bias, others)


class RowSums:
    def __init__(self, clips, g_ref, at, pair_in, cross_out, cross_in, shares, shares_in, sums,
                 frame_sems, part_sems, sum_sems):
        self.clips = clips
        self.g = g_ref
        self.at = at
        self.pair_in = pair_in
        self.cross_out = cross_out
        self.cross_in = cross_in
        self.shares = shares
        self.shares_in = shares_in
        self.sums = sums
        self.part_sems = part_sems
        self.sum_sems = sum_sems
        f, near, across, far = frame_peers()
        self.f, self.across = f, across
        self.c = lax.axis_index("clip")
        sem = frame_sems
        part = lambda owner: g_ref.at[owner, pl.ds(at.start, at.stop - at.start), :]
        self.first = send(part(far), pair_in.at[0], sem.at[0, 0], sem.at[1, 0], near)
        self.second = send(part(near), pair_in.at[1], sem.at[0, 1], sem.at[1, 1], near)
        self.cross = send(cross_out, cross_in, sem.at[0, 2], sem.at[1, 2], across)

    def peer(self, step):
        return lax.rem(self.c + step, self.clips)

    def part_copy(self, step):
        return pltpu.make_async_remote_copy(
            src_ref=self.shares.at[self.peer(step)],
            dst_ref=self.shares_in.at[step],
            send_sem=self.part_sems.at[0, step],
            recv_sem=self.part_sems.at[1, step],
            device_id={"clip": self.peer(step)},
            device_id_type=MESH,
        )

    def sum_copy(self, step):
        return pltpu.make_async_remote_copy(
            src_ref=self.sums.at[self.c],
            dst_ref=self.sums.at[self.c],
            send_sem=self.sum_sems.at[0, step],
            recv_sem=self.sum_sems.at[1, step],
            device_id={"clip": self.peer(step)},
            device_id_type=MESH,
        )

    def each(self, act):
        def body(step, carry):
            act(step)
            return carry

        lax.fori_loop(1, self.clips, body, 0)

    def pair_step(self):
        self.first.start()
        self.second.start()

    def cross_step(self):
        self.first.wait()
        self.cross_out[...] = (
            self.g[self.across, self.at, :].astype(F32) + self.pair_in[0].astype(F32)
        ).astype(BF)
        self.cross.start()

    def share_step(self):
        self.second.wait()
        self.cross.wait()
        mine = (
            self.g[self.f, self.at, :].astype(F32)
            + self.pair_in[1].astype(F32)
            + self.cross_in[...].astype(F32)
        ).astype(BF)
        rows, chunk = mine.shape[0], self.shares.shape[1]
        spare = self.clips * chunk - rows
        if spare:
            mine = jnp.concatenate([mine, jnp.zeros((spare, D), BF)], axis=0)
        self.shares[...] = mine.reshape(self.clips, chunk, D)
        self.each(lambda step: self.part_copy(step).start())

    def sum_step(self):
        self.each(lambda step: self.part_copy(step).wait())

        def add_part(step, total):
            return total + self.shares_in[step].astype(F32)

        total = lax.fori_loop(1, self.clips, add_part, self.shares[self.c].astype(F32))
        self.sums[self.c] = total.astype(BF)
        self.each(lambda step: self.sum_copy(step).start())

    def finish(self):
        self.each(lambda step: self.sum_copy(step).wait())


def row_sums_scratch(rows, clips):
    chunk = share_rows(rows, clips)
    return [
        pltpu.VMEM((2, rows, D), BF),
        pltpu.VMEM((rows, D), BF),
        pltpu.VMEM((rows, D), BF),
        pltpu.VMEM((clips, chunk, D), BF),
        pltpu.VMEM((clips, chunk, D), BF),
        pltpu.VMEM((clips, chunk, D), BF),
        pltpu.SemaphoreType.DMA((2, 3)),
        pltpu.SemaphoreType.DMA((2, clips)),
        pltpu.SemaphoreType.DMA((2, clips)),
    ]


EARLY_PARTS = (slice(0, 400), slice(400, 720))


def row_pieces(start, size, block):
    pieces, skip = [], 0
    while skip < size:
        owner, row = divmod(start + skip, block)
        step = min(size - skip, block - row)
        pieces.append((owner, row, skip, step))
        skip += step
    return pieces


def back_kernel(
    clips,
    q_ref,
    dout_ref,
    kept_ref,
    cross_ref,
    home_in,
    nhome_in,
    ncross_in,
    wq_in,
    wkv_in,
    side_ref,
    cells_ref,
    early_ref,
    gnorm_ref,
    own_ref,
    out_ref,
    bsum_ref,
    one_ref,
    two_ref,
    home_ref,
    nhome_ref,
    ncross_ref,
    wq_ref,
    wkv_ref,
    grads_ref,
    grads_in,
    extra,
    qd_t,
    tail,
    low_one,
    low_two,
    low_three,
    dq_sum,
    dq_low,
    turned_pairs,
    pair_grad,
    dnormed,
    pair_out,
    pair_in,
    cross_out,
    cross_in,
    pair_sems,
    cross_sems,
    late_sems,
    grad_sems,
    *sum_refs,
):
    f, near, across, far = frame_peers()
    rows = q_ref.shape[1]
    greet_all(clips)
    late = [
        pltpu.make_async_copy(src, dst, late_sems.at[k])
        for k, (src, dst) in enumerate(
            (
                (ncross_in, ncross_ref),
                (wkv_in, wkv_ref),
                (home_in, home_ref),
                (nhome_in, nhome_ref),
                (wq_in, wq_ref),
            )
        )
    ]
    for copy in late:
        copy.start()
    half = len(sum_refs) // 2
    one = RowSums(clips, early_ref, EARLY_PARTS[0], *sum_refs[:half])
    two = RowSums(clips, early_ref, EARLY_PARTS[1], *sum_refs[half:])
    tail[...] = tail_lanes(inside_of(side_ref, cells_ref[...]), 4)
    await_greetings(3 + clips - 1)
    one.pair_step()
    two.pair_step()
    lower = lax.broadcasted_iota(jnp.int32, (PAIR, 1), 0) < HEAD_DIM
    scale_of = jnp.where(lower, SCORE_SCALE, 1.0)
    chunks = ((0, 512, low_one), (512, 512, low_two), (1024, 576, low_three))

    def minus_parts(column, lane):
        high = column.astype(BF).astype(F32)
        mid = (column - high).astype(BF).astype(F32)
        rest = column - high - mid
        return jnp.where(
            lane == HEAD_DIM + 1,
            -high,
            jnp.where(lane == HEAD_DIM + 2, -mid, jnp.where(lane == HEAD_DIM + 3, -rest, 0.0)),
        )

    def prepare(h):
        lane = lanes_of(rows)
        kept = kept_ref[h]
        queries, douts = q_ref[h].astype(F32), dout_ref[h].astype(F32)
        log_sum = kept[:, 0:1]
        row_dot = jnp.sum(douts * kept, axis=-1, keepdims=True)
        of_queries = jnp.where(lane == HEAD_DIM, 1.0, minus_parts(log_sum, lane))
        extra[h, 0:rows, :] = of_queries.astype(BF)
        extra[h, rows : 2 * rows, :] = minus_parts(row_dot, lane).astype(BF)
        qd_t[h] = jnp.concatenate([queries, douts], axis=0).T.astype(BF)
        bsum_ref[1, h] = column_sum(douts)

    def head_pass(h, source, add):
        pairs = source[h]
        both = jnp.concatenate([q_ref[h], dout_ref[h]], axis=0)
        both = jnp.concatenate([both, extra[h]], axis=1)
        products = [
            dot_nt(
                both,
                jnp.concatenate(
                    [pairs[start : start + size, :], tail[start : start + size, :]], axis=1
                ),
            )
            for start, size, low in chunks
        ]
        total = dq_sum[h] if add else None
        at = pl.ds(pl.multiple_of(h * PAIR, PAIR), PAIR)
        for (start, size, low), product in zip(chunks, products):
            probs = jnp.exp2(product[0:rows, :] * EXP_SCALE)
            low[0:rows, :] = (probs * product[rows : 2 * rows, :]).astype(BF)
            low[rows : 2 * rows, :] = probs.astype(BF)
            part = dot_nn(low[0:rows, :], pairs[start : start + size, :])
            total = part if total is None else total + part
            turned = dot_nn(qd_t[h], low[...]) * scale_of
            turned_pairs[at, start : start + size] = turned.astype(BF)
        if add:
            total = jnp.where(lanes_of(rows) < HEAD_DIM, total * SCORE_SCALE, 0.0)
            dq_low[h] = total.astype(BF)
            bsum_ref[0, h] = column_sum(total)
        else:
            dq_sum[h] = total

    def of_normed(normed, add):
        grad = dot_nn(turned_pairs[...], normed[...])
        pair_grad[...] = pair_grad[...] + grad if add else grad
        total = dot_nn(wkv_ref[...].astype(F32).T.astype(BF), turned_pairs[...]).T
        dnormed[...] = total[0:rows, :]
        pair_out[...] = total[rows : 2 * rows, :].astype(BF)

    def pair_copy(phase):
        return send(
            pair_out, pair_in.at[phase], pair_sems.at[0, phase], pair_sems.at[1, phase], near
        )

    to_across = send(cross_out, cross_in, cross_sems.at[0], cross_sems.at[1], across)

    def cross_pass(h, carry):
        prepare(h)
        head_pass(h, cross_ref, False)

        @pl.when(h == 0)
        def _():
            one.cross_step()
            two.cross_step()

        @pl.when(h == 3)
        def _():
            one.share_step()

        return carry

    def home_pass(h, carry):
        head_pass(h, home_ref, True)

        @pl.when(h == 0)
        def _():
            pair_copy(0).wait()
            cross_out[...] = (dnormed[...] + pair_in[0].astype(F32)).astype(BF)
            to_across.start()
            two.share_step()

        @pl.when(h == 1)
        def _():
            one.sum_step()

        @pl.when(h == 3)
        def _():
            two.sum_step()

        return carry

    lax.fori_loop(0, HEADS, cross_pass, 0)
    for copy in late:
        copy.wait()
    of_normed(ncross_ref, False)
    pair_copy(0).start()
    lax.fori_loop(0, HEADS, home_pass, 0)
    of_normed(nhome_ref, True)
    pair_copy(1).start()

    block = grads_ref.shape[1]

    def place(start, values):
        for owner, row, skip, size in row_pieces(start, values.shape[0], block):
            grads_ref[owner, row : row + size, :] = values[skip : skip + size, :]

    dq = jnp.concatenate([dq_low[h] for h in range(HEADS)], axis=1)
    of_queries = dot_tn(dq, nhome_ref[0:rows, :]).astype(BF)
    for h in range(HEADS):
        of_pairs = pair_grad[PAIR * h : PAIR * (h + 1), :].astype(BF)
        place(HEAD_DIM * h, of_queries[PAIR * h : PAIR * h + HEAD_DIM, :])
        place(D + HEAD_DIM * h, of_pairs[0:HEAD_DIM, :])
        place(2 * D + HEAD_DIM * h, of_pairs[HEAD_DIM:PAIR, :])
    to_pair = [
        send(grads_ref.at[peer], grads_in.at[k], grad_sems.at[0, k], grad_sems.at[1, k], near)
        for k, peer in enumerate((far, near))
    ]
    for copy in to_pair:
        copy.start()
    total = dnormed[...] + dot_nn(dq, wq_ref[...])
    to_across.wait()
    pair_copy(1).wait()
    gnorm_ref[...] = total + pair_in[1].astype(F32) + cross_in[...].astype(F32)
    one.finish()
    two.finish()
    for copy in to_pair:
        copy.wait()
    out_ref[...] = (grads_ref[across].astype(F32) + grads_in[0].astype(F32)).astype(BF)
    own_ref[...] = grads_ref[f].astype(F32) + grads_in[1].astype(F32)
    one_ref[...] = one.sums[...].reshape(one_ref.shape)
    two_ref[...] = two.sums[...].reshape(two_ref.shape)


def attention_back(operands, clips, collective_id):
    rows, block = 800, 3 * D // 4
    wide = lambda *shape: jax.ShapeDtypeStruct(shape, F32)
    low = lambda *shape: jax.ShapeDtypeStruct(shape, BF)
    parts = [part.stop - part.start for part in EARLY_PARTS]
    return pl.pallas_call(
        functools.partial(back_kernel, clips),
        in_specs=[VMEM_SPEC] * 4
        + [pl.BlockSpec(memory_space=pl.ANY)] * 5
        + [pl.BlockSpec(memory_space=pltpu.SMEM)]
        + [VMEM_SPEC] * 2,
        out_specs=[VMEM_SPEC] * 6,
        out_shape=[
            wide(rows, D),
            wide(block, D),
            low(block, D),
            wide(2, HEADS, 1, PAIR),
        ]
        + [low(clips * share_rows(part, clips), D) for part in parts],
        scratch_shapes=[
            pltpu.VMEM((HEADS, 2 * rows, PAIR), BF),
            pltpu.VMEM((2 * rows, D), BF),
            pltpu.VMEM((2 * rows, D), BF),
            pltpu.VMEM((WIDE, D), BF),
            pltpu.VMEM((WIDE, D), BF),
            pltpu.VMEM((4, block, D), BF),
            pltpu.VMEM((2, block, D), BF),
            pltpu.VMEM((HEADS, 2 * rows, PAIR), BF),
            pltpu.VMEM((HEADS, PAIR, 2 * rows), BF),
            pltpu.VMEM((2 * rows, PAIR), BF),
            pltpu.VMEM((2 * rows, 512), BF),
            pltpu.VMEM((2 * rows, 512), BF),
            pltpu.VMEM((2 * rows, 576), BF),
            pltpu.VMEM((HEADS, rows, PAIR), F32),
            pltpu.VMEM((HEADS, rows, PAIR), BF),
            pltpu.VMEM((WIDE, 2 * rows), BF),
            pltpu.VMEM((WIDE, D), F32),
            pltpu.VMEM((rows, D), F32),
            pltpu.VMEM((rows, D), BF),
            pltpu.VMEM((2, rows, D), BF),
            pltpu.VMEM((rows, D), BF),
            pltpu.VMEM((rows, D), BF),
            pltpu.SemaphoreType.DMA((2, 2)),
            pltpu.SemaphoreType.DMA((2,)),
            pltpu.SemaphoreType.DMA((5,)),
            pltpu.SemaphoreType.DMA((2, 2)),
        ]
        + row_sums_scratch(parts[0], clips)
        + row_sums_scratch(parts[1], clips),
        compiler_params=pltpu.CompilerParams(
            collective_id=collective_id, has_side_effects=True, vmem_limit_bytes=62 * 2**20
        ),
        cost_estimate=pl.CostEstimate(
            flops=2**35, bytes_accessed=24 * 2**20, transcendentals=2**24
        ),
    )(*operands)


def newton_schulz(whole):
    wide = whole.astype(F32)
    norm = jnp.sqrt(jnp.sum(wide * wide)) + 1e-07
    eye = (
        lax.broadcasted_iota(jnp.int32, (D, D), 0) == lax.broadcasted_iota(jnp.int32, (D, D), 1)
    ).astype(F32)
    turned = dot_nt(eye.astype(BF), whole) / norm

    def iterate(step, current):
        held = current.astype(BF)
        gram = dot_nt(held, held)
        gram_low = gram.astype(BF)
        poly = POLY_TWO * gram + POLY_THREE * dot_nn(gram_low, gram_low)
        return POLY_ONE * current + dot_nn(poly.astype(BF), held)

    return lax.fori_loop(0, NS_STEPS, iterate, turned)


OWNER_OF = (3, 1, 0, 2)
QKV_AT = OWNER_OF[0]


def tail_kernel(
    clips,
    gnorm_ref,
    own_ref,
    across_ref,
    bsum_ref,
    tok_ref,
    gsec_ref,
    x_ref,
    side_ref,
    cells_ref,
    taps_ref,
    vec_ref,
    mid_sums_ref,
    one_ref,
    two_ref,
    qkv_m_ref,
    proj_m_ref,
    up_m_ref,
    down_m_ref,
    ingrad_ref,
    late_ref,
    scaled_ref,
    vsum_ref,
    cross_in,
    shares,
    shares_in,
    old_rows,
    new_rows,
    new_low,
    first,
    first_low,
    rim,
    outer,
    center,
    edged,
    v_mine,
    v_frames,
    v_total,
    v_clips,
    low,
    gathered,
    grad_sems,
    part_sems,
    row_sems,
    spread_sems,
    rim_sems,
    vf_sems,
    vc_sems,
    there_sems,
    back_sems,
):
    f, near, across, far = frame_peers()
    c = lax.axis_index("clip")
    block = own_ref.shape[0]
    owners, chunk = shares.shape[0], shares.shape[1]

    def each(count, act):
        def body(step, carry):
            act(step)
            return carry

        lax.fori_loop(0, count, body, 0)

    def other_clips(act):
        each(clips - 1, lambda step: act(lax.rem(c + 1 + step, clips)))

    @pl.when(f == QKV_AT)
    def _():
        gathered[:, owners * chunk : SHARE, :] = jnp.zeros((4, SHARE - owners * chunk, D), BF)

    proj_rows = proj_m_ref.shape[0]

    @pl.when(f == OWNER_OF[1])
    def _():
        gathered[:, proj_rows:SHARE, :] = jnp.zeros((4, SHARE - proj_rows, D), BF)

    greet_all(clips)
    barrier = pltpu.get_barrier_semaphore()

    def greet(clip, frame):
        pl.semaphore_signal(
            barrier, inc=1, device_id={"clip": clip, "frame": frame}, device_id_type=MESH
        )

    @pl.when(f == QKV_AT)
    def _():
        for step in (1, 2, 3):
            other_clips(lambda clip, step=step: greet(clip, (QKV_AT + step) % 4))

    @pl.when(f != QKV_AT)
    def _():
        other_clips(lambda clip: greet(clip, QKV_AT))

    down, up = halo_copies(first_low.at[0], first_low.at[1], rim, rim_sems)

    @pl.when(f == QKV_AT)
    def _():
        await_greetings(3 + 4 * (clips - 1))

    @pl.when(f != QKV_AT)
    def _():
        await_greetings(3 + 2 * (clips - 1))

    to_across = send(across_ref, cross_in, grad_sems.at[0], grad_sems.at[1], across)
    to_across.start()

    upstream = gnorm_ref[...]
    unit, scale = norm_parts(tok_ref[...])
    grad_first = gsec_ref[...] + norm_back(upstream, unit, scale, vec_ref[0:1, :])
    first[...] = grad_first
    first_low[...] = grad_first.astype(BF).reshape(first_low.shape)
    start_halos(down, up, rim)

    moments = (None, proj_m_ref, up_m_ref, down_m_ref)

    def to_owner(which):
        at = pl.ds(0, moments[which].shape[0])
        return send(
            low.at[which, at, :],
            gathered.at[f, at, :],
            there_sems.at[0, which],
            there_sems.at[1, f],
            OWNER_OF[which],
        )

    for which in (3, 2, 1):
        rows = moments[which].shape[0]
        summed = one_ref[80:400, :] if which == 2 else (two_ref if which == 3 else one_ref)[0:rows, :]
        low[which, 0:rows, :] = (0.95 * moments[which][...] + summed.astype(F32)).astype(BF)

        @pl.when(f != OWNER_OF[which])
        def _(which=which):
            to_owner(which).start()

    old_rows[0:block, :] = qkv_m_ref[...].T
    if owners * chunk > block:
        old_rows[block : owners * chunk, :] = jnp.zeros((owners * chunk - block, D), F32)

    v_mine[0:1, :] = column_sum(upstream * unit)
    v_mine[1:2, :] = column_sum(upstream)
    v_mine[2:4, :] = mid_sums_ref[0:2, :]
    v_mine[4:5, :] = column_sum(grad_first)
    v_mine[5:6, :] = jnp.concatenate(
        [bsum_ref[0, h, :, 0:HEAD_DIM] for h in range(HEADS)], axis=1
    )
    v_mine[6:7, :] = jnp.concatenate(
        [bsum_ref[1, h, :, HEAD_DIM:PAIR] for h in range(HEADS)], axis=1
    )
    v_mine[7:9, :] = mid_sums_ref[2:4, :]
    v_mine[9:13, :] = mid_sums_ref[4:8, :]

    cells = cells_ref[...]
    inside = inside_of(side_ref, cells)
    for t in range(2):
        build_slabs(center, edged, t + 1, first[400 * t : 400 * t + 400, :], cells)

    def part_copy(owner):
        return pltpu.make_async_remote_copy(
            src_ref=shares.at[owner],
            dst_ref=shares_in.at[c],
            send_sem=part_sems.at[0, owner],
            recv_sem=part_sems.at[1, c],
            device_id={"clip": owner},
            device_id_type=MESH,
        )

    def other_owners(act):
        def step(owner):
            @pl.when(owner != c)
            def _():
                act(owner)

        each(owners, step)

    to_across.wait()
    mine = (own_ref[...] + cross_in[...].astype(F32)).astype(BF)
    if owners * chunk > block:
        mine = jnp.concatenate([mine, jnp.zeros((owners * chunk - block, D), BF)], axis=0)
    shares[...] = mine.reshape(owners, chunk, D)
    other_owners(lambda owner: part_copy(owner).start())

    wait_halos(down, up)
    for side, slot in ((0, 0), (1, 3)):
        build_slabs(center, edged, slot, rim[side].astype(F32), cells)

    def row_copy(clip):
        return pltpu.make_async_remote_copy(
            src_ref=new_rows.at[c],
            dst_ref=new_rows.at[c],
            send_sem=row_sems.at[0, clip],
            recv_sem=row_sems.at[1, c],
            device_id={"clip": clip},
            device_id_type=MESH,
        )

    def spread_copy(clip):
        return pltpu.make_async_remote_copy(
            src_ref=new_low,
            dst_ref=gathered.at[f, pl.ds(pl.multiple_of(c * chunk, 16), chunk), :],
            send_sem=spread_sems.at[4, clip],
            recv_sem=spread_sems.at[f, c],
            device_id={"clip": clip, "frame": QKV_AT},
            device_id_type=MESH,
        )

    def share_sum():
        @pl.when(c < owners)
        def _():
            shares_in[c] = shares[c]

            def arrive(clip):
                pltpu.make_async_remote_copy(
                    src_ref=shares.at[0],
                    dst_ref=shares_in.at[clip],
                    send_sem=part_sems.at[0, 0],
                    recv_sem=part_sems.at[1, clip],
                    device_id={"clip": clip},
                    device_id_type=MESH,
                ).wait_recv()

            other_clips(arrive)

            def add_part(clip, total):
                return total + shares_in[clip].astype(F32)

            total = lax.fori_loop(0, clips, add_part, jnp.zeros((chunk, D), F32))
            at = pl.ds(pl.multiple_of(c * chunk, 16), chunk)
            fresh = 0.95 * old_rows[at, :] + total
            new_rows[c] = fresh
            new_low[...] = fresh.astype(BF)
            other_clips(lambda clip: spread_copy(clip).start())

            @pl.when(f != QKV_AT)
            def _():
                spread_copy(c).start()

            @pl.when(f == QKV_AT)
            def _():
                gathered[QKV_AT, at, :] = new_low[...]

            other_clips(lambda clip: row_copy(clip).start())

    for t in range(2):
        flatten_frame(lambda row, t=t: x_ref[0, t, row], outer, 0)
        outer[...] = jnp.where(inside, outer[...], 0.0)
        for a in range(3):

            def plane(step, totals, t=t, a=a):
                start = pl.multiple_of(step * 16, 16)
                at = pl.ds(pl.multiple_of(start + 400 * t, 16), 16)
                masked = outer[pl.ds(start, 16), :]
                total = jnp.zeros((16, D), F32)
                sums_out = []
                for b in range(3):
                    for e in range(3):
                        offset = 9 * a + 3 * b + e
                        piece = slab(center, edged, t + 2 - a, 2 - b, 2 - e, start, 16)
                        total = total + taps_ref[offset : offset + 1, :] * piece
                        product = masked * piece
                        sums_out.append(totals[3 * b + e] + (product[0:8, :] + product[8:16, :]))
                if a == 0:
                    ingrad_ref[at, :] = total
                else:
                    ingrad_ref[at, :] += total
                return tuple(sums_out)

            totals = lax.fori_loop(0, 25, plane, tuple(jnp.zeros((8, D), F32) for _ in range(9)))
            for which, total in enumerate(totals):
                at = slice(13 + 9 * a + which, 14 + 9 * a + which)
                if t == 0:
                    v_mine[at, :] = column_sum(total)
                else:
                    v_mine[at, :] += column_sum(total)
        at = slice(400 * t, 400 * t + 400)
        ingrad_ref[at, :] = first[at, :] + jnp.where(inside, ingrad_ref[at, :], 0.0)
        if t == 0:
            share_sum()

    v_copies = []
    for which, peer in enumerate((near, across, far)):
        copy = send(v_mine, v_frames.at[f], vf_sems.at[0, which], vf_sems.at[1, which], peer)
        copy.start()
        v_copies.append(copy)
    v_frames[f] = v_mine[...]

    @pl.when(f == QKV_AT)
    def _():
        def rows_arrive(frame, clip):
            pltpu.make_async_remote_copy(
                src_ref=new_low,
                dst_ref=gathered.at[frame, pl.ds(pl.multiple_of(clip * chunk, 16), chunk), :],
                send_sem=spread_sems.at[4, clip],
                recv_sem=spread_sems.at[frame, clip],
                device_id={"clip": clip, "frame": frame},
                device_id_type=MESH,
            ).wait_recv()

        other_owners(lambda clip: rows_arrive(QKV_AT, clip))
        for step in (1, 2, 3):
            frame = (QKV_AT + step) % 4
            each(owners, lambda clip, frame=frame: rows_arrive(frame, clip))

    for which in (1, 2, 3):

        @pl.when(f != OWNER_OF[which])
        def _(which=which):
            to_owner(which).wait_send()

        @pl.when(f == OWNER_OF[which])
        def _(which=which):
            at = pl.ds(0, moments[which].shape[0])
            gathered[OWNER_OF[which], at, :] = low[which, at, :]
            for other in range(4):
                if other != OWNER_OF[which]:
                    send(
                        low.at[0, at, :],
                        gathered.at[other, at, :],
                        there_sems.at[0, 0],
                        there_sems.at[1, other],
                        other,
                    ).wait_recv()

    turned = newton_schulz(gathered[...].reshape(4 * SHARE, D))
    low[...] = turned.T.astype(BF).reshape(low.shape)
    row_counts = (block, *(ref.shape[0] for ref in moments[1:]))

    def back_copy(which, step):
        at = pl.ds(0, row_counts[which])
        to = (OWNER_OF[which] + step) % 4
        return send(
            low.at[to, at, :],
            scaled_ref.at[which, at, :],
            back_sems.at[0, step],
            back_sems.at[1, which],
            to,
        )

    for which in range(4):

        @pl.when(f == OWNER_OF[which])
        def _(which=which):
            for step in (2, 1, 3):
                back_copy(which, step).start()
            at = pl.ds(0, row_counts[which])
            scaled_ref[which, at, :] = low[OWNER_OF[which], at, :]

    for copy in v_copies:
        copy.wait()
    v_total[...] = v_frames[0] + v_frames[1] + v_frames[2] + v_frames[3]

    def v_copy(clip):
        return pltpu.make_async_remote_copy(
            src_ref=v_total,
            dst_ref=v_clips.at[c],
            send_sem=vc_sems.at[0, clip],
            recv_sem=vc_sems.at[1, c],
            device_id={"clip": clip},
            device_id_type=MESH,
        )

    other_clips(lambda clip: v_copy(clip).start())
    v_clips[c] = v_total[...]

    other_owners(lambda owner: part_copy(owner).wait_send())

    @pl.when(c < owners)
    def _():
        other_clips(lambda clip: spread_copy(clip).wait_send())

        @pl.when(f != QKV_AT)
        def _():
            spread_copy(c).wait_send()

        other_clips(lambda clip: row_copy(clip).wait_send())

    def new_rows_arrive(clip):
        pltpu.make_async_remote_copy(
            src_ref=new_rows.at[0],
            dst_ref=new_rows.at[clip],
            send_sem=row_sems.at[0, 0],
            recv_sem=row_sems.at[1, clip],
            device_id={"clip": clip},
            device_id_type=MESH,
        ).wait_recv()

    other_owners(new_rows_arrive)
    late_ref[...] = new_rows[...].reshape(late_ref.shape)

    def v_arrives(clip):
        v_copy(clip).wait_send()
        pltpu.make_async_remote_copy(
            src_ref=v_total,
            dst_ref=v_clips.at[clip],
            send_sem=vc_sems.at[0, clip],
            recv_sem=vc_sems.at[1, clip],
            device_id={"clip": clip},
            device_id_type=MESH,
        ).wait_recv()

    other_clips(v_arrives)

    def add_v(step, total):
        return total + v_clips[step]

    vsum_ref[...] = lax.fori_loop(0, clips, add_v, jnp.zeros(vsum_ref.shape, F32))
    for which in range(4):

        @pl.when(f == OWNER_OF[which])
        def _(which=which):
            for step in (2, 1, 3):
                back_copy(which, step).wait_send()

        @pl.when(f != OWNER_OF[which])
        def _(which=which):
            back_copy(which, 1).wait_recv()


def tail_part(operands, clips, qkv_rows, collective_id):
    rows = 800
    chunk = share_rows(qkv_rows, clips)
    owners = -(-qkv_rows // chunk)
    vector_shape = (40, D)
    vmem = pltpu.VMEM
    dma = pltpu.SemaphoreType.DMA
    return pl.pallas_call(
        functools.partial(tail_kernel, clips),
        in_specs=[VMEM_SPEC] * 7 + [pl.BlockSpec(memory_space=pltpu.SMEM)] + [VMEM_SPEC] * 10,
        out_specs=[VMEM_SPEC] * 4,
        out_shape=[
            jax.ShapeDtypeStruct((rows, D), F32),
            jax.ShapeDtypeStruct((owners * chunk, D), F32),
            jax.ShapeDtypeStruct((4, SHARE, D), BF),
            jax.ShapeDtypeStruct(vector_shape, F32),
        ],
        scratch_shapes=[
            vmem((qkv_rows, D), BF),
            vmem((owners, chunk, D), BF),
            vmem((clips, chunk, D), BF),
            vmem((owners * chunk, D), F32),
            vmem((owners, chunk, D), F32),
            vmem((chunk, D), BF),
            vmem((rows, D), F32),
            vmem((2, 400, D), BF),
            vmem((2, 400, D), BF),
            vmem((400, D), F32),
            vmem((3, 4, 400, D), F32),
            vmem((3, 4, 440, D), F32),
            vmem(vector_shape, F32),
            vmem((4,) + vector_shape, F32),
            vmem(vector_shape, F32),
            vmem((clips,) + vector_shape, F32),
            vmem((4, SHARE, D), BF),
            vmem((4, SHARE, D), BF),
            dma((2,)),
            dma((2, clips)),
            dma((2, clips)),
            dma((5, clips)),
            dma((2, 2)),
            dma((2, 3)),
            dma((2, clips)),
            dma((2, 4)),
            dma((2, 4)),
        ],
        compiler_params=pltpu.CompilerParams(
            collective_id=collective_id, has_side_effects=True, vmem_limit_bytes=60 * 2**20
        ),
        cost_estimate=pl.CostEstimate(
            flops=2**33, bytes_accessed=16 * 2**20, transcendentals=2**20
        ),
    )(*operands)


def adamw(param, mean_old, square_old, gradient, rate_value, decay):
    mean_new = 0.9 * mean_old + 0.1 * gradient
    square_new = 0.999 * square_old + 0.001 * gradient * gradient
    mean_hat = mean_new / (1.0 - 0.9**STEP)
    square_hat = square_new / (1.0 - 0.999**STEP)
    return (
        mean_new,
        square_new,
        param - rate_value * (mean_hat / (jnp.sqrt(square_hat) + 1e-08) + decay * param),
    )


RATES = (0.2 * math.sqrt(3.0), 0.12 * math.sqrt(CLIP_TOK), 0.2 * math.sqrt(FF / D), 0.2)


def update_kernel(*refs):
    ingrad_ref, late_ref, one_ref, two_ref, scaled_ref, vsum_ref = refs[:6]
    weights, moments, vectors, taps = refs[6:10], refs[10:13], refs[13:16], refs[16:19]
    out_ref, new_moments, new_weights = refs[19], refs[20:24], refs[24:28]
    new_vectors, new_taps = refs[28:31], refs[31:34]
    for t in range(2):
        for row in range(20):
            at = 400 * t + 20 * row
            out_ref[0, t, row] = ingrad_ref[at : at + 20, :]
    rows = weights[0].shape[1]
    new_moments[0][...] = late_ref[0:rows, :].T
    new_weights[0][...] = 0.999 * weights[0][...] - RATES[0] * (
        scaled_ref[0, 0:rows, :].astype(F32).T
    )
    for which in (1, 2, 3):
        rows = weights[which].shape[0]
        summed = one_ref[80:400, :] if which == 2 else (two_ref if which == 3 else one_ref)[0:rows, :]
        new_moments[which][...] = 0.95 * moments[which - 1][...] + summed.astype(F32)
        new_weights[which][...] = 0.999 * weights[which][...] - RATES[which] * scaled_ref[
            which, 0:rows, :
        ].astype(F32)
    for (param, mean, square), outs, at, rate, decay in (
        (vectors, new_vectors, slice(0, 9), 0.2, 0.0),
        (taps, new_taps, slice(13, 40), 0.05, 0.01),
    ):
        for ref, value in zip(
            outs, adamw(param[...], mean[...], square[...], vsum_ref[at, :], rate, decay)
        ):
            ref[...] = value


def update(ingrad, late, one, two, scaled, vector_sums, weights, moments, vectors, taps, grid_shape):
    operands = [ingrad, late, one, two, scaled, vector_sums, *weights, *moments[1:], *vectors, *taps]
    outs = [jax.ShapeDtypeStruct(grid_shape, F32)]
    outs += [jax.ShapeDtypeStruct(x.shape, F32) for x in (*moments, *weights, *vectors, *taps)]
    return pl.pallas_call(
        update_kernel,
        in_specs=[VMEM_SPEC] * len(operands),
        out_specs=[VMEM_SPEC] * len(outs),
        out_shape=outs,
        compiler_params=pltpu.CompilerParams(vmem_limit_bytes=62 * 2**20),
        cost_estimate=pl.CostEstimate(
            flops=2**22, bytes_accessed=12 * 2**20, transcendentals=2**14
        ),
    )(*operands)


def per_device(
    clips_in,
    out_grad,
    clip_side,
    qkv_weight,
    proj_weight,
    up_weight,
    down_weight,
    qkv_moment,
    proj_moment,
    up_moment,
    down_moment,
    vectors,
    vector_mean,
    vector_square,
    up_bias,
    up_bias_mean,
    up_bias_square,
    conv_kernel,
    kernel_mean,
    kernel_square,
):
    clips = lax.axis_size("clip")
    weights = (qkv_weight, proj_weight, up_weight, down_weight)
    moments = (qkv_moment, proj_moment, up_moment, down_moment)
    (
        tokens,
        normed_home,
        normed_cross,
        heads_q,
        home,
        cross,
        kept,
        heads_out,
        query_weight,
        pair_weight,
        other_weights,
    ) = front(clips_in, clip_side, qkv_weight.T, *weights[1:], vectors, conv_kernel, clips, 0)
    block_out, grad_second, douts, early_grads, mid_sums = middle(
        heads_out,
        tokens,
        out_grad,
        clip_side,
        vectors,
        up_bias.reshape(1, FF),
        other_weights,
    )
    grad_normed, qkv_own, qkv_out, bias_sums, sums_one, sums_two = attention_back(
        (
            heads_q,
            douts,
            kept,
            cross,
            home,
            normed_home,
            normed_cross,
            query_weight,
            pair_weight,
            clip_side,
            jnp.asarray(CELL_AT),
            early_grads,
        ),
        clips,
        1,
    )
    ingrad, late_moment, scaled, vector_sums = tail_part(
        (
            grad_normed,
            qkv_own,
            qkv_out,
            bias_sums,
            tokens,
            grad_second,
            clips_in,
            clip_side,
            jnp.asarray(CELL_AT),
            conv_kernel,
            vectors,
            mid_sums,
            sums_one,
            sums_two,
            qkv_moment.T,
            *moments[1:],
        ),
        clips,
        qkv_weight.shape[0],
        2,
    )
    updated = update(
        ingrad,
        late_moment,
        sums_one,
        sums_two,
        scaled,
        vector_sums,
        (qkv_weight.T, *weights[1:]),
        (qkv_moment.T, *moments[1:]),
        (vectors, vector_mean, vector_square),
        (conv_kernel, kernel_mean, kernel_square),
        clips_in.shape,
    )
    input_grad = updated[0]
    new_moments = (updated[1].T, *updated[2:5])
    new_weights = (updated[5].T, *updated[6:9])
    bias_new = adamw(
        up_bias, up_bias_mean, up_bias_square, vector_sums[9:13].reshape(FF), 0.2, 0.0
    )
    outs = [block_out, input_grad]
    for moment, weight in zip(new_moments, new_weights):
        outs += [moment, weight]
    return (*outs, *updated[9:12], *bias_new, *updated[12:15])


def solution(mesh):
    big = P("clip", "frame", None, None, None)
    rows = P("frame", None)
    return jax.shard_map(
        per_device,
        mesh=mesh,
        in_specs=(big, big, P("clip")) + (rows,) * 8 + (P(),) * 9,
        out_specs=(big, big) + (rows,) * 8 + (P(),) * 9,
        check_vma=False,
    )
```

```python
import functools
import math

import jax
import jax.numpy as jnp
import numpy as np
from jax import lax
from jax.experimental import pallas as pl
from jax.experimental.pallas import tpu as pltpu
from jax.sharding import PartitionSpec as P

D = 320
HEADS = 5
HEAD_DIM = 64
PAIR = 2 * HEAD_DIM
WIDE = HEADS * PAIR
FF = 1280
NS_STEPS = 5
STEP = 10
CLIP_TOK = 3200
SHARE = 320

POLY_ONE = 3.4445
POLY_TWO = -4.775
POLY_THREE = 2.0315
LOG2E = math.log2(math.e)
SCORE_SCALE = HEAD_DIM**-0.5
MASKED = -1e30
MESH = pl.DeviceIdType.MESH
BF = jnp.bfloat16
F32 = jnp.float32
NT = (((1,), (1,)), ((), ()))
VMEM_SPEC = pl.BlockSpec(memory_space=pltpu.VMEM)


def dot_nt(left, right):
    return lax.dot_general(left, right, NT, preferred_element_type=F32)


def dot_nn(left, right):
    return jnp.dot(left, right, preferred_element_type=F32)


def lanes_of(rows):
    return lax.broadcasted_iota(jnp.int32, (rows, PAIR), 1)


CELL_AT = np.stack([np.arange(400) // 20, np.arange(400) % 20], axis=1).astype(np.float32)


def select_lanes(upper):
    row = lax.broadcasted_iota(jnp.int32, (D, WIDE), 0)
    col = lax.broadcasted_iota(jnp.int32, (D, WIDE), 1)
    source = lax.shift_left(lax.shift_right_logical(col, 7), 6) + (col & (HEAD_DIM - 1))
    half = col & HEAD_DIM
    return (source == row) & (half == (HEAD_DIM if upper else 0))


def flatten_frame(read_row, dst, base):
    for row in range(20):
        dst[base + 20 * row : base + 20 * row + 20, :] = read_row(row).astype(F32)


def build_slabs(center, edged, slot, flat, cells):
    blank = jnp.zeros((20, D), F32)
    edged[1, slot, 0:20, :] = blank
    edged[1, slot, 420:440, :] = blank
    edged[1, slot, 20:420, :] = flat
    center[1, slot] = flat
    col = cells[:, 1:2]
    for e, keep in ((0, col > 0.5), (2, col < 18.5)):
        moved = jnp.where(keep, edged[1, slot, 19 + e : 419 + e, :], 0.0)
        center[e, slot] = moved
        edged[e, slot, 0:20, :] = blank
        edged[e, slot, 420:440, :] = blank
        edged[e, slot, 20:420, :] = moved


def slab(center, edged, slot, b, e, start, size):
    if b == 1:
        return center[e, slot, pl.ds(start, size), :]
    return edged[e, slot, pl.ds(start + 20 * b, size), :]


def inside_of(side_ref, cells):
    side = side_ref[0].astype(F32) - 0.5
    return (cells[:, 0:1] < side) & (cells[:, 1:2] < side)


def norm_parts(rows):
    average = jnp.sum(rows, axis=-1, keepdims=True) * (1.0 / D)
    centered = rows - average
    variance = jnp.sum(centered * centered, axis=-1, keepdims=True) * (1.0 / D)
    scale = lax.rsqrt(variance + 1e-05)
    return centered * scale, scale


def frame_peers():
    f = lax.axis_index("frame")
    near = f + 1 - 2 * lax.rem(f, 2)
    across = lax.rem(f + 2, 4)
    return f, near, across, lax.rem(near + 2, 4)


def share_rows(rows, clips):
    return 16 * (-(-rows // (16 * clips)))


def greet_all(clips):
    barrier = pltpu.get_barrier_semaphore()
    for peer in frame_peers()[1:]:
        pl.semaphore_signal(barrier, inc=1, device_id={"frame": peer}, device_id_type=MESH)
    c = lax.axis_index("clip")

    def greet(step, carry):
        pl.semaphore_signal(
            barrier, inc=1, device_id={"clip": lax.rem(c + step, clips)}, device_id_type=MESH
        )
        return carry

    lax.fori_loop(1, clips, greet, 0)


def await_greetings(count):
    pl.semaphore_wait(pltpu.get_barrier_semaphore(), count)


def send(src, dst, send_sem, recv_sem, peer):
    return pltpu.make_async_remote_copy(
        src_ref=src,
        dst_ref=dst,
        send_sem=send_sem,
        recv_sem=recv_sem,
        device_id={"frame": peer},
        device_id_type=MESH,
    )


def halo_copies(first, last, halo, sems):
    f = lax.axis_index("frame")
    down = send(first, halo.at[1], sems.at[0, 0], sems.at[1, 0], jnp.maximum(f - 1, 0))
    up = send(last, halo.at[0], sems.at[0, 1], sems.at[1, 1], jnp.minimum(f + 1, 3))
    return down, up


def start_halos(down, up, halo):
    f = lax.axis_index("frame")

    @pl.when(f > 0)
    def _():
        down.start()

    @pl.when(f < 3)
    def _():
        up.start()

    @pl.when(f == 0)
    def _():
        halo[0] = jnp.zeros(halo.shape[1:], halo.dtype)

    @pl.when(f == 3)
    def _():
        halo[1] = jnp.zeros(halo.shape[1:], halo.dtype)


def wait_halos(down, up):
    f = lax.axis_index("frame")

    @pl.when(f > 0)
    def _():
        down.wait_send()
        up.wait_recv()

    @pl.when(f < 3)
    def _():
        up.wait_send()
        down.wait_recv()


EXP_SCALE = SCORE_SCALE * LOG2E


def tail_lanes(inside, copies):
    lane = lax.broadcasted_iota(jnp.int32, (inside.shape[0], PAIR), 1)
    tail = jnp.where(
        lane == HEAD_DIM,
        jnp.where(inside, 0.0, MASKED),
        jnp.where((lane > HEAD_DIM) & (lane < HEAD_DIM + 4), 1.0, 0.0),
    )
    return jnp.concatenate([tail] * copies, axis=0).astype(BF)


def front_kernel(
    clips,
    x_ref,
    side_ref,
    cells_ref,
    qkv_ref,
    proj_ref,
    up_ref,
    down_ref,
    vec_ref,
    taps_ref,
    tok_out,
    nhome_out,
    ncross_out,
    q_out,
    home_out,
    cross_out,
    kept_out,
    att_out,
    wq_out,
    wkv_out,
    others_out,
    tok_ref,
    nhome_ref,
    ncross_ref,
    q_ref,
    home_ref,
    cross_ref,
    kept_ref,
    att_ref,
    wq_ref,
    wkv_ref,
    others_ref,
    halo_ref,
    raw,
    outer,
    center,
    edged,
    qkv_full,
    tail,
    halo_sems,
    qkv_sems,
    other_sems,
    spread_sems,
    near_sems,
    cross_sems,
    out_sems,
):
    leaving = []

    def leave(src, dst):
        copy = pltpu.make_async_copy(src, dst, out_sems.at[len(leaving)])
        copy.start()
        leaving.append(copy)

    f, near, across, far = frame_peers()
    c = lax.axis_index("clip")
    greet_all(clips)
    part_rows = qkv_ref.shape[1]

    def qkv_rows(owner):
        return qkv_full.at[pl.ds(pl.multiple_of(owner * part_rows, 16), part_rows), :]

    qkv_full[pl.ds(pl.multiple_of(f * part_rows, 16), part_rows), :] = qkv_ref[...].T.astype(BF)
    start = 0
    for shard in (proj_ref, up_ref, down_ref):
        size = shard.shape[0]
        others_ref[f, start : start + size, :] = shard[...].astype(BF)
        start += size
    spare = others_ref.shape[1] - start
    if spare:
        others_ref[f, start : start + spare, :] = jnp.zeros((spare, D), BF)
    cells = cells_ref[...]
    inside = inside_of(side_ref, cells)
    for t in range(2):
        flatten_frame(lambda row, t=t: x_ref[0, t, row], raw, 400 * t)

    await_greetings(3 + clips - 1)
    down, up = halo_copies(x_ref.at[0, 0], x_ref.at[0, 1], halo_ref, halo_sems)
    start_halos(down, up, halo_ref)
    qkv_cross = send(qkv_rows(f), qkv_rows(f), qkv_sems.at[0, 1], qkv_sems.at[1, 1], across)
    qkv_near = send(qkv_rows(f), qkv_rows(f), qkv_sems.at[0, 0], qkv_sems.at[1, 0], near)
    qkv_relay = send(
        qkv_rows(across), qkv_rows(across), qkv_sems.at[0, 2], qkv_sems.at[1, 2], near
    )
    qkv_cross.start()
    qkv_near.start()

    part = others_ref.shape[1] // clips

    def part_of(owner, clip):
        return others_ref.at[owner, pl.ds(pl.multiple_of(clip * part, 16), part), :]

    other_near = send(
        others_ref.at[f], others_ref.at[f], other_sems.at[0, 0], other_sems.at[1, 0], near
    )
    other_cross = send(
        part_of(f, c), part_of(f, c), other_sems.at[0, 1], other_sems.at[1, 1], across
    )
    other_relay = send(
        others_ref.at[across],
        others_ref.at[across],
        other_sems.at[0, 2],
        other_sems.at[1, 2],
        near,
    )

    def spread(clip, landing):
        return pltpu.make_async_remote_copy(
            src_ref=part_of(across, c),
            dst_ref=part_of(across, landing),
            send_sem=spread_sems.at[0, clip],
            recv_sem=spread_sems.at[1, landing],
            device_id={"clip": clip},
            device_id_type=MESH,
        )

    def other_clips(act):
        def body(step, carry):
            act(lax.rem(c + step, clips))
            return carry

        lax.fori_loop(1, clips, body, 0)

    other_cross.start()
    other_near.start()

    for t in range(2):
        build_slabs(
            center, edged, t + 1, jnp.where(inside, raw[400 * t : 400 * t + 400, :], 0.0), cells
        )

    def conv_part(t, depths, start, total):
        for a in depths:
            for b in range(3):
                for e in range(3):
                    offset = 9 * a + 3 * b + e
                    total = total + taps_ref[offset : offset + 1, :] * slab(
                        center, edged, t + a, b, e, start, 40
                    )
        return total

    for t, depths in ((0, (1, 2)), (1, (0, 1))):

        def own_part(step, carry, t=t, depths=depths):
            start = pl.multiple_of(step * 40, 8)
            at = pl.ds(pl.multiple_of(start + 400 * t, 8), 40)
            tok_ref[at, :] = conv_part(t, depths, start, raw[at, :] + vec_ref[4:5, :])
            return carry

        lax.fori_loop(0, 10, own_part, 0)
    other_cross.wait_recv()
    other_clips(lambda clip: spread(clip, c).start())
    qkv_cross.wait_recv()
    qkv_relay.start()
    wait_halos(down, up)
    for side, slot in ((0, 0), (1, 3)):
        flatten_frame(lambda row, side=side: halo_ref[side, row], outer, 0)
        build_slabs(center, edged, slot, jnp.where(inside, outer[...], 0.0), cells)
    for t, depths in ((0, (0,)), (1, (2,))):

        def rim_part(step, carry, t=t, depths=depths):
            start = pl.multiple_of(step * 40, 8)
            at = pl.ds(pl.multiple_of(start + 400 * t, 8), 40)
            rows = conv_part(t, depths, start, tok_ref[at, :])
            tok_ref[at, :] = rows
            raw[at, :] = norm_parts(rows)[0] * vec_ref[0:1, :] + vec_ref[1:2, :]
            return carry

        lax.fori_loop(0, 10, rim_part, 0)
    rows = tok_ref.shape[0]
    nhome_ref[0:rows, :] = raw[...].astype(BF)

    piece = rows // HEADS

    def cross_copy(k):
        at = pl.ds(pl.multiple_of(k * piece, 16), piece)
        return send(
            nhome_ref.at[at, :],
            ncross_ref.at[at, :],
            cross_sems.at[0, 0, k],
            cross_sems.at[1, 0, k],
            across,
        )

    def relay_copy(k):
        return send(
            ncross_ref.at[pl.ds(pl.multiple_of(k * piece, 16), piece), :],
            ncross_ref.at[pl.ds(pl.multiple_of(rows + k * piece, 16), piece), :],
            cross_sems.at[0, 1, k],
            cross_sems.at[1, 1, k],
            near,
        )

    near_copy = send(
        nhome_ref.at[pl.ds(0, rows), :],
        nhome_ref.at[pl.ds(rows, rows), :],
        near_sems.at[0],
        near_sems.at[1],
        near,
    )
    for k in range(HEADS):
        cross_copy(k).start()
    near_copy.start()

    blank = jnp.zeros((1, HEAD_DIM), F32)

    def head_bias(row, h):
        return vec_ref[row : row + 1, HEAD_DIM * h : HEAD_DIM * (h + 1)]

    qkv_near.wait_recv()
    qkv_relay.wait_recv()
    for h in range(HEADS):
        wq_ref[PAIR * h : PAIR * h + HEAD_DIM, :] = qkv_full[HEAD_DIM * h : HEAD_DIM * (h + 1), :]
        wq_ref[PAIR * h + HEAD_DIM : PAIR * (h + 1), :] = jnp.zeros((HEAD_DIM, D), BF)
        wkv_ref[PAIR * h : PAIR * h + HEAD_DIM, :] = qkv_full[
            D + HEAD_DIM * h : D + HEAD_DIM * (h + 1), :
        ]
        wkv_ref[PAIR * h + HEAD_DIM : PAIR * (h + 1), :] = qkv_full[
            2 * D + HEAD_DIM * h : 2 * D + HEAD_DIM * (h + 1), :
        ]
    leave(tok_ref, tok_out)
    leave(wq_ref, wq_out)
    leave(wkv_ref, wkv_out)
    wide_query = jnp.concatenate(
        [part for h in range(HEADS) for part in (head_bias(5, h), blank)], axis=1
    )
    wide_pair = jnp.concatenate(
        [part for h in range(HEADS) for part in (blank, head_bias(6, h))], axis=1
    )

    def project(normed, weight, bias, place):
        joined = (dot_nt(normed, weight[...]) + bias).astype(BF)
        for h in range(HEADS):
            place(h, joined[:, PAIR * h : PAIR * (h + 1)])

    def place_query(h, value):
        q_ref[h] = value

    def place_own(h, value):
        home_ref[h, 0:rows, :] = value

    def place_near(h, value):
        home_ref[h, rows : 2 * rows, :] = value

    def place_cross(h, value):
        cross_ref[h] = value

    project(nhome_ref[0:rows, :], wq_ref, wide_query, place_query)
    project(nhome_ref[0:rows, :], wkv_ref, wide_pair, place_own)
    leave(q_ref, q_out)
    tail[...] = tail_lanes(inside, 4)
    tile = rows // 2
    mask_lane = jnp.where(lanes_of(tile) == HEAD_DIM, 1.0, 0.0).astype(BF)

    def tile_pass(t, source, last):
        at = pl.ds(pl.multiple_of(t * tile, 16), tile)
        lane = lanes_of(tile)
        for h in range(HEADS):
            keys = jnp.concatenate([source[h], tail[...]], axis=1)
            score = dot_nt(jnp.concatenate([q_ref[h, at, :], mask_lane], axis=1), keys)
            peak = jnp.max(score, axis=-1, keepdims=True)
            if last:
                kept = kept_ref[h, at, :]
                old_peak = kept[:, 0:1]
                peak = jnp.maximum(peak, old_peak)
            terms = jnp.exp2((score - peak) * EXP_SCALE).astype(BF)
            mixed = dot_nn(terms, keys)
            total = mixed[:, PAIR + HEAD_DIM + 1 : PAIR + HEAD_DIM + 2]
            mixed = mixed[:, 0:PAIR]
            if last:
                fade = jnp.exp2((old_peak - peak) * EXP_SCALE)
                total = total + fade * kept[:, 32:33]
                mixed = (mixed + fade * kept) / total
                log_sum = peak + jnp.log2(total) * (1.0 / EXP_SCALE)
                kept_ref[h, at, :] = jnp.where(lane < HEAD_DIM, log_sum, mixed)
                att_ref[h, at, :] = jnp.where(lane < HEAD_DIM, 0.0, mixed).astype(BF)
            else:
                kept_ref[h, at, :] = jnp.where(
                    lane < 32, peak, jnp.where(lane < HEAD_DIM, total, mixed)
                )

    def pass_on(k):
        cross_copy(k).wait_recv()
        relay_copy(k).start()

    def first_pass(t, carry):
        tile_pass(t, home_ref, False)

        @pl.when(t == 0)
        def _():
            for k in (0, 1, 2):
                pass_on(k)

        return carry

    def second_pass(t, carry):
        tile_pass(t, cross_ref, True)

        @pl.when(t == 0)
        def _():
            other_clips(lambda clip: spread(clip, clip).wait_recv())
            other_relay.start()

        return carry

    near_copy.wait_recv()
    leave(nhome_ref, nhome_out)
    project(nhome_ref[rows : 2 * rows, :], wkv_ref, wide_pair, place_near)
    leave(home_ref, home_out)
    lax.fori_loop(0, 2, first_pass, 0)
    for k in (3, 4):
        pass_on(k)
    for k in range(HEADS):
        relay_copy(k).wait_recv()
    leave(ncross_ref, ncross_out)
    project(ncross_ref[...], wkv_ref, wide_pair, place_cross)
    leave(cross_ref, cross_out)
    lax.fori_loop(0, 2, second_pass, 0)
    leave(kept_ref, kept_out)
    leave(att_ref, att_out)
    other_near.wait()
    other_relay.wait()
    leave(others_ref, others_out)
    other_clips(lambda clip: spread(clip, c).wait_send())
    for copy in (other_cross, near_copy, qkv_cross, qkv_near, qkv_relay):
        copy.wait_send()
    for k in range(HEADS):
        cross_copy(k).wait_send()
        relay_copy(k).wait_send()
    for copy in leaving:
        copy.wait()


def front(clips_in, clip_side, qkv, proj, up, down, vectors, taps, clips, collective_id):
    rows = 800
    other_rows = clips * share_rows(proj.shape[0] + up.shape[0] + down.shape[0], clips)
    outs = (
        ((rows, D), F32),
        ((2 * rows, D), BF),
        ((2 * rows, D), BF),
        ((HEADS, rows, PAIR), BF),
        ((HEADS, 2 * rows, PAIR), BF),
        ((HEADS, 2 * rows, PAIR), BF),
        ((HEADS, rows, PAIR), F32),
        ((HEADS, rows, PAIR), BF),
        ((WIDE, D), BF),
        ((WIDE, D), BF),
        ((4, other_rows, D), BF),
    )
    return pl.pallas_call(
        functools.partial(front_kernel, clips),
        in_specs=[VMEM_SPEC, pl.BlockSpec(memory_space=pltpu.SMEM)] + [VMEM_SPEC] * 7,
        out_specs=[pl.BlockSpec(memory_space=pl.ANY)] * len(outs),
        out_shape=[jax.ShapeDtypeStruct(*out) for out in outs],
        scratch_shapes=[pltpu.VMEM(*out) for out in outs]
        + [
            pltpu.VMEM((2, 20, 20, D), BF),
            pltpu.VMEM((rows, D), F32),
            pltpu.VMEM((400, D), F32),
            pltpu.VMEM((3, 4, 400, D), F32),
            pltpu.VMEM((3, 4, 440, D), F32),
            pltpu.VMEM((3 * D, D), BF),
            pltpu.VMEM((2 * rows, PAIR), BF),
            pltpu.SemaphoreType.DMA((2, 2)),
            pltpu.SemaphoreType.DMA((2, 3)),
            pltpu.SemaphoreType.DMA((2, 3)),
            pltpu.SemaphoreType.DMA((2, clips)),
            pltpu.SemaphoreType.DMA((2,)),
            pltpu.SemaphoreType.DMA((2, 2, HEADS)),
            pltpu.SemaphoreType.DMA((len(outs),)),
        ],
        compiler_params=pltpu.CompilerParams(
            collective_id=collective_id, has_side_effects=True, vmem_limit_bytes=60 * 2**20
        ),
        cost_estimate=pl.CostEstimate(
            flops=2**34, bytes_accessed=16 * 2**20, transcendentals=2**23
        ),
    )(clips_in, clip_side, jnp.asarray(CELL_AT), qkv, proj, up, down, vectors, taps)


INV_SQRT2 = math.sqrt(0.5)
INV_SQRT_2PI = 1.0 / math.sqrt(2.0 * math.pi)


def dot_tn(left, right):
    return lax.dot_general(left, right, (((0,), (0,)), ((), ())), preferred_element_type=F32)


def norm_back(upstream, unit, scale, gain):
    through = upstream * gain
    mean_one = jnp.sum(through, axis=-1, keepdims=True) * (1.0 / D)
    mean_two = jnp.sum(through * unit, axis=-1, keepdims=True) * (1.0 / D)
    return scale * (through - mean_one - unit * mean_two)


def column_sum(rows):
    return jnp.sum(rows, axis=0, keepdims=True)


def mid_phase(
    att_ref,
    tok_ref,
    og_ref,
    side_ref,
    cells_ref,
    vec_ref,
    ubias_ref,
    others_ref,
    out_ref,
    gsec_ref,
    dout_ref,
    grads_ref,
    vsum_ref,
    raw,
    wide,
    act,
    ghid,
    normed,
    top,
    branch_low,
    att_low,
    proj_ref,
    up_ref,
    down_ref,
):
    start = 0
    for full in (proj_ref, up_ref, down_ref):
        size = full.shape[0] // 4
        for owner in range(4):
            full[size * owner : size * (owner + 1), :] = others_ref[owner, start : start + size, :]
        start += size
    inside = inside_of(side_ref, cells_ref[...])
    pick = select_lanes(True).astype(F32).astype(BF)
    wide[...] = dot_nn(proj_ref[...], pick).astype(BF)
    vsum_ref[...] = jnp.zeros(vsum_ref.shape, F32)
    for t in range(2):
        at = slice(400 * t, 400 * t + 400)
        heads = jnp.concatenate([att_ref[h, at, :] for h in range(HEADS)], axis=1)
        att_low[at, :] = dot_nt(heads, pick).astype(BF)
        second = tok_ref[at, :] + (dot_nt(heads, wide[...]) + vec_ref[7:8, :])
        unit, scale = norm_parts(second)
        normed_two = (unit * vec_ref[2:3, :] + vec_ref[3:4, :]).astype(BF)
        normed[at, :] = normed_two
        flatten_frame(lambda row, t=t: og_ref[0, t, row], raw, 0)
        grad_top = jnp.where(inside, raw[...], 0.0)
        top_low = grad_top.astype(BF)
        top[at, :] = top_low
        hidden = dot_nt(normed_two, up_ref[...]) + ubias_ref[...]
        half = 0.5 + 0.5 * lax.erf(hidden * INV_SQRT2)
        activated = (hidden * half).astype(BF)
        act[at, :] = activated
        slope = half + hidden * (INV_SQRT_2PI * jnp.exp(-0.5 * hidden * hidden))
        grad_hidden = (dot_nt(top_low, down_ref[...]) * slope).astype(BF)
        ghid[at, :] = grad_hidden
        raw[...] = second + (dot_nn(activated, down_ref[...]) + vec_ref[8:9, :])
        for row in range(20):
            out_ref[0, t, row] = raw[20 * row : 20 * row + 20, :].astype(BF)
        upstream = dot_nn(grad_hidden, up_ref[...])
        grad_second = grad_top + norm_back(upstream, unit, scale, vec_ref[2:3, :])
        gsec_ref[at, :] = grad_second
        low = grad_second.astype(BF)
        branch_low[at, :] = low
        dout = dot_nn(low, wide[...]).astype(BF)
        for h in range(HEADS):
            dout_ref[h, at, :] = dout[:, PAIR * h : PAIR * (h + 1)]
        vsum_ref[0:1, :] += column_sum(upstream * unit)
        vsum_ref[1:2, :] += column_sum(upstream)
        vsum_ref[2:3, :] += column_sum(low.astype(F32))
        vsum_ref[3:4, :] += column_sum(grad_top)
        bias_sum = column_sum(grad_hidden.astype(F32))
        for part in range(4):
            vsum_ref[4 + part : 5 + part, :] += bias_sum[:, D * part : D * (part + 1)]
    rows = up_ref.shape[0] // 4
    proj_rows = D // 4
    grad = dot_tn(branch_low[...], att_low[...]).astype(BF)
    for owner in range(4):
        grads_ref[owner, 0:proj_rows, :] = grad[proj_rows * owner : proj_rows * (owner + 1), :]
    for owner in range(4):
        at = slice(rows * owner, rows * (owner + 1))
        start = proj_rows
        grads_ref[owner, start : start + rows, :] = dot_tn(ghid[:, at], normed[...]).astype(BF)
        start = proj_rows + rows
        grads_ref[owner, start : start + rows, :] = dot_tn(act[:, at], top[...]).astype(BF)


class RowSums:
    def __init__(self, clips, g_ref, at, pair_in, cross_out, cross_in, shares, shares_in, sums,
                 frame_sems, part_sems, sum_sems):
        self.clips = clips
        self.g = g_ref
        self.at = at
        self.pair_in = pair_in
        self.cross_out = cross_out
        self.cross_in = cross_in
        self.shares = shares
        self.shares_in = shares_in
        self.sums = sums
        self.part_sems = part_sems
        self.sum_sems = sum_sems
        f, near, across, far = frame_peers()
        self.f, self.across = f, across
        self.c = lax.axis_index("clip")
        sem = frame_sems
        part = lambda owner: g_ref.at[owner, pl.ds(at.start, at.stop - at.start), :]
        self.first = send(part(far), pair_in.at[0], sem.at[0, 0], sem.at[1, 0], near)
        self.second = send(part(near), pair_in.at[1], sem.at[0, 1], sem.at[1, 1], near)
        self.cross = send(cross_out, cross_in, sem.at[0, 2], sem.at[1, 2], across)

    def peer(self, step):
        return lax.rem(self.c + step, self.clips)

    def part_copy(self, step):
        return pltpu.make_async_remote_copy(
            src_ref=self.shares.at[self.peer(step)],
            dst_ref=self.shares_in.at[step],
            send_sem=self.part_sems.at[0, step],
            recv_sem=self.part_sems.at[1, step],
            device_id={"clip": self.peer(step)},
            device_id_type=MESH,
        )

    def sum_copy(self, step):
        return pltpu.make_async_remote_copy(
            src_ref=self.sums.at[self.c],
            dst_ref=self.sums.at[self.c],
            send_sem=self.sum_sems.at[0, step],
            recv_sem=self.sum_sems.at[1, step],
            device_id={"clip": self.peer(step)},
            device_id_type=MESH,
        )

    def each(self, act):
        def body(step, carry):
            act(step)
            return carry

        lax.fori_loop(1, self.clips, body, 0)

    def pair_step(self):
        self.first.start()
        self.second.start()

    def cross_step(self):
        self.first.wait()
        self.cross_out[...] = (
            self.g[self.across, self.at, :].astype(F32) + self.pair_in[0].astype(F32)
        ).astype(BF)
        self.cross.start()

    def share_step(self):
        self.second.wait()
        self.cross.wait()
        mine = (
            self.g[self.f, self.at, :].astype(F32)
            + self.pair_in[1].astype(F32)
            + self.cross_in[...].astype(F32)
        ).astype(BF)
        rows, chunk = mine.shape[0], self.shares.shape[1]
        spare = self.clips * chunk - rows
        if spare:
            mine = jnp.concatenate([mine, jnp.zeros((spare, D), BF)], axis=0)
        self.shares[...] = mine.reshape(self.clips, chunk, D)
        self.each(lambda step: self.part_copy(step).start())

    def sum_step(self):
        self.each(lambda step: self.part_copy(step).wait())

        def add_part(step, total):
            return total + self.shares_in[step].astype(F32)

        total = lax.fori_loop(1, self.clips, add_part, self.shares[self.c].astype(F32))
        self.sums[self.c] = total.astype(BF)
        self.each(lambda step: self.sum_copy(step).start())

    def finish(self):
        self.each(lambda step: self.sum_copy(step).wait())


def row_sums_scratch(rows, clips):
    chunk = share_rows(rows, clips)
    return [
        pltpu.VMEM((2, rows, D), BF),
        pltpu.VMEM((rows, D), BF),
        pltpu.VMEM((rows, D), BF),
        pltpu.VMEM((clips, chunk, D), BF),
        pltpu.VMEM((clips, chunk, D), BF),
        pltpu.VMEM((clips, chunk, D), BF),
        pltpu.SemaphoreType.DMA((2, 3)),
        pltpu.SemaphoreType.DMA((2, clips)),
        pltpu.SemaphoreType.DMA((2, clips)),
    ]


EARLY_PARTS = (slice(0, 400), slice(400, 720))


def row_pieces(start, size, block):
    pieces, skip = [], 0
    while skip < size:
        owner, row = divmod(start + skip, block)
        step = min(size - skip, block - row)
        pieces.append((owner, row, skip, step))
        skip += step
    return pieces


def back_phase(
    one,
    two,
    arrived,
    q_ref,
    dout_ref,
    kept_ref,
    cross_ref,
    home_ref,
    nhome_ref,
    ncross_ref,
    wq_ref,
    wkv_ref,
    side_ref,
    cells_ref,
    gnorm_ref,
    own_ref,
    out_ref,
    bsum_ref,
    grads_ref,
    grads_in,
    pair_out,
    pair_in,
    cross_out,
    cross_in,
    pair_sems,
    cross_sems,
    grad_sems,
    extra,
    qd_t,
    tail,
    low_one,
    low_two,
    low_three,
    dq_sum,
    turned_pairs,
    pair_grad,
):
    f, near, across, far = frame_peers()
    rows = q_ref.shape[1]
    dnormed = gnorm_ref
    dq_low = q_ref
    tail[...] = tail_lanes(inside_of(side_ref, cells_ref[...]), 4)
    arrived(0, 3)
    lower = lax.broadcasted_iota(jnp.int32, (PAIR, 1), 0) < HEAD_DIM
    scale_of = jnp.where(lower, SCORE_SCALE, 1.0)
    chunks = ((0, 512, low_one), (512, 512, low_two), (1024, 576, low_three))

    def minus_parts(column, lane):
        high = column.astype(BF).astype(F32)
        mid = (column - high).astype(BF).astype(F32)
        rest = column - high - mid
        return jnp.where(
            lane == HEAD_DIM + 1,
            -high,
            jnp.where(lane == HEAD_DIM + 2, -mid, jnp.where(lane == HEAD_DIM + 3, -rest, 0.0)),
        )

    def prepare(h):
        lane = lanes_of(rows)
        kept = kept_ref[h]
        queries, douts = q_ref[h].astype(F32), dout_ref[h].astype(F32)
        log_sum = kept[:, 0:1]
        row_dot = jnp.sum(douts * kept, axis=-1, keepdims=True)
        of_queries = jnp.where(lane == HEAD_DIM, 1.0, minus_parts(log_sum, lane))
        extra[h, 0:rows, :] = of_queries.astype(BF)
        extra[h, rows : 2 * rows, :] = minus_parts(row_dot, lane).astype(BF)
        qd_t[h] = jnp.concatenate([queries, douts], axis=0).T.astype(BF)
        bsum_ref[1, h] = column_sum(douts)

    def head_pass(h, source, add):
        pairs = source[h]
        both = jnp.concatenate([q_ref[h], dout_ref[h]], axis=0)
        both = jnp.concatenate([both, extra[h]], axis=1)
        products = [
            dot_nt(
                both,
                jnp.concatenate(
                    [pairs[start : start + size, :], tail[start : start + size, :]], axis=1
                ),
            )
            for start, size, low in chunks
        ]
        total = dq_sum[h] if add else None
        at = pl.ds(pl.multiple_of(h * PAIR, PAIR), PAIR)
        for (start, size, low), product in zip(chunks, products):
            probs = jnp.exp2(product[0:rows, :] * EXP_SCALE)
            low[0:rows, :] = (probs * product[rows : 2 * rows, :]).astype(BF)
            low[rows : 2 * rows, :] = probs.astype(BF)
            part = dot_nn(low[0:rows, :], pairs[start : start + size, :])
            total = part if total is None else total + part
            turned = dot_nn(qd_t[h], low[...]) * scale_of
            turned_pairs[at, start : start + size] = turned.astype(BF)
        if add:
            total = jnp.where(lanes_of(rows) < HEAD_DIM, total * SCORE_SCALE, 0.0)
            dq_low[h] = total.astype(BF)
            bsum_ref[0, h] = column_sum(total)
        else:
            dq_sum[h] = total

    def of_normed(normed, add):
        grad = dot_nn(turned_pairs[...], normed[...])
        pair_grad[...] = pair_grad[...] + grad if add else grad
        total = dot_nn(wkv_ref[...].astype(F32).T.astype(BF), turned_pairs[...]).T
        dnormed[...] = total[0:rows, :]
        pair_out[...] = total[rows : 2 * rows, :].astype(BF)

    def pair_copy(phase):
        return send(
            pair_out, pair_in.at[phase], pair_sems.at[0, phase], pair_sems.at[1, phase], near
        )

    to_across = send(cross_out, cross_in, cross_sems.at[0], cross_sems.at[1], across)

    def cross_pass(h, carry):
        prepare(h)
        head_pass(h, cross_ref, False)

        @pl.when(h == 0)
        def _():
            one.cross_step()
            two.cross_step()

        @pl.when(h == 3)
        def _():
            one.share_step()

        return carry

    def home_pass(h, carry):
        head_pass(h, home_ref, True)

        @pl.when(h == 0)
        def _():
            pair_copy(0).wait()
            cross_out[...] = (dnormed[...] + pair_in[0].astype(F32)).astype(BF)
            to_across.start()
            two.share_step()

        @pl.when(h == 1)
        def _():
            one.sum_step()

        @pl.when(h == 3)
        def _():
            two.sum_step()

        return carry

    lax.fori_loop(0, HEADS, cross_pass, 0)
    arrived(3, 8)
    of_normed(ncross_ref, False)
    pair_copy(0).start()
    lax.fori_loop(0, HEADS, home_pass, 0)
    of_normed(nhome_ref, True)
    pair_copy(1).start()

    block = grads_ref.shape[1]

    def place(start, values):
        for owner, row, skip, size in row_pieces(start, values.shape[0], block):
            grads_ref[owner, row : row + size, :] = values[skip : skip + size, :]

    dq = jnp.concatenate([dq_low[h] for h in range(HEADS)], axis=1)
    of_queries = dot_tn(dq, nhome_ref[0:rows, :]).astype(BF)
    for h in range(HEADS):
        of_pairs = pair_grad[PAIR * h : PAIR * (h + 1), :].astype(BF)
        place(HEAD_DIM * h, of_queries[PAIR * h : PAIR * h + HEAD_DIM, :])
        place(D + HEAD_DIM * h, of_pairs[0:HEAD_DIM, :])
        place(2 * D + HEAD_DIM * h, of_pairs[HEAD_DIM:PAIR, :])
    to_pair = [
        send(grads_ref.at[peer], grads_in.at[k], grad_sems.at[0, k], grad_sems.at[1, k], near)
        for k, peer in enumerate((far, near))
    ]
    for copy in to_pair:
        copy.start()
    total = dnormed[...] + dot_nn(dq, wq_ref[...])
    to_across.wait()
    pair_copy(1).wait()
    gnorm_ref[...] = total + pair_in[1].astype(F32) + cross_in[...].astype(F32)
    for copy in to_pair:
        copy.wait()
    out_ref[...] = (grads_ref[across].astype(F32) + grads_in[0].astype(F32)).astype(BF)
    own_ref[...] = grads_ref[f].astype(F32) + grads_in[1].astype(F32)


def newton_schulz(whole):
    wide = whole.astype(F32)
    norm = jnp.sqrt(jnp.sum(wide * wide)) + 1e-07
    eye = (
        lax.broadcasted_iota(jnp.int32, (D, D), 0) == lax.broadcasted_iota(jnp.int32, (D, D), 1)
    ).astype(F32)
    turned = dot_nt(eye.astype(BF), whole) / norm

    def iterate(step, current):
        held = current.astype(BF)
        gram = dot_nt(held, held)
        gram_low = gram.astype(BF)
        poly = POLY_TWO * gram + POLY_THREE * dot_nn(gram_low, gram_low)
        return POLY_ONE * current + dot_nn(poly.astype(BF), held)

    return lax.fori_loop(0, NS_STEPS, iterate, turned)


OWNER_OF = (3, 1, 0, 2)
QKV_AT = OWNER_OF[0]


def tail_phase(
    clips,
    one,
    two,
    arrived,
    copy_out,
    gnorm_ref,
    own_ref,
    across_ref,
    bsum_ref,
    tok_ref,
    gsec_ref,
    x_ref,
    side_ref,
    cells_ref,
    taps_ref,
    vec_ref,
    mid_sums_ref,
    one_ref,
    two_ref,
    qkv_m_ref,
    proj_m_ref,
    up_m_ref,
    down_m_ref,
    late_ref,
    scaled_ref,
    vsum_ref,
    cross_in,
    shares,
    shares_in,
    new_rows,
    new_low,
    first_low,
    rim,
    v_mine,
    v_frames,
    v_total,
    v_clips,
    gathered,
    old_rows,
    outer,
    center,
    edged,
    low,
    grad_sems,
    part_sems,
    row_sems,
    spread_sems,
    rim_sems,
    vf_sems,
    vc_sems,
    there_sems,
    back_sems,
):
    first, ingrad_ref = gnorm_ref, gsec_ref
    f, near, across, far = frame_peers()
    c = lax.axis_index("clip")
    block = own_ref.shape[0]
    owners, chunk = shares.shape[0], shares.shape[1]

    def each(count, act):
        def body(step, carry):
            act(step)
            return carry

        lax.fori_loop(0, count, body, 0)

    def other_clips(act):
        each(clips - 1, lambda step: act(lax.rem(c + 1 + step, clips)))

    down, up = halo_copies(first_low.at[0], first_low.at[1], rim, rim_sems)

    to_across = send(across_ref, cross_in, grad_sems.at[0], grad_sems.at[1], across)
    to_across.start()

    upstream = gnorm_ref[...]
    unit, scale = norm_parts(tok_ref[...])
    grad_first = gsec_ref[...] + norm_back(upstream, unit, scale, vec_ref[0:1, :])
    first[...] = grad_first
    first_low[...] = grad_first.astype(BF).reshape(first_low.shape)
    start_halos(down, up, rim)

    one.finish()
    two.finish()
    one_ref[...] = one.sums[...].reshape(one_ref.shape)
    two_ref[...] = two.sums[...].reshape(two_ref.shape)
    arrived(0, 5)
    old_rows[0:block, :] = qkv_m_ref[...].T
    if owners * chunk > block:
        old_rows[block : owners * chunk, :] = jnp.zeros((owners * chunk - block, D), F32)

    v_mine[0:1, :] = column_sum(upstream * unit)
    v_mine[1:2, :] = column_sum(upstream)
    v_mine[2:4, :] = mid_sums_ref[0:2, :]
    v_mine[4:5, :] = column_sum(grad_first)
    v_mine[5:6, :] = jnp.concatenate(
        [bsum_ref[0, h, :, 0:HEAD_DIM] for h in range(HEADS)], axis=1
    )
    v_mine[6:7, :] = jnp.concatenate(
        [bsum_ref[1, h, :, HEAD_DIM:PAIR] for h in range(HEADS)], axis=1
    )
    v_mine[7:9, :] = mid_sums_ref[2:4, :]
    v_mine[9:13, :] = mid_sums_ref[4:8, :]

    cells = cells_ref[...]
    inside = inside_of(side_ref, cells)
    for t in range(2):
        build_slabs(center, edged, t + 1, first[400 * t : 400 * t + 400, :], cells)

    def part_copy(owner):
        return pltpu.make_async_remote_copy(
            src_ref=shares.at[owner],
            dst_ref=shares_in.at[c],
            send_sem=part_sems.at[0, owner],
            recv_sem=part_sems.at[1, c],
            device_id={"clip": owner},
            device_id_type=MESH,
        )

    def other_owners(act):
        def step(owner):
            @pl.when(owner != c)
            def _():
                act(owner)

        each(owners, step)

    to_across.wait()
    mine = (own_ref[...] + cross_in[...].astype(F32)).astype(BF)
    if owners * chunk > block:
        mine = jnp.concatenate([mine, jnp.zeros((owners * chunk - block, D), BF)], axis=0)
    shares[...] = mine.reshape(owners, chunk, D)
    other_owners(lambda owner: part_copy(owner).start())

    moments = (None, proj_m_ref, up_m_ref, down_m_ref)

    def to_owner(which):
        at = pl.ds(0, moments[which].shape[0])
        return send(
            low.at[which, at, :],
            gathered.at[f, at, :],
            there_sems.at[0, which],
            there_sems.at[1, f],
            OWNER_OF[which],
        )

    for which in (3, 2, 1):
        rows = moments[which].shape[0]
        summed = one_ref[80:400, :] if which == 2 else (two_ref if which == 3 else one_ref)[0:rows, :]
        low[which, 0:rows, :] = (0.95 * moments[which][...] + summed.astype(F32)).astype(BF)

        @pl.when(f != OWNER_OF[which])
        def _(which=which):
            to_owner(which).start()

    wait_halos(down, up)
    for side, slot in ((0, 0), (1, 3)):
        build_slabs(center, edged, slot, rim[side].astype(F32), cells)

    def row_copy(clip):
        return pltpu.make_async_remote_copy(
            src_ref=new_rows.at[c],
            dst_ref=new_rows.at[c],
            send_sem=row_sems.at[0, clip],
            recv_sem=row_sems.at[1, c],
            device_id={"clip": clip},
            device_id_type=MESH,
        )

    def spread_copy(clip):
        return pltpu.make_async_remote_copy(
            src_ref=new_low,
            dst_ref=gathered.at[f, pl.ds(pl.multiple_of(c * chunk, 16), chunk), :],
            send_sem=spread_sems.at[4, clip],
            recv_sem=spread_sems.at[f, c],
            device_id={"clip": clip, "frame": QKV_AT},
            device_id_type=MESH,
        )

    def share_sum():
        @pl.when(c < owners)
        def _():
            shares_in[c] = shares[c]

            def arrive(clip):
                pltpu.make_async_remote_copy(
                    src_ref=shares.at[0],
                    dst_ref=shares_in.at[clip],
                    send_sem=part_sems.at[0, 0],
                    recv_sem=part_sems.at[1, clip],
                    device_id={"clip": clip},
                    device_id_type=MESH,
                ).wait_recv()

            other_clips(arrive)

            def add_part(clip, total):
                return total + shares_in[clip].astype(F32)

            total = lax.fori_loop(0, clips, add_part, jnp.zeros((chunk, D), F32))
            at = pl.ds(pl.multiple_of(c * chunk, 16), chunk)
            fresh = 0.95 * old_rows[at, :] + total
            new_rows[c] = fresh
            new_low[...] = fresh.astype(BF)
            other_clips(lambda clip: spread_copy(clip).start())

            @pl.when(f != QKV_AT)
            def _():
                spread_copy(c).start()

            @pl.when(f == QKV_AT)
            def _():
                gathered[QKV_AT, at, :] = new_low[...]

            other_clips(lambda clip: row_copy(clip).start())

    for t in range(2):
        flatten_frame(lambda row, t=t: x_ref[0, t, row], outer, 0)
        outer[...] = jnp.where(inside, outer[...], 0.0)
        for a in range(3):

            def plane(step, totals, t=t, a=a):
                start = pl.multiple_of(step * 16, 16)
                at = pl.ds(pl.multiple_of(start + 400 * t, 16), 16)
                masked = outer[pl.ds(start, 16), :]
                total = jnp.zeros((16, D), F32)
                sums_out = []
                for b in range(3):
                    for e in range(3):
                        offset = 9 * a + 3 * b + e
                        piece = slab(center, edged, t + 2 - a, 2 - b, 2 - e, start, 16)
                        total = total + taps_ref[offset : offset + 1, :] * piece
                        product = masked * piece
                        sums_out.append(totals[3 * b + e] + (product[0:8, :] + product[8:16, :]))
                if a == 0:
                    ingrad_ref[at, :] = total
                else:
                    ingrad_ref[at, :] += total
                return tuple(sums_out)

            totals = lax.fori_loop(0, 25, plane, tuple(jnp.zeros((8, D), F32) for _ in range(9)))
            for which, total in enumerate(totals):
                at = slice(13 + 9 * a + which, 14 + 9 * a + which)
                if t == 0:
                    v_mine[at, :] = column_sum(total)
                else:
                    v_mine[at, :] += column_sum(total)
        at = slice(400 * t, 400 * t + 400)
        ingrad_ref[at, :] = first[at, :] + jnp.where(inside, ingrad_ref[at, :], 0.0)
        if t == 0:
            share_sum()

    copy_out()

    v_copies = []
    for which, peer in enumerate((near, across, far)):
        copy = send(v_mine, v_frames.at[f], vf_sems.at[0, which], vf_sems.at[1, which], peer)
        copy.start()
        v_copies.append(copy)
    v_frames[f] = v_mine[...]

    @pl.when(f == QKV_AT)
    def _():
        def rows_arrive(frame, clip):
            pltpu.make_async_remote_copy(
                src_ref=new_low,
                dst_ref=gathered.at[frame, pl.ds(pl.multiple_of(clip * chunk, 16), chunk), :],
                send_sem=spread_sems.at[4, clip],
                recv_sem=spread_sems.at[frame, clip],
                device_id={"clip": clip, "frame": frame},
                device_id_type=MESH,
            ).wait_recv()

        other_owners(lambda clip: rows_arrive(QKV_AT, clip))
        for step in (1, 2, 3):
            frame = (QKV_AT + step) % 4
            each(owners, lambda clip, frame=frame: rows_arrive(frame, clip))

    for which in (1, 2, 3):

        @pl.when(f != OWNER_OF[which])
        def _(which=which):
            to_owner(which).wait_send()

        @pl.when(f == OWNER_OF[which])
        def _(which=which):
            at = pl.ds(0, moments[which].shape[0])
            gathered[OWNER_OF[which], at, :] = low[which, at, :]
            for other in range(4):
                if other != OWNER_OF[which]:
                    send(
                        low.at[0, at, :],
                        gathered.at[other, at, :],
                        there_sems.at[0, 0],
                        there_sems.at[1, other],
                        other,
                    ).wait_recv()

    turned = newton_schulz(gathered[...].reshape(4 * SHARE, D))
    low[:, 0:SHARE, :] = turned.T.astype(BF).reshape(4, SHARE, D)
    row_counts = (block, *(ref.shape[0] for ref in moments[1:]))

    def back_copy(which, step):
        at = pl.ds(0, row_counts[which])
        to = (OWNER_OF[which] + step) % 4
        return send(
            low.at[to, at, :],
            scaled_ref.at[which, at, :],
            back_sems.at[0, step],
            back_sems.at[1, which],
            to,
        )

    for which in range(4):

        @pl.when(f == OWNER_OF[which])
        def _(which=which):
            for step in (2, 1, 3):
                back_copy(which, step).start()
            at = pl.ds(0, row_counts[which])
            scaled_ref[which, at, :] = low[OWNER_OF[which], at, :]

    for copy in v_copies:
        copy.wait()
    v_total[...] = v_frames[0] + v_frames[1] + v_frames[2] + v_frames[3]

    def v_copy(clip):
        return pltpu.make_async_remote_copy(
            src_ref=v_total,
            dst_ref=v_clips.at[c],
            send_sem=vc_sems.at[0, clip],
            recv_sem=vc_sems.at[1, c],
            device_id={"clip": clip},
            device_id_type=MESH,
        )

    other_clips(lambda clip: v_copy(clip).start())
    v_clips[c] = v_total[...]

    other_owners(lambda owner: part_copy(owner).wait_send())

    @pl.when(c < owners)
    def _():
        other_clips(lambda clip: spread_copy(clip).wait_send())

        @pl.when(f != QKV_AT)
        def _():
            spread_copy(c).wait_send()

        other_clips(lambda clip: row_copy(clip).wait_send())

    def new_rows_arrive(clip):
        pltpu.make_async_remote_copy(
            src_ref=new_rows.at[0],
            dst_ref=new_rows.at[clip],
            send_sem=row_sems.at[0, 0],
            recv_sem=row_sems.at[1, clip],
            device_id={"clip": clip},
            device_id_type=MESH,
        ).wait_recv()

    other_owners(new_rows_arrive)
    late_ref[...] = new_rows[...].reshape(late_ref.shape)

    def v_arrives(clip):
        v_copy(clip).wait_send()
        pltpu.make_async_remote_copy(
            src_ref=v_total,
            dst_ref=v_clips.at[clip],
            send_sem=vc_sems.at[0, clip],
            recv_sem=vc_sems.at[1, clip],
            device_id={"clip": clip},
            device_id_type=MESH,
        ).wait_recv()

    other_clips(v_arrives)

    def add_v(step, total):
        return total + v_clips[step]

    vsum_ref[...] = lax.fori_loop(0, clips, add_v, jnp.zeros(vsum_ref.shape, F32))
    for which in range(4):

        @pl.when(f == OWNER_OF[which])
        def _(which=which):
            for step in (2, 1, 3):
                back_copy(which, step).wait_send()

        @pl.when(f != OWNER_OF[which])
        def _(which=which):
            back_copy(which, 1).wait_recv()


def rest_kernel(
    clips,
    att_in,
    tok_in,
    og_in,
    others_in,
    side_ref,
    cells_ref,
    vec_ref,
    ubias_ref,
    taps_ref,
    *refs,
):
    refs = list(refs)

    def take(count):
        taken, refs[:count] = refs[:count], []
        return taken

    back_sources = take(8)
    tail_sources = take(5)
    block_out, ingrad_out, one_ref, two_ref, late_ref, scaled_ref, vsum_ref = take(7)
    tok, out, gsec, dout, early, mid_sums = take(6)
    back_inputs = take(8)
    gnorm, own, across_rows, bsum = take(4)
    back_buffers = take(6)
    back_sems = take(3)
    tail_landing = take(12)
    tail_sems = take(9)
    (copy_sems,) = take(1)
    half = len(refs) // 2
    f, near, across, far = frame_peers()
    c = lax.axis_index("clip")
    gathered = tail_landing[-1]
    block, proj_rows = own.shape[0], D // 4
    chunk = share_rows(block, clips)
    owned = -(-block // chunk) * chunk

    @pl.when(f == QKV_AT)
    def _():
        gathered[:, owned:SHARE, :] = jnp.zeros((4, SHARE - owned, D), BF)

    @pl.when(f == OWNER_OF[1])
    def _():
        gathered[:, proj_rows:SHARE, :] = jnp.zeros((4, SHARE - proj_rows, D), BF)

    greet_all(clips)
    barrier = pltpu.get_barrier_semaphore()

    def greet(frame):
        def body(step, carry):
            pl.semaphore_signal(
                barrier,
                inc=1,
                device_id={"clip": lax.rem(c + step, clips), "frame": frame},
                device_id_type=MESH,
            )
            return carry

        lax.fori_loop(1, clips, body, 0)

    @pl.when(f == QKV_AT)
    def _():
        for step in (1, 2, 3):
            greet((QKV_AT + step) % 4)

    @pl.when(f != QKV_AT)
    def _():
        greet(QKV_AT)

    def copies(sources, targets, first):
        return [
            pltpu.make_async_copy(src, dst, copy_sems.at[first + k])
            for k, (src, dst) in enumerate(zip(sources, targets))
        ]

    def arrival(waiting):
        def arrived(start, stop):
            for copy in waiting[start:stop]:
                copy.wait()

        return arrived

    for_back = copies(back_sources, back_inputs, 4)

    def middle(att, og, others, *scratch):
        for_mid = copies((others_in, att_in, tok_in, og_in), (others, att, tok, og), 0)
        for copy in for_mid:
            copy.start()
        for copy in for_mid:
            copy.wait()
        for copy in for_back:
            copy.start()
        mid_phase(
            att, tok, og, side_ref, cells_ref, vec_ref, ubias_ref, others, out, gsec, dout, early,
            mid_sums, *scratch,
        )

    rows = tok.shape[0]
    vmem = pltpu.VMEM
    pl.run_scoped(
        middle,
        vmem(att_in.shape, BF),
        vmem(og_in.shape, BF),
        vmem(others_in.shape, BF),
        vmem((400, D), F32),
        vmem((D, WIDE), BF),
        vmem((rows, FF), BF),
        vmem((rows, FF), BF),
        vmem((rows, D), BF),
        vmem((rows, D), BF),
        vmem((rows, D), BF),
        vmem((rows, D), BF),
        vmem((D, D), BF),
        vmem((FF, D), BF),
        vmem((FF, D), BF),
    )
    out_copy = pltpu.make_async_copy(out, block_out, copy_sems.at[0])
    out_copy.start()

    @pl.when(f == QKV_AT)
    def _():
        await_greetings(3 + 4 * (clips - 1))

    @pl.when(f != QKV_AT)
    def _():
        await_greetings(3 + 2 * (clips - 1))

    one = RowSums(clips, early, EARLY_PARTS[0], *refs[:half])
    two = RowSums(clips, early, EARLY_PARTS[1], *refs[half:])
    one.pair_step()
    two.pair_step()

    def backward(*scratch):
        back_phase(
            one, two, arrival(for_back), back_inputs[0], dout, *back_inputs[1:], side_ref,
            cells_ref, gnorm, own, across_rows, bsum, *back_buffers, *back_sems, *scratch,
        )

    pl.run_scoped(
        backward,
        vmem((HEADS, 2 * rows, PAIR), BF),
        vmem((HEADS, PAIR, 2 * rows), BF),
        vmem((2 * rows, PAIR), BF),
        vmem((2 * rows, 512), BF),
        vmem((2 * rows, 512), BF),
        vmem((2 * rows, 576), BF),
        vmem((HEADS, rows, PAIR), F32),
        vmem((WIDE, 2 * rows), BF),
        vmem((WIDE, D), F32),
    )

    def finish(x, qkv_m, proj_m, up_m, down_m, *scratch):
        for_tail = copies(tail_sources, (x, qkv_m, proj_m, up_m, down_m), 12)
        for copy in for_tail:
            copy.start()
        leave = pltpu.make_async_copy(gsec, ingrad_out, copy_sems.at[1])
        tail_phase(
            clips, one, two, arrival(for_tail), leave.start, gnorm, own, across_rows, bsum, tok,
            gsec, x, side_ref, cells_ref, taps_ref, vec_ref, mid_sums, one_ref, two_ref, qkv_m,
            proj_m, up_m, down_m, late_ref, scaled_ref, vsum_ref, *tail_landing, *scratch, early,
            *tail_sems,
        )
        leave.wait()

    pl.run_scoped(
        finish,
        *(vmem(ref.shape, ref.dtype) for ref in tail_sources),
        vmem((owned, D), F32),
        vmem((400, D), F32),
        vmem((3, 4, 400, D), F32),
        vmem((3, 4, 440, D), F32),
    )
    out_copy.wait()


def rest(mid_inputs, small, back_inputs, tail_inputs, clips, collective_id):
    rows, block = 800, 3 * D // 4
    chunk = share_rows(block, clips)
    owners = -(-block // chunk)
    vector_shape = (40, D)
    vmem = pltpu.VMEM
    dma = pltpu.SemaphoreType.DMA
    parts = [part.stop - part.start for part in EARLY_PARTS]
    hbm = pl.BlockSpec(memory_space=pl.ANY)
    return pl.pallas_call(
        functools.partial(rest_kernel, clips),
        in_specs=[hbm] * 4
        + [pl.BlockSpec(memory_space=pltpu.SMEM)]
        + [VMEM_SPEC] * 4
        + [hbm] * (len(back_inputs) + len(tail_inputs)),
        out_specs=[hbm] * 2 + [VMEM_SPEC] * 5,
        out_shape=[
            jax.ShapeDtypeStruct(mid_inputs[2].shape, BF),
            jax.ShapeDtypeStruct((rows, D), F32),
        ]
        + [
            jax.ShapeDtypeStruct((clips * share_rows(part, clips), D), BF) for part in parts
        ]
        + [
            jax.ShapeDtypeStruct((owners * chunk, D), F32),
            jax.ShapeDtypeStruct((4, SHARE, D), BF),
            jax.ShapeDtypeStruct(vector_shape, F32),
        ],
        scratch_shapes=[
            vmem((rows, D), F32),
            vmem(mid_inputs[2].shape, BF),
            vmem((rows, D), F32),
            vmem((HEADS, rows, PAIR), BF),
            vmem((4, (D + 2 * FF) // 4, D), BF),
            vmem((8, D), F32),
        ]
        + [vmem(ref.shape, ref.dtype) for ref in back_inputs]
        + [
            vmem((rows, D), F32),
            vmem((block, D), F32),
            vmem((block, D), BF),
            vmem((2, HEADS, 1, PAIR), F32),
            vmem((4, block, D), BF),
            vmem((2, block, D), BF),
            vmem((rows, D), BF),
            vmem((2, rows, D), BF),
            vmem((rows, D), BF),
            vmem((rows, D), BF),
            dma((2, 2)),
            dma((2,)),
            dma((2, 2)),
            vmem((block, D), BF),
            vmem((owners, chunk, D), BF),
            vmem((clips, chunk, D), BF),
            vmem((owners, chunk, D), F32),
            vmem((chunk, D), BF),
            vmem((2, 400, D), BF),
            vmem((2, 400, D), BF),
            vmem(vector_shape, F32),
            vmem((4,) + vector_shape, F32),
            vmem(vector_shape, F32),
            vmem((clips,) + vector_shape, F32),
            vmem((4, SHARE, D), BF),
            dma((2,)),
            dma((2, clips)),
            dma((2, clips)),
            dma((5, clips)),
            dma((2, 2)),
            dma((2, 3)),
            dma((2, clips)),
            dma((2, 4)),
            dma((2, 4)),
            dma((17,)),
        ]
        + row_sums_scratch(parts[0], clips)
        + row_sums_scratch(parts[1], clips),
        compiler_params=pltpu.CompilerParams(
            collective_id=collective_id, has_side_effects=True, vmem_limit_bytes=63 * 2**20
        ),
        cost_estimate=pl.CostEstimate(
            flops=2**36, bytes_accessed=32 * 2**20, transcendentals=2**25
        ),
    )(*mid_inputs, *small, *back_inputs, *tail_inputs)


def adamw(param, mean_old, square_old, gradient, rate_value, decay):
    mean_new = 0.9 * mean_old + 0.1 * gradient
    square_new = 0.999 * square_old + 0.001 * gradient * gradient
    mean_hat = mean_new / (1.0 - 0.9**STEP)
    square_hat = square_new / (1.0 - 0.999**STEP)
    return (
        mean_new,
        square_new,
        param - rate_value * (mean_hat / (jnp.sqrt(square_hat) + 1e-08) + decay * param),
    )


RATES = (0.2 * math.sqrt(3.0), 0.12 * math.sqrt(CLIP_TOK), 0.2 * math.sqrt(FF / D), 0.2)


def update_kernel(*refs):
    ingrad_ref, late_ref, one_ref, two_ref, scaled_ref, vsum_ref = refs[:6]
    weights, moments, vectors, taps = refs[6:10], refs[10:13], refs[13:16], refs[16:19]
    out_ref, new_moments, new_weights = refs[19], refs[20:24], refs[24:28]
    new_vectors, new_taps = refs[28:31], refs[31:34]
    for t in range(2):
        for row in range(20):
            at = 400 * t + 20 * row
            out_ref[0, t, row] = ingrad_ref[at : at + 20, :]
    rows = weights[0].shape[1]
    new_moments[0][...] = late_ref[0:rows, :].T
    new_weights[0][...] = 0.999 * weights[0][...] - RATES[0] * (
        scaled_ref[0, 0:rows, :].astype(F32).T
    )
    for which in (1, 2, 3):
        rows = weights[which].shape[0]
        summed = one_ref[80:400, :] if which == 2 else (two_ref if which == 3 else one_ref)[0:rows, :]
        new_moments[which][...] = 0.95 * moments[which - 1][...] + summed.astype(F32)
        new_weights[which][...] = 0.999 * weights[which][...] - RATES[which] * scaled_ref[
            which, 0:rows, :
        ].astype(F32)
    for (param, mean, square), outs, at, rate, decay in (
        (vectors, new_vectors, slice(0, 9), 0.2, 0.0),
        (taps, new_taps, slice(13, 40), 0.05, 0.01),
    ):
        for ref, value in zip(
            outs, adamw(param[...], mean[...], square[...], vsum_ref[at, :], rate, decay)
        ):
            ref[...] = value


def update(ingrad, late, one, two, scaled, vector_sums, weights, moments, vectors, taps, grid_shape):
    operands = [ingrad, late, one, two, scaled, vector_sums, *weights, *moments[1:], *vectors, *taps]
    outs = [jax.ShapeDtypeStruct(grid_shape, F32)]
    outs += [jax.ShapeDtypeStruct(x.shape, F32) for x in (*moments, *weights, *vectors, *taps)]
    return pl.pallas_call(
        update_kernel,
        in_specs=[VMEM_SPEC] * len(operands),
        out_specs=[VMEM_SPEC] * len(outs),
        out_shape=outs,
        compiler_params=pltpu.CompilerParams(vmem_limit_bytes=62 * 2**20),
        cost_estimate=pl.CostEstimate(
            flops=2**22, bytes_accessed=12 * 2**20, transcendentals=2**14
        ),
    )(*operands)


def per_device(
    clips_in,
    out_grad,
    clip_side,
    qkv_weight,
    proj_weight,
    up_weight,
    down_weight,
    qkv_moment,
    proj_moment,
    up_moment,
    down_moment,
    vectors,
    vector_mean,
    vector_square,
    up_bias,
    up_bias_mean,
    up_bias_square,
    conv_kernel,
    kernel_mean,
    kernel_square,
):
    clips = lax.axis_size("clip")
    weights = (qkv_weight, proj_weight, up_weight, down_weight)
    moments = (qkv_moment, proj_moment, up_moment, down_moment)
    (
        tokens,
        normed_home,
        normed_cross,
        heads_q,
        home,
        cross,
        kept,
        heads_out,
        query_weight,
        pair_weight,
        other_weights,
    ) = front(clips_in, clip_side, qkv_weight.T, *weights[1:], vectors, conv_kernel, clips, 0)
    block_out, ingrad, sums_one, sums_two, late_moment, scaled, vector_sums = rest(
        (heads_out, tokens, out_grad, other_weights),
        (clip_side, jnp.asarray(CELL_AT), vectors, up_bias.reshape(1, FF), conv_kernel),
        (
            heads_q,
            kept,
            cross,
            home,
            normed_home,
            normed_cross,
            query_weight,
            pair_weight,
        ),
        (clips_in, qkv_moment.T, *moments[1:]),
        clips,
        1,
    )
    updated = update(
        ingrad,
        late_moment,
        sums_one,
        sums_two,
        scaled,
        vector_sums,
        (qkv_weight.T, *weights[1:]),
        (qkv_moment.T, *moments[1:]),
        (vectors, vector_mean, vector_square),
        (conv_kernel, kernel_mean, kernel_square),
        clips_in.shape,
    )
    input_grad = updated[0]
    new_moments = (updated[1].T, *updated[2:5])
    new_weights = (updated[5].T, *updated[6:9])
    bias_new = adamw(
        up_bias, up_bias_mean, up_bias_square, vector_sums[9:13].reshape(FF), 0.2, 0.0
    )
    outs = [block_out, input_grad]
    for moment, weight in zip(new_moments, new_weights):
        outs += [moment, weight]
    return (*outs, *updated[9:12], *bias_new, *updated[12:15])


def solution(mesh):
    big = P("clip", "frame", None, None, None)
    rows = P("frame", None)
    return jax.shard_map(
        per_device,
        mesh=mesh,
        in_specs=(big, big, P("clip")) + (rows,) * 8 + (P(),) * 9,
        out_specs=(big, big) + (rows,) * 8 + (P(),) * 9,
        check_vma=False,
    )
```

```python
import functools
import math

import jax
import jax.numpy as jnp
import numpy as np
from jax import lax
from jax.experimental import pallas as pl
from jax.experimental.pallas import tpu as pltpu
from jax.sharding import PartitionSpec as P

D = 320
HEADS = 5
HEAD_DIM = 64
PAIR = 2 * HEAD_DIM
WIDE = HEADS * PAIR
FF = 1280
NS_STEPS = 5
STEP = 10
CLIP_TOK = 3200
SHARE = 320

POLY_ONE = 3.4445
POLY_TWO = -4.775
POLY_THREE = 2.0315
LOG2E = math.log2(math.e)
SCORE_SCALE = HEAD_DIM**-0.5
MASKED = -1e30
MESH = pl.DeviceIdType.MESH
BF = jnp.bfloat16
F32 = jnp.float32
NT = (((1,), (1,)), ((), ()))
VMEM_SPEC = pl.BlockSpec(memory_space=pltpu.VMEM)


def dot_nt(left, right):
    return lax.dot_general(left, right, NT, preferred_element_type=F32)


def dot_nn(left, right):
    return jnp.dot(left, right, preferred_element_type=F32)


def lanes_of(rows):
    return lax.broadcasted_iota(jnp.int32, (rows, PAIR), 1)


CELL_AT = np.stack([np.arange(400) // 20, np.arange(400) % 20], axis=1).astype(np.float32)


def select_lanes(upper):
    row = lax.broadcasted_iota(jnp.int32, (D, WIDE), 0)
    col = lax.broadcasted_iota(jnp.int32, (D, WIDE), 1)
    source = lax.shift_left(lax.shift_right_logical(col, 7), 6) + (col & (HEAD_DIM - 1))
    half = col & HEAD_DIM
    return (source == row) & (half == (HEAD_DIM if upper else 0))


def flatten_frame(read_row, dst, base):
    for row in range(20):
        dst[base + 20 * row : base + 20 * row + 20, :] = read_row(row).astype(F32)


def build_slabs(center, edged, slot, flat, cells):
    blank = jnp.zeros((20, D), F32)
    edged[1, slot, 0:20, :] = blank
    edged[1, slot, 420:440, :] = blank
    edged[1, slot, 20:420, :] = flat
    center[1, slot] = flat
    col = cells[:, 1:2]
    for e, keep in ((0, col > 0.5), (2, col < 18.5)):
        moved = jnp.where(keep, edged[1, slot, 19 + e : 419 + e, :], 0.0)
        center[e, slot] = moved
        edged[e, slot, 0:20, :] = blank
        edged[e, slot, 420:440, :] = blank
        edged[e, slot, 20:420, :] = moved


def slab(center, edged, slot, b, e, start, size):
    if b == 1:
        return center[e, slot, pl.ds(start, size), :]
    return edged[e, slot, pl.ds(start + 20 * b, size), :]


def inside_of(side_ref, cells):
    side = side_ref[0].astype(F32) - 0.5
    return (cells[:, 0:1] < side) & (cells[:, 1:2] < side)


def norm_parts(rows):
    average = jnp.sum(rows, axis=-1, keepdims=True) * (1.0 / D)
    centered = rows - average
    variance = jnp.sum(centered * centered, axis=-1, keepdims=True) * (1.0 / D)
    scale = lax.rsqrt(variance + 1e-05)
    return centered * scale, scale


def frame_peers():
    f = lax.axis_index("frame")
    near = f + 1 - 2 * lax.rem(f, 2)
    across = lax.rem(f + 2, 4)
    return f, near, across, lax.rem(near + 2, 4)


def share_rows(rows, clips):
    return 16 * (-(-rows // (16 * clips)))


def greet_all(clips):
    barrier = pltpu.get_barrier_semaphore()
    for peer in frame_peers()[1:]:
        pl.semaphore_signal(barrier, inc=1, device_id={"frame": peer}, device_id_type=MESH)
    c = lax.axis_index("clip")

    def greet(step, carry):
        pl.semaphore_signal(
            barrier, inc=1, device_id={"clip": lax.rem(c + step, clips)}, device_id_type=MESH
        )
        return carry

    lax.fori_loop(1, clips, greet, 0)


def await_greetings(count):
    pl.semaphore_wait(pltpu.get_barrier_semaphore(), count)


def send(src, dst, send_sem, recv_sem, peer):
    return pltpu.make_async_remote_copy(
        src_ref=src,
        dst_ref=dst,
        send_sem=send_sem,
        recv_sem=recv_sem,
        device_id={"frame": peer},
        device_id_type=MESH,
    )


def halo_copies(first, last, halo, sems):
    f = lax.axis_index("frame")
    down = send(first, halo.at[1], sems.at[0, 0], sems.at[1, 0], jnp.maximum(f - 1, 0))
    up = send(last, halo.at[0], sems.at[0, 1], sems.at[1, 1], jnp.minimum(f + 1, 3))
    return down, up


def start_halos(down, up, halo):
    f = lax.axis_index("frame")

    @pl.when(f > 0)
    def _():
        down.start()

    @pl.when(f < 3)
    def _():
        up.start()

    @pl.when(f == 0)
    def _():
        halo[0] = jnp.zeros(halo.shape[1:], halo.dtype)

    @pl.when(f == 3)
    def _():
        halo[1] = jnp.zeros(halo.shape[1:], halo.dtype)


def wait_halos(down, up):
    f = lax.axis_index("frame")

    @pl.when(f > 0)
    def _():
        down.wait_send()
        up.wait_recv()

    @pl.when(f < 3)
    def _():
        up.wait_send()
        down.wait_recv()


EXP_SCALE = SCORE_SCALE * LOG2E


def tail_lanes(inside, copies):
    lane = lax.broadcasted_iota(jnp.int32, (inside.shape[0], PAIR), 1)
    tail = jnp.where(
        lane == HEAD_DIM,
        jnp.where(inside, 0.0, MASKED),
        jnp.where((lane > HEAD_DIM) & (lane < HEAD_DIM + 4), 1.0, 0.0),
    )
    return jnp.concatenate([tail] * copies, axis=0).astype(BF)


def front_kernel(
    clips,
    x_ref,
    side_ref,
    cells_ref,
    qkv_ref,
    proj_ref,
    up_ref,
    down_ref,
    vec_ref,
    taps_ref,
    tok_out,
    nhome_out,
    ncross_out,
    q_out,
    home_out,
    cross_out,
    kept_out,
    att_out,
    wq_out,
    wkv_out,
    others_out,
    tok_ref,
    nhome_ref,
    ncross_ref,
    q_ref,
    home_ref,
    cross_ref,
    kept_ref,
    att_ref,
    wq_ref,
    wkv_ref,
    others_ref,
    halo_ref,
    edge,
    raw,
    center,
    edged,
    qkv_full,
    tail,
    halo_sems,
    qkv_sems,
    other_sems,
    spread_sems,
    near_sems,
    cross_sems,
    out_sems,
):
    leaving = []

    def leave(src, dst):
        copy = pltpu.make_async_copy(src, dst, out_sems.at[len(leaving)])
        copy.start()
        leaving.append(copy)

    f, near, across, far = frame_peers()
    c = lax.axis_index("clip")
    greet_all(clips)
    part_rows = qkv_ref.shape[1]

    def qkv_rows(owner):
        return qkv_full.at[pl.ds(pl.multiple_of(owner * part_rows, 16), part_rows), :]

    qkv_full[pl.ds(pl.multiple_of(f * part_rows, 16), part_rows), :] = qkv_ref[...].T.astype(BF)
    start = 0
    for shard in (proj_ref, up_ref, down_ref):
        size = shard.shape[0]
        others_ref[f, start : start + size, :] = shard[...].astype(BF)
        start += size
    spare = others_ref.shape[1] - start
    if spare:
        others_ref[f, start : start + spare, :] = jnp.zeros((spare, D), BF)
    cells = cells_ref[...]
    inside = inside_of(side_ref, cells)
    for t in range(2):
        flatten_frame(lambda row, t=t: x_ref[0, row, :, t, :], raw, 400 * t)
        edge[t] = raw[400 * t : 400 * t + 400, :].astype(BF)

    await_greetings(3 + clips - 1)
    down, up = halo_copies(edge.at[0], edge.at[1], halo_ref, halo_sems)
    start_halos(down, up, halo_ref)
    qkv_cross = send(qkv_rows(f), qkv_rows(f), qkv_sems.at[0, 1], qkv_sems.at[1, 1], across)
    qkv_near = send(qkv_rows(f), qkv_rows(f), qkv_sems.at[0, 0], qkv_sems.at[1, 0], near)
    qkv_relay = send(
        qkv_rows(across), qkv_rows(across), qkv_sems.at[0, 2], qkv_sems.at[1, 2], near
    )
    qkv_near.start()

    part = others_ref.shape[1] // clips

    def part_of(owner, clip):
        return others_ref.at[owner, pl.ds(pl.multiple_of(clip * part, 16), part), :]

    other_near = send(
        others_ref.at[f], others_ref.at[f], other_sems.at[0, 0], other_sems.at[1, 0], near
    )
    other_cross = send(
        part_of(f, c), part_of(f, c), other_sems.at[0, 1], other_sems.at[1, 1], across
    )
    other_relay = send(
        others_ref.at[across],
        others_ref.at[across],
        other_sems.at[0, 2],
        other_sems.at[1, 2],
        near,
    )

    def spread(clip, landing):
        return pltpu.make_async_remote_copy(
            src_ref=part_of(across, c),
            dst_ref=part_of(across, landing),
            send_sem=spread_sems.at[0, clip],
            recv_sem=spread_sems.at[1, landing],
            device_id={"clip": clip},
            device_id_type=MESH,
        )

    def other_clips(act):
        def body(step, carry):
            act(lax.rem(c + step, clips))
            return carry

        lax.fori_loop(1, clips, body, 0)

    other_near.start()

    for t in range(2):
        build_slabs(
            center, edged, t + 1, jnp.where(inside, raw[400 * t : 400 * t + 400, :], 0.0), cells
        )

    def conv_part(t, depths, start, total):
        for a in depths:
            for b in range(3):
                for e in range(3):
                    offset = 9 * a + 3 * b + e
                    total = total + taps_ref[offset : offset + 1, :] * slab(
                        center, edged, t + a, b, e, start, 40
                    )
        return total

    for t, depths in ((0, (1, 2)), (1, (0, 1))):

        def own_part(step, carry, t=t, depths=depths):
            start = pl.multiple_of(step * 40, 8)
            at = pl.ds(pl.multiple_of(start + 400 * t, 8), 40)
            tok_ref[at, :] = conv_part(t, depths, start, raw[at, :] + vec_ref[4:5, :])
            return carry

        lax.fori_loop(0, 10, own_part, 0)
        if t == 0:
            qkv_cross.start()
            other_cross.start()
    wait_halos(down, up)
    for side, slot in ((0, 0), (1, 3)):
        rim = halo_ref[side].astype(F32)
        build_slabs(center, edged, slot, jnp.where(inside, rim, 0.0), cells)
    rows = tok_ref.shape[0]
    piece = rows // HEADS

    def cross_copy(k):
        at = pl.ds(pl.multiple_of(k * piece, 16), piece)
        return send(
            nhome_ref.at[at, :],
            ncross_ref.at[at, :],
            cross_sems.at[0, 0, k],
            cross_sems.at[1, 0, k],
            across,
        )

    def relay_copy(k):
        return send(
            ncross_ref.at[pl.ds(pl.multiple_of(k * piece, 16), piece), :],
            ncross_ref.at[pl.ds(pl.multiple_of(rows + k * piece, 16), piece), :],
            cross_sems.at[0, 1, k],
            cross_sems.at[1, 1, k],
            near,
        )

    near_copy = send(
        nhome_ref.at[pl.ds(0, rows), :],
        nhome_ref.at[pl.ds(rows, rows), :],
        near_sems.at[0],
        near_sems.at[1],
        near,
    )
    for t, depths, ready in ((0, (0,), (0, 1)), (1, (2,), (2, 3, 4))):

        def rim_part(step, carry, t=t, depths=depths):
            start = pl.multiple_of(step * 40, 8)
            at = pl.ds(pl.multiple_of(start + 400 * t, 8), 40)
            rows = conv_part(t, depths, start, tok_ref[at, :])
            tok_ref[at, :] = rows
            raw[at, :] = norm_parts(rows)[0] * vec_ref[0:1, :] + vec_ref[1:2, :]
            return carry

        lax.fori_loop(0, 10, rim_part, 0)
        at = slice(400 * t, 400 * t + 400)
        nhome_ref[at, :] = raw[at, :].astype(BF)
        for k in ready:
            cross_copy(k).start()
    near_copy.start()
    qkv_cross.wait_recv()
    qkv_relay.start()
    other_cross.wait_recv()
    other_clips(lambda clip: spread(clip, c).start())

    blank = jnp.zeros((1, HEAD_DIM), F32)

    def head_bias(row, h):
        return vec_ref[row : row + 1, HEAD_DIM * h : HEAD_DIM * (h + 1)]

    qkv_near.wait_recv()
    qkv_relay.wait_recv()
    for h in range(HEADS):
        wq_ref[PAIR * h : PAIR * h + HEAD_DIM, :] = qkv_full[HEAD_DIM * h : HEAD_DIM * (h + 1), :]
        wq_ref[PAIR * h + HEAD_DIM : PAIR * (h + 1), :] = jnp.zeros((HEAD_DIM, D), BF)
        wkv_ref[PAIR * h : PAIR * h + HEAD_DIM, :] = qkv_full[
            D + HEAD_DIM * h : D + HEAD_DIM * (h + 1), :
        ]
        wkv_ref[PAIR * h + HEAD_DIM : PAIR * (h + 1), :] = qkv_full[
            2 * D + HEAD_DIM * h : 2 * D + HEAD_DIM * (h + 1), :
        ]
    leave(tok_ref, tok_out)
    leave(wq_ref, wq_out)
    leave(wkv_ref, wkv_out)
    wide_query = jnp.concatenate(
        [part for h in range(HEADS) for part in (head_bias(5, h), blank)], axis=1
    )
    wide_pair = jnp.concatenate(
        [part for h in range(HEADS) for part in (blank, head_bias(6, h))], axis=1
    )

    def project(normed, weight, bias, place):
        joined = (dot_nt(normed, weight[...]) + bias).astype(BF)
        for h in range(HEADS):
            place(h, joined[:, PAIR * h : PAIR * (h + 1)])

    def place_query(h, value):
        q_ref[h] = value

    def place_own(h, value):
        home_ref[h, 0:rows, :] = value

    def place_near(h, value):
        home_ref[h, rows : 2 * rows, :] = value

    def place_cross(h, value):
        cross_ref[h] = value

    project(nhome_ref[0:rows, :], wq_ref, wide_query, place_query)
    project(nhome_ref[0:rows, :], wkv_ref, wide_pair, place_own)
    leave(q_ref, q_out)
    tail[...] = tail_lanes(inside, 4)
    tile = rows // 2
    mask_lane = jnp.where(lanes_of(tile) == HEAD_DIM, 1.0, 0.0).astype(BF)

    def tile_pass(t, source, last):
        at = pl.ds(pl.multiple_of(t * tile, 16), tile)
        lane = lanes_of(tile)
        for h in range(HEADS):
            keys = jnp.concatenate([source[h], tail[...]], axis=1)
            score = dot_nt(jnp.concatenate([q_ref[h, at, :], mask_lane], axis=1), keys)
            peak = jnp.max(score, axis=-1, keepdims=True)
            if last:
                kept = kept_ref[h, at, :]
                old_peak = kept[:, 0:1]
                peak = jnp.maximum(peak, old_peak)
            terms = jnp.exp2((score - peak) * EXP_SCALE).astype(BF)
            mixed = dot_nn(terms, keys)
            total = mixed[:, PAIR + HEAD_DIM + 1 : PAIR + HEAD_DIM + 2]
            mixed = mixed[:, 0:PAIR]
            if last:
                fade = jnp.exp2((old_peak - peak) * EXP_SCALE)
                total = total + fade * kept[:, 32:33]
                mixed = (mixed + fade * kept) / total
                log_sum = peak + jnp.log2(total) * (1.0 / EXP_SCALE)
                kept_ref[h, at, :] = jnp.where(lane < HEAD_DIM, log_sum, mixed)
                att_ref[h, at, :] = jnp.where(lane < HEAD_DIM, 0.0, mixed).astype(BF)
            else:
                kept_ref[h, at, :] = jnp.where(
                    lane < 32, peak, jnp.where(lane < HEAD_DIM, total, mixed)
                )

    def pass_on(k):
        cross_copy(k).wait_recv()
        relay_copy(k).start()

    def first_pass(t, carry):
        tile_pass(t, home_ref, False)

        @pl.when(t == 0)
        def _():
            for k in (0, 1, 2):
                pass_on(k)

        return carry

    def second_pass(t, carry):
        tile_pass(t, cross_ref, True)

        @pl.when(t == 0)
        def _():
            other_relay.wait_recv()
            others_leave.start()

        return carry

    near_copy.wait_recv()
    other_near.wait()
    leave(nhome_ref, nhome_out)
    project(nhome_ref[rows : 2 * rows, :], wkv_ref, wide_pair, place_near)
    leave(home_ref, home_out)
    lax.fori_loop(0, 2, first_pass, 0)
    for k in (3, 4):
        pass_on(k)
    other_clips(lambda clip: spread(clip, clip).wait_recv())
    other_relay.start()
    others_leave = pltpu.make_async_copy(others_ref, others_out, out_sems.at[out_sems.shape[0] - 1])
    for k in range(HEADS):
        relay_copy(k).wait_recv()
    leave(ncross_ref, ncross_out)
    project(ncross_ref[...], wkv_ref, wide_pair, place_cross)
    leave(cross_ref, cross_out)
    lax.fori_loop(0, 2, second_pass, 0)
    leave(kept_ref, kept_out)
    leave(att_ref, att_out)
    other_relay.wait_send()
    other_clips(lambda clip: spread(clip, c).wait_send())
    for copy in (other_cross, near_copy, qkv_cross, qkv_near, qkv_relay):
        copy.wait_send()
    for k in range(HEADS):
        cross_copy(k).wait_send()
        relay_copy(k).wait_send()
    others_leave.wait()
    for copy in leaving:
        copy.wait()


def front(clips_in, clip_side, qkv, proj, up, down, vectors, taps, clips, collective_id):
    rows = 800
    other_rows = clips * share_rows(proj.shape[0] + up.shape[0] + down.shape[0], clips)
    outs = (
        ((rows, D), F32),
        ((2 * rows, D), BF),
        ((2 * rows, D), BF),
        ((HEADS, rows, PAIR), BF),
        ((HEADS, 2 * rows, PAIR), BF),
        ((HEADS, 2 * rows, PAIR), BF),
        ((HEADS, rows, PAIR), F32),
        ((HEADS, rows, PAIR), BF),
        ((WIDE, D), BF),
        ((WIDE, D), BF),
        ((4, other_rows, D), BF),
    )
    return pl.pallas_call(
        functools.partial(front_kernel, clips),
        in_specs=[VMEM_SPEC, pl.BlockSpec(memory_space=pltpu.SMEM)] + [VMEM_SPEC] * 7,
        out_specs=[pl.BlockSpec(memory_space=pl.ANY)] * len(outs),
        out_shape=[jax.ShapeDtypeStruct(*out) for out in outs],
        scratch_shapes=[pltpu.VMEM(*out) for out in outs]
        + [
            pltpu.VMEM((2, 400, D), BF),
            pltpu.VMEM((2, 400, D), BF),
            pltpu.VMEM((rows, D), F32),
            pltpu.VMEM((3, 4, 400, D), F32),
            pltpu.VMEM((3, 4, 440, D), F32),
            pltpu.VMEM((3 * D, D), BF),
            pltpu.VMEM((2 * rows, PAIR), BF),
            pltpu.SemaphoreType.DMA((2, 2)),
            pltpu.SemaphoreType.DMA((2, 3)),
            pltpu.SemaphoreType.DMA((2, 3)),
            pltpu.SemaphoreType.DMA((2, clips)),
            pltpu.SemaphoreType.DMA((2,)),
            pltpu.SemaphoreType.DMA((2, 2, HEADS)),
            pltpu.SemaphoreType.DMA((len(outs),)),
        ],
        compiler_params=pltpu.CompilerParams(
            collective_id=collective_id, has_side_effects=True, vmem_limit_bytes=60 * 2**20
        ),
        cost_estimate=pl.CostEstimate(
            flops=2**34, bytes_accessed=16 * 2**20, transcendentals=2**23
        ),
    )(clips_in, clip_side, jnp.asarray(CELL_AT), qkv, proj, up, down, vectors, taps)


INV_SQRT2 = math.sqrt(0.5)
INV_SQRT_2PI = 1.0 / math.sqrt(2.0 * math.pi)


def dot_tn(left, right):
    return lax.dot_general(left, right, (((0,), (0,)), ((), ())), preferred_element_type=F32)


def norm_back(upstream, unit, scale, gain):
    through = upstream * gain
    mean_one = jnp.sum(through, axis=-1, keepdims=True) * (1.0 / D)
    mean_two = jnp.sum(through * unit, axis=-1, keepdims=True) * (1.0 / D)
    return scale * (through - mean_one - unit * mean_two)


def column_sum(rows):
    return jnp.sum(rows, axis=0, keepdims=True)


def mid_phase(
    att_ref,
    tok_ref,
    og_ref,
    side_ref,
    cells_ref,
    vec_ref,
    ubias_ref,
    others_ref,
    out_ref,
    gsec_ref,
    dout_ref,
    grads_ref,
    vsum_ref,
    raw,
    first_out,
    wide,
    act,
    ghid,
    normed,
    top,
    branch_low,
    att_low,
    proj_ref,
    up_ref,
    down_ref,
):
    start = 0
    for full in (proj_ref, up_ref, down_ref):
        size = full.shape[0] // 4
        for owner in range(4):
            full[size * owner : size * (owner + 1), :] = others_ref[owner, start : start + size, :]
        start += size
    up_bias = jnp.concatenate([ubias_ref[r : r + 1, :] for r in range(FF // 128)], axis=1)
    inside = inside_of(side_ref, cells_ref[...])
    pick = select_lanes(True).astype(F32).astype(BF)
    wide[...] = dot_nn(proj_ref[...], pick).astype(BF)
    vsum_ref[...] = jnp.zeros(vsum_ref.shape, F32)
    for t in range(2):
        at = slice(400 * t, 400 * t + 400)
        heads = jnp.concatenate([att_ref[h, at, :] for h in range(HEADS)], axis=1)
        att_low[at, :] = dot_nt(heads, pick).astype(BF)
        second = tok_ref[at, :] + (dot_nt(heads, wide[...]) + vec_ref[7:8, :])
        unit, scale = norm_parts(second)
        normed_two = (unit * vec_ref[2:3, :] + vec_ref[3:4, :]).astype(BF)
        normed[at, :] = normed_two
        flatten_frame(lambda row, t=t: og_ref[0, row, :, t, :], raw, 0)
        grad_top = jnp.where(inside, raw[...], 0.0)
        top_low = grad_top.astype(BF)
        top[at, :] = top_low
        hidden = dot_nt(normed_two, up_ref[...]) + up_bias
        half = 0.5 + 0.5 * lax.erf(hidden * INV_SQRT2)
        activated = (hidden * half).astype(BF)
        act[at, :] = activated
        slope = half + hidden * (INV_SQRT_2PI * jnp.exp(-0.5 * hidden * hidden))
        grad_hidden = (dot_nt(top_low, down_ref[...]) * slope).astype(BF)
        ghid[at, :] = grad_hidden
        result = second + (dot_nn(activated, down_ref[...]) + vec_ref[8:9, :])
        if t == 0:
            first_out[...] = result
        else:
            raw[...] = result
            for row in range(20):
                part = slice(20 * row, 20 * row + 20)
                out_ref[0, row] = jnp.stack([first_out[part, :], raw[part, :]], axis=1).astype(BF)
        upstream = dot_nn(grad_hidden, up_ref[...])
        grad_second = grad_top + norm_back(upstream, unit, scale, vec_ref[2:3, :])
        gsec_ref[at, :] = grad_second
        low = grad_second.astype(BF)
        branch_low[at, :] = low
        dout = dot_nn(low, wide[...]).astype(BF)
        for h in range(HEADS):
            dout_ref[h, at, :] = dout[:, PAIR * h : PAIR * (h + 1)]
        vsum_ref[0:1, :] += column_sum(upstream * unit)
        vsum_ref[1:2, :] += column_sum(upstream)
        vsum_ref[2:3, :] += column_sum(low.astype(F32))
        vsum_ref[3:4, :] += column_sum(grad_top)
        bias_sum = column_sum(grad_hidden.astype(F32))
        for part in range(4):
            vsum_ref[4 + part : 5 + part, :] += bias_sum[:, D * part : D * (part + 1)]
    rows = up_ref.shape[0] // 4
    proj_rows = D // 4
    grad = dot_tn(branch_low[...], att_low[...]).astype(BF)
    for owner in range(4):
        grads_ref[owner, 0:proj_rows, :] = grad[proj_rows * owner : proj_rows * (owner + 1), :]
    for owner in range(4):
        at = slice(rows * owner, rows * (owner + 1))
        start = proj_rows
        grads_ref[owner, start : start + rows, :] = dot_tn(ghid[:, at], normed[...]).astype(BF)
        start = proj_rows + rows
        grads_ref[owner, start : start + rows, :] = dot_tn(act[:, at], top[...]).astype(BF)


class RowSums:
    def __init__(self, clips, g_ref, at, pair_in, cross_out, cross_in, shares, shares_in, sums,
                 frame_sems, part_sems, sum_sems):
        self.clips = clips
        self.g = g_ref
        self.at = at
        self.pair_in = pair_in
        self.cross_out = cross_out
        self.cross_in = cross_in
        self.shares = shares
        self.shares_in = shares_in
        self.sums = sums
        self.part_sems = part_sems
        self.sum_sems = sum_sems
        f, near, across, far = frame_peers()
        self.f, self.across = f, across
        self.c = lax.axis_index("clip")
        sem = frame_sems
        part = lambda owner: g_ref.at[owner, pl.ds(at.start, at.stop - at.start), :]
        self.first = send(part(far), pair_in.at[0], sem.at[0, 0], sem.at[1, 0], near)
        self.second = send(part(near), pair_in.at[1], sem.at[0, 1], sem.at[1, 1], near)
        self.cross = send(cross_out, cross_in, sem.at[0, 2], sem.at[1, 2], across)

    def peer(self, step):
        return lax.rem(self.c + step, self.clips)

    def part_copy(self, step):
        return pltpu.make_async_remote_copy(
            src_ref=self.shares.at[self.peer(step)],
            dst_ref=self.shares_in.at[step],
            send_sem=self.part_sems.at[0, step],
            recv_sem=self.part_sems.at[1, step],
            device_id={"clip": self.peer(step)},
            device_id_type=MESH,
        )

    def sum_copy(self, step):
        return pltpu.make_async_remote_copy(
            src_ref=self.sums.at[self.c],
            dst_ref=self.sums.at[self.c],
            send_sem=self.sum_sems.at[0, step],
            recv_sem=self.sum_sems.at[1, step],
            device_id={"clip": self.peer(step)},
            device_id_type=MESH,
        )

    def each(self, act):
        def body(step, carry):
            act(step)
            return carry

        lax.fori_loop(1, self.clips, body, 0)

    def pair_step(self):
        self.first.start()
        self.second.start()

    def cross_step(self):
        self.first.wait()
        self.cross_out[...] = (
            self.g[self.across, self.at, :].astype(F32) + self.pair_in[0].astype(F32)
        ).astype(BF)
        self.cross.start()

    def share_step(self):
        self.second.wait()
        self.cross.wait()
        mine = (
            self.g[self.f, self.at, :].astype(F32)
            + self.pair_in[1].astype(F32)
            + self.cross_in[...].astype(F32)
        ).astype(BF)
        rows, chunk = mine.shape[0], self.shares.shape[1]
        spare = self.clips * chunk - rows
        if spare:
            mine = jnp.concatenate([mine, jnp.zeros((spare, D), BF)], axis=0)
        self.shares[...] = mine.reshape(self.clips, chunk, D)
        self.each(lambda step: self.part_copy(step).start())

    def sum_step(self):
        self.each(lambda step: self.part_copy(step).wait())

        def add_part(step, total):
            return total + self.shares_in[step].astype(F32)

        total = lax.fori_loop(1, self.clips, add_part, self.shares[self.c].astype(F32))
        self.sums[self.c] = total.astype(BF)
        self.each(lambda step: self.sum_copy(step).start())

    def finish(self):
        self.each(lambda step: self.sum_copy(step).wait())


def row_sums_scratch(rows, clips):
    chunk = share_rows(rows, clips)
    return [
        pltpu.VMEM((2, rows, D), BF),
        pltpu.VMEM((rows, D), BF),
        pltpu.VMEM((rows, D), BF),
        pltpu.VMEM((clips, chunk, D), BF),
        pltpu.VMEM((clips, chunk, D), BF),
        pltpu.VMEM((clips, chunk, D), BF),
        pltpu.SemaphoreType.DMA((2, 3)),
        pltpu.SemaphoreType.DMA((2, clips)),
        pltpu.SemaphoreType.DMA((2, clips)),
    ]


EARLY_PARTS = (slice(0, 400), slice(400, 720))


def row_pieces(start, size, block):
    pieces, skip = [], 0
    while skip < size:
        owner, row = divmod(start + skip, block)
        step = min(size - skip, block - row)
        pieces.append((owner, row, skip, step))
        skip += step
    return pieces


def back_phase(
    one,
    two,
    arrived,
    q_ref,
    dout_ref,
    kept_ref,
    cross_ref,
    home_ref,
    nhome_ref,
    ncross_ref,
    wq_ref,
    wkv_ref,
    side_ref,
    cells_ref,
    gnorm_ref,
    own_ref,
    out_ref,
    bsum_ref,
    grads_ref,
    grads_in,
    pair_out,
    pair_in,
    cross_out,
    cross_in,
    pair_sems,
    cross_sems,
    grad_sems,
    extra,
    qd_t,
    tail,
    low_one,
    low_two,
    low_three,
    dq_sum,
    turned_pairs,
    pair_grad,
):
    f, near, across, far = frame_peers()
    rows = q_ref.shape[1]
    dnormed = gnorm_ref
    dq_low = q_ref
    tail[...] = tail_lanes(inside_of(side_ref, cells_ref[...]), 4)
    arrived(0, 3)
    lower = lax.broadcasted_iota(jnp.int32, (PAIR, 1), 0) < HEAD_DIM
    scale_of = jnp.where(lower, SCORE_SCALE, 1.0)
    chunks = ((0, 512, low_one), (512, 512, low_two), (1024, 576, low_three))

    def minus_parts(column, lane):
        high = column.astype(BF).astype(F32)
        mid = (column - high).astype(BF).astype(F32)
        rest = column - high - mid
        return jnp.where(
            lane == HEAD_DIM + 1,
            -high,
            jnp.where(lane == HEAD_DIM + 2, -mid, jnp.where(lane == HEAD_DIM + 3, -rest, 0.0)),
        )

    def prepare(h):
        lane = lanes_of(rows)
        kept = kept_ref[h]
        queries, douts = q_ref[h].astype(F32), dout_ref[h].astype(F32)
        log_sum = kept[:, 0:1]
        row_dot = jnp.sum(douts * kept, axis=-1, keepdims=True)
        of_queries = jnp.where(lane == HEAD_DIM, 1.0, minus_parts(log_sum, lane))
        extra[h, 0:rows, :] = of_queries.astype(BF)
        extra[h, rows : 2 * rows, :] = minus_parts(row_dot, lane).astype(BF)
        qd_t[h] = jnp.concatenate([queries, douts], axis=0).T.astype(BF)
        bsum_ref[1, h] = column_sum(douts)

    def head_pass(h, source, add):
        pairs = source[h]
        both = jnp.concatenate([q_ref[h], dout_ref[h]], axis=0)
        both = jnp.concatenate([both, extra[h]], axis=1)
        products = [
            dot_nt(
                both,
                jnp.concatenate(
                    [pairs[start : start + size, :], tail[start : start + size, :]], axis=1
                ),
            )
            for start, size, low in chunks
        ]
        total = dq_sum[h] if add else None
        at = pl.ds(pl.multiple_of(h * PAIR, PAIR), PAIR)
        for (start, size, low), product in zip(chunks, products):
            probs = jnp.exp2(product[0:rows, :] * EXP_SCALE)
            low[0:rows, :] = (probs * product[rows : 2 * rows, :]).astype(BF)
            low[rows : 2 * rows, :] = probs.astype(BF)
            part = dot_nn(low[0:rows, :], pairs[start : start + size, :])
            total = part if total is None else total + part
            turned = dot_nn(qd_t[h], low[...]) * scale_of
            turned_pairs[at, start : start + size] = turned.astype(BF)
        if add:
            total = jnp.where(lanes_of(rows) < HEAD_DIM, total * SCORE_SCALE, 0.0)
            dq_low[h] = total.astype(BF)
            bsum_ref[0, h] = column_sum(total)
        else:
            dq_sum[h] = total

    def of_normed(normed, add):
        grad = dot_nn(turned_pairs[...], normed[...])
        pair_grad[...] = pair_grad[...] + grad if add else grad
        total = dot_nn(wkv_ref[...].astype(F32).T.astype(BF), turned_pairs[...]).T
        dnormed[...] = total[0:rows, :]
        pair_out[...] = total[rows : 2 * rows, :].astype(BF)

    def pair_copy(phase):
        return send(
            pair_out, pair_in.at[phase], pair_sems.at[0, phase], pair_sems.at[1, phase], near
        )

    to_across = send(cross_out, cross_in, cross_sems.at[0], cross_sems.at[1], across)

    def cross_pass(h, carry):
        prepare(h)
        head_pass(h, cross_ref, False)

        @pl.when(h == 0)
        def _():
            one.cross_step()
            two.cross_step()

        @pl.when(h == 3)
        def _():
            one.share_step()

        return carry

    def home_pass(h, carry):
        head_pass(h, home_ref, True)

        @pl.when(h == 0)
        def _():
            pair_copy(0).wait()
            cross_out[...] = (dnormed[...] + pair_in[0].astype(F32)).astype(BF)
            to_across.start()
            two.share_step()

        @pl.when(h == 1)
        def _():
            one.sum_step()

        @pl.when(h == 3)
        def _():
            two.sum_step()

        return carry

    lax.fori_loop(0, HEADS, cross_pass, 0)
    arrived(3, 8)
    of_normed(ncross_ref, False)
    pair_copy(0).start()
    lax.fori_loop(0, HEADS, home_pass, 0)
    of_normed(nhome_ref, True)
    pair_copy(1).start()

    block = grads_ref.shape[1]

    def place(start, values):
        for owner, row, skip, size in row_pieces(start, values.shape[0], block):
            grads_ref[owner, row : row + size, :] = values[skip : skip + size, :]

    dq = jnp.concatenate([dq_low[h] for h in range(HEADS)], axis=1)
    of_queries = dot_tn(dq, nhome_ref[0:rows, :]).astype(BF)
    for h in range(HEADS):
        of_pairs = pair_grad[PAIR * h : PAIR * (h + 1), :].astype(BF)
        place(HEAD_DIM * h, of_queries[PAIR * h : PAIR * h + HEAD_DIM, :])
        place(D + HEAD_DIM * h, of_pairs[0:HEAD_DIM, :])
        place(2 * D + HEAD_DIM * h, of_pairs[HEAD_DIM:PAIR, :])
    to_pair = [
        send(grads_ref.at[peer], grads_in.at[k], grad_sems.at[0, k], grad_sems.at[1, k], near)
        for k, peer in enumerate((far, near))
    ]
    for copy in to_pair:
        copy.start()
    total = dnormed[...] + dot_nn(dq, wq_ref[...])
    to_across.wait()
    pair_copy(1).wait()
    gnorm_ref[...] = total + pair_in[1].astype(F32) + cross_in[...].astype(F32)
    for copy in to_pair:
        copy.wait()
    out_ref[...] = (grads_ref[across].astype(F32) + grads_in[0].astype(F32)).astype(BF)
    own_ref[...] = grads_ref[f].astype(F32) + grads_in[1].astype(F32)


def newton_schulz(whole):
    wide = whole.astype(F32)
    norm = jnp.sqrt(jnp.sum(wide * wide)) + 1e-07
    eye = (
        lax.broadcasted_iota(jnp.int32, (D, D), 0) == lax.broadcasted_iota(jnp.int32, (D, D), 1)
    ).astype(F32)
    turned = dot_nt(eye.astype(BF), whole) / norm

    def iterate(step, current):
        held = current.astype(BF)
        gram = dot_nt(held, held)
        gram_low = gram.astype(BF)
        poly = POLY_TWO * gram + POLY_THREE * dot_nn(gram_low, gram_low)
        return POLY_ONE * current + dot_nn(poly.astype(BF), held)

    return lax.fori_loop(0, NS_STEPS, iterate, turned)


OWNER_OF = (3, 1, 0, 2)
QKV_AT = OWNER_OF[0]


def tail_phase(
    clips,
    one,
    two,
    arrived,
    copy_out,
    gnorm_ref,
    own_ref,
    across_ref,
    bsum_ref,
    tok_ref,
    gsec_ref,
    x_ref,
    side_ref,
    cells_ref,
    taps_ref,
    vec_ref,
    mid_sums_ref,
    one_ref,
    two_ref,
    qkv_m_ref,
    proj_m_ref,
    up_m_ref,
    down_m_ref,
    late_ref,
    scaled_ref,
    vsum_ref,
    cross_in,
    shares,
    shares_in,
    new_rows,
    new_low,
    first_low,
    rim,
    v_mine,
    v_frames,
    v_total,
    v_clips,
    gathered,
    old_rows,
    center,
    edged,
    low,
    grad_sems,
    part_sems,
    row_sems,
    spread_sems,
    rim_sems,
    vf_sems,
    vc_sems,
    there_sems,
    back_sems,
):
    first, ingrad_ref, outer = gnorm_ref, gsec_ref, tok_ref
    f, near, across, far = frame_peers()
    c = lax.axis_index("clip")
    block = own_ref.shape[0]
    owners, chunk = shares.shape[0], shares.shape[1]

    def each(count, act):
        def body(step, carry):
            act(step)
            return carry

        lax.fori_loop(0, count, body, 0)

    def other_clips(act):
        each(clips - 1, lambda step: act(lax.rem(c + 1 + step, clips)))

    down, up = halo_copies(first_low.at[0], first_low.at[1], rim, rim_sems)

    to_across = send(across_ref, cross_in, grad_sems.at[0], grad_sems.at[1], across)
    to_across.start()

    upstream = gnorm_ref[...]
    unit, scale = norm_parts(tok_ref[...])
    grad_first = gsec_ref[...] + norm_back(upstream, unit, scale, vec_ref[0:1, :])
    first[...] = grad_first
    first_low[...] = grad_first.astype(BF).reshape(first_low.shape)
    one.finish()
    two.finish()
    one_ref[...] = one.sums[...].reshape(one_ref.shape)
    two_ref[...] = two.sums[...].reshape(two_ref.shape)
    arrived(0, 5)
    old_rows[0:block, :] = qkv_m_ref[...].T
    if owners * chunk > block:
        old_rows[block : owners * chunk, :] = jnp.zeros((owners * chunk - block, D), F32)

    v_mine[0:1, :] = column_sum(upstream * unit)
    v_mine[1:2, :] = column_sum(upstream)
    v_mine[2:4, :] = mid_sums_ref[0:2, :]
    v_mine[4:5, :] = column_sum(grad_first)
    v_mine[5:6, :] = jnp.concatenate(
        [bsum_ref[0, h, :, 0:HEAD_DIM] for h in range(HEADS)], axis=1
    )
    v_mine[6:7, :] = jnp.concatenate(
        [bsum_ref[1, h, :, HEAD_DIM:PAIR] for h in range(HEADS)], axis=1
    )
    v_mine[7:9, :] = mid_sums_ref[2:4, :]
    v_mine[9:13, :] = mid_sums_ref[4:8, :]

    cells = cells_ref[...]
    inside = inside_of(side_ref, cells)
    for t in range(2):
        build_slabs(center, edged, t + 1, first[400 * t : 400 * t + 400, :], cells)

    def part_copy(owner):
        return pltpu.make_async_remote_copy(
            src_ref=shares.at[owner],
            dst_ref=shares_in.at[c],
            send_sem=part_sems.at[0, owner],
            recv_sem=part_sems.at[1, c],
            device_id={"clip": owner},
            device_id_type=MESH,
        )

    def other_owners(act):
        def step(owner):
            @pl.when(owner != c)
            def _():
                act(owner)

        each(owners, step)

    to_across.wait()
    mine = (own_ref[...] + cross_in[...].astype(F32)).astype(BF)
    if owners * chunk > block:
        mine = jnp.concatenate([mine, jnp.zeros((owners * chunk - block, D), BF)], axis=0)
    shares[...] = mine.reshape(owners, chunk, D)
    other_owners(lambda owner: part_copy(owner).start())
    start_halos(down, up, rim)

    moments = (None, proj_m_ref, up_m_ref, down_m_ref)

    def to_owner(which):
        at = pl.ds(0, moments[which].shape[0])
        return send(
            low.at[which, at, :],
            gathered.at[f, at, :],
            there_sems.at[0, which],
            there_sems.at[1, f],
            OWNER_OF[which],
        )

    for which in (3, 2, 1):
        rows = moments[which].shape[0]
        summed = one_ref[80:400, :] if which == 2 else (two_ref if which == 3 else one_ref)[0:rows, :]
        low[which, 0:rows, :] = (0.95 * moments[which][...] + summed.astype(F32)).astype(BF)

        @pl.when(f != OWNER_OF[which])
        def _(which=which):
            to_owner(which).start()

    def row_copy(clip):
        return pltpu.make_async_remote_copy(
            src_ref=new_rows.at[c],
            dst_ref=new_rows.at[c],
            send_sem=row_sems.at[0, clip],
            recv_sem=row_sems.at[1, c],
            device_id={"clip": clip},
            device_id_type=MESH,
        )

    def spread_copy(clip):
        return pltpu.make_async_remote_copy(
            src_ref=new_low,
            dst_ref=gathered.at[f, pl.ds(pl.multiple_of(c * chunk, 16), chunk), :],
            send_sem=spread_sems.at[4, clip],
            recv_sem=spread_sems.at[f, c],
            device_id={"clip": clip, "frame": QKV_AT},
            device_id_type=MESH,
        )

    def share_sum():
        @pl.when(c < owners)
        def _():
            shares_in[c] = shares[c]

            def arrive(clip):
                pltpu.make_async_remote_copy(
                    src_ref=shares.at[0],
                    dst_ref=shares_in.at[clip],
                    send_sem=part_sems.at[0, 0],
                    recv_sem=part_sems.at[1, clip],
                    device_id={"clip": clip},
                    device_id_type=MESH,
                ).wait_recv()

            other_clips(arrive)

            def add_part(clip, total):
                return total + shares_in[clip].astype(F32)

            total = lax.fori_loop(0, clips, add_part, jnp.zeros((chunk, D), F32))
            at = pl.ds(pl.multiple_of(c * chunk, 16), chunk)
            fresh = 0.95 * old_rows[at, :] + total
            new_rows[c] = fresh
            new_low[...] = fresh.astype(BF)
            other_clips(lambda clip: spread_copy(clip).start())

            @pl.when(f != QKV_AT)
            def _():
                spread_copy(c).start()

            @pl.when(f == QKV_AT)
            def _():
                gathered[QKV_AT, at, :] = new_low[...]

            other_clips(lambda clip: row_copy(clip).start())

    for t in range(2):
        at = slice(400 * t, 400 * t + 400)
        flatten_frame(lambda row, t=t: x_ref[0, row, :, t, :], outer, 400 * t)
        outer[at, :] = jnp.where(inside, outer[at, :], 0.0)

    def plane(t, a, add_rows, add_taps):
        def step(number, totals):
            start = pl.multiple_of(number * 16, 16)
            at = pl.ds(pl.multiple_of(start + 400 * t, 16), 16)
            masked = outer[at, :]
            total = jnp.zeros((16, D), F32)
            sums_out = []
            for b in range(3):
                for e in range(3):
                    offset = 9 * a + 3 * b + e
                    piece = slab(center, edged, t + 2 - a, 2 - b, 2 - e, start, 16)
                    total = total + taps_ref[offset : offset + 1, :] * piece
                    product = masked * piece
                    sums_out.append(totals[3 * b + e] + (product[0:8, :] + product[8:16, :]))
            if add_rows:
                ingrad_ref[at, :] += total
            else:
                ingrad_ref[at, :] = total
            return tuple(sums_out)

        totals = lax.fori_loop(0, 25, step, tuple(jnp.zeros((8, D), F32) for _ in range(9)))
        for which, total in enumerate(totals):
            at = slice(13 + 9 * a + which, 14 + 9 * a + which)
            if add_taps:
                v_mine[at, :] += column_sum(total)
            else:
                v_mine[at, :] = column_sum(total)

    plane(0, 0, False, False)
    plane(0, 1, True, False)
    share_sum()
    plane(1, 1, False, True)
    plane(1, 2, True, False)
    wait_halos(down, up)
    for side, slot in ((0, 0), (1, 3)):
        build_slabs(center, edged, slot, rim[side].astype(F32), cells)
    plane(0, 2, True, True)
    plane(1, 0, True, True)
    for t in range(2):
        at = slice(400 * t, 400 * t + 400)
        ingrad_ref[at, :] = first[at, :] + jnp.where(inside, ingrad_ref[at, :], 0.0)
    copy_out()

    v_copies = []
    for which, peer in enumerate((near, across, far)):
        copy = send(v_mine, v_frames.at[f], vf_sems.at[0, which], vf_sems.at[1, which], peer)
        copy.start()
        v_copies.append(copy)
    v_frames[f] = v_mine[...]

    @pl.when(f == QKV_AT)
    def _():
        def rows_arrive(frame, clip):
            pltpu.make_async_remote_copy(
                src_ref=new_low,
                dst_ref=gathered.at[frame, pl.ds(pl.multiple_of(clip * chunk, 16), chunk), :],
                send_sem=spread_sems.at[4, clip],
                recv_sem=spread_sems.at[frame, clip],
                device_id={"clip": clip, "frame": frame},
                device_id_type=MESH,
            ).wait_recv()

        other_owners(lambda clip: rows_arrive(QKV_AT, clip))
        for step in (1, 2, 3):
            frame = (QKV_AT + step) % 4
            each(owners, lambda clip, frame=frame: rows_arrive(frame, clip))

    for which in (1, 2, 3):

        @pl.when(f != OWNER_OF[which])
        def _(which=which):
            to_owner(which).wait_send()

        @pl.when(f == OWNER_OF[which])
        def _(which=which):
            at = pl.ds(0, moments[which].shape[0])
            gathered[OWNER_OF[which], at, :] = low[which, at, :]
            for other in range(4):
                if other != OWNER_OF[which]:
                    send(
                        low.at[0, at, :],
                        gathered.at[other, at, :],
                        there_sems.at[0, 0],
                        there_sems.at[1, other],
                        other,
                    ).wait_recv()

    turned = newton_schulz(gathered[...].reshape(4 * SHARE, D))
    low[:, 0:SHARE, :] = turned.T.astype(BF).reshape(4, SHARE, D)
    row_counts = (block, *(ref.shape[0] for ref in moments[1:]))

    def back_copy(which, step):
        at = pl.ds(0, row_counts[which])
        to = (OWNER_OF[which] + step) % 4
        return send(
            low.at[to, at, :],
            scaled_ref.at[which, at, :],
            back_sems.at[0, step],
            back_sems.at[1, which],
            to,
        )

    for which in range(4):

        @pl.when(f == OWNER_OF[which])
        def _(which=which):
            for step in (2, 1, 3):
                back_copy(which, step).start()
            at = pl.ds(0, row_counts[which])
            scaled_ref[which, at, :] = low[OWNER_OF[which], at, :]

    for copy in v_copies:
        copy.wait()
    v_total[...] = v_frames[0] + v_frames[1] + v_frames[2] + v_frames[3]

    def v_copy(clip):
        return pltpu.make_async_remote_copy(
            src_ref=v_total,
            dst_ref=v_clips.at[c],
            send_sem=vc_sems.at[0, clip],
            recv_sem=vc_sems.at[1, c],
            device_id={"clip": clip},
            device_id_type=MESH,
        )

    other_clips(lambda clip: v_copy(clip).start())
    v_clips[c] = v_total[...]

    other_owners(lambda owner: part_copy(owner).wait_send())

    @pl.when(c < owners)
    def _():
        other_clips(lambda clip: spread_copy(clip).wait_send())

        @pl.when(f != QKV_AT)
        def _():
            spread_copy(c).wait_send()

        other_clips(lambda clip: row_copy(clip).wait_send())

    def new_rows_arrive(clip):
        pltpu.make_async_remote_copy(
            src_ref=new_rows.at[0],
            dst_ref=new_rows.at[clip],
            send_sem=row_sems.at[0, 0],
            recv_sem=row_sems.at[1, clip],
            device_id={"clip": clip},
            device_id_type=MESH,
        ).wait_recv()

    other_owners(new_rows_arrive)
    late_ref[...] = new_rows[...].reshape(late_ref.shape)

    def v_arrives(clip):
        v_copy(clip).wait_send()
        pltpu.make_async_remote_copy(
            src_ref=v_total,
            dst_ref=v_clips.at[clip],
            send_sem=vc_sems.at[0, clip],
            recv_sem=vc_sems.at[1, clip],
            device_id={"clip": clip},
            device_id_type=MESH,
        ).wait_recv()

    other_clips(v_arrives)

    def add_v(step, total):
        return total + v_clips[step]

    vsum_ref[...] = lax.fori_loop(0, clips, add_v, jnp.zeros(vsum_ref.shape, F32))
    for which in range(4):

        @pl.when(f == OWNER_OF[which])
        def _(which=which):
            for step in (2, 1, 3):
                back_copy(which, step).wait_send()

        @pl.when(f != OWNER_OF[which])
        def _(which=which):
            back_copy(which, 1).wait_recv()


def rest_kernel(
    clips,
    att_in,
    tok_in,
    og_in,
    others_in,
    side_ref,
    cells_ref,
    vec_ref,
    ubias_ref,
    taps_ref,
    *refs,
):
    refs = list(refs)

    def take(count):
        taken, refs[:count] = refs[:count], []
        return taken

    back_sources = take(8)
    tail_sources = take(5)
    block_out, ingrad_out, one_ref, two_ref, late_ref, scaled_ref, vsum_ref = take(7)
    tok, out, gsec, dout, early, mid_sums = take(6)
    back_inputs = take(8)
    gnorm, own, across_rows, bsum = take(4)
    back_buffers = take(6)
    back_sems = take(3)
    tail_landing = take(12)
    tail_sems = take(9)
    (copy_sems,) = take(1)
    half = len(refs) // 2
    f, near, across, far = frame_peers()
    c = lax.axis_index("clip")
    gathered = tail_landing[-1]
    block, proj_rows = own.shape[0], D // 4
    chunk = share_rows(block, clips)
    owned = -(-block // chunk) * chunk

    @pl.when(f == QKV_AT)
    def _():
        gathered[:, owned:SHARE, :] = jnp.zeros((4, SHARE - owned, D), BF)

    @pl.when(f == OWNER_OF[1])
    def _():
        gathered[:, proj_rows:SHARE, :] = jnp.zeros((4, SHARE - proj_rows, D), BF)

    greet_all(clips)
    barrier = pltpu.get_barrier_semaphore()

    def greet(frame):
        def body(step, carry):
            pl.semaphore_signal(
                barrier,
                inc=1,
                device_id={"clip": lax.rem(c + step, clips), "frame": frame},
                device_id_type=MESH,
            )
            return carry

        lax.fori_loop(1, clips, body, 0)

    @pl.when(f == QKV_AT)
    def _():
        for step in (1, 2, 3):
            greet((QKV_AT + step) % 4)

    @pl.when(f != QKV_AT)
    def _():
        greet(QKV_AT)

    def copies(sources, targets, first):
        return [
            pltpu.make_async_copy(src, dst, copy_sems.at[first + k])
            for k, (src, dst) in enumerate(zip(sources, targets))
        ]

    def arrival(waiting):
        def arrived(start, stop):
            for copy in waiting[start:stop]:
                copy.wait()

        return arrived

    for_back = copies(back_sources, back_inputs, 4)

    def middle(att, og, others, *scratch):
        for_mid = copies((others_in, att_in, tok_in, og_in), (others, att, tok, og), 0)
        for copy in for_mid:
            copy.start()
        for copy in for_mid:
            copy.wait()
        for copy in for_back:
            copy.start()
        mid_phase(
            att, tok, og, side_ref, cells_ref, vec_ref, ubias_ref, others, out, gsec, dout, early,
            mid_sums, *scratch,
        )

    rows = tok.shape[0]
    vmem = pltpu.VMEM
    pl.run_scoped(
        middle,
        vmem(att_in.shape, BF),
        vmem(og_in.shape, BF),
        vmem(others_in.shape, BF),
        vmem((400, D), F32),
        vmem((400, D), F32),
        vmem((D, WIDE), BF),
        vmem((rows, FF), BF),
        vmem((rows, FF), BF),
        vmem((rows, D), BF),
        vmem((rows, D), BF),
        vmem((rows, D), BF),
        vmem((rows, D), BF),
        vmem((D, D), BF),
        vmem((FF, D), BF),
        vmem((FF, D), BF),
    )
    out_copy = pltpu.make_async_copy(out, block_out, copy_sems.at[0])
    out_copy.start()

    @pl.when(f == QKV_AT)
    def _():
        await_greetings(3 + 4 * (clips - 1))

    @pl.when(f != QKV_AT)
    def _():
        await_greetings(3 + 2 * (clips - 1))

    one = RowSums(clips, early, EARLY_PARTS[0], *refs[:half])
    two = RowSums(clips, early, EARLY_PARTS[1], *refs[half:])
    one.pair_step()
    two.pair_step()

    def backward(*scratch):
        back_phase(
            one, two, arrival(for_back), back_inputs[0], dout, *back_inputs[1:], side_ref,
            cells_ref, gnorm, own, across_rows, bsum, *back_buffers, *back_sems, *scratch,
        )

    pl.run_scoped(
        backward,
        vmem((HEADS, 2 * rows, PAIR), BF),
        vmem((HEADS, PAIR, 2 * rows), BF),
        vmem((2 * rows, PAIR), BF),
        vmem((2 * rows, 512), BF),
        vmem((2 * rows, 512), BF),
        vmem((2 * rows, 576), BF),
        vmem((HEADS, rows, PAIR), F32),
        vmem((WIDE, 2 * rows), BF),
        vmem((WIDE, D), F32),
    )

    def finish(x, qkv_m, proj_m, up_m, down_m, *scratch):
        for_tail = copies(tail_sources, (x, qkv_m, proj_m, up_m, down_m), 12)
        for copy in for_tail:
            copy.start()
        leave = pltpu.make_async_copy(gsec, ingrad_out, copy_sems.at[1])
        tail_phase(
            clips, one, two, arrival(for_tail), leave.start, gnorm, own, across_rows, bsum, tok,
            gsec, x, side_ref, cells_ref, taps_ref, vec_ref, mid_sums, one_ref, two_ref, qkv_m,
            proj_m, up_m, down_m, late_ref, scaled_ref, vsum_ref, *tail_landing, *scratch, early,
            *tail_sems,
        )
        leave.wait()

    pl.run_scoped(
        finish,
        *(vmem(ref.shape, ref.dtype) for ref in tail_sources),
        vmem((owned, D), F32),
        vmem((3, 4, 400, D), F32),
        vmem((3, 4, 440, D), F32),
    )
    out_copy.wait()


def rest(mid_inputs, small, back_inputs, tail_inputs, clips, collective_id):
    rows, block = 800, 3 * D // 4
    chunk = share_rows(block, clips)
    owners = -(-block // chunk)
    vector_shape = (40, D)
    vmem = pltpu.VMEM
    dma = pltpu.SemaphoreType.DMA
    parts = [part.stop - part.start for part in EARLY_PARTS]
    hbm = pl.BlockSpec(memory_space=pl.ANY)
    return pl.pallas_call(
        functools.partial(rest_kernel, clips),
        in_specs=[hbm] * 4
        + [pl.BlockSpec(memory_space=pltpu.SMEM)]
        + [VMEM_SPEC] * 4
        + [hbm] * (len(back_inputs) + len(tail_inputs)),
        out_specs=[hbm] * 2 + [VMEM_SPEC] * 5,
        out_shape=[
            jax.ShapeDtypeStruct(mid_inputs[2].shape, BF),
            jax.ShapeDtypeStruct((rows, D), F32),
        ]
        + [
            jax.ShapeDtypeStruct((clips * share_rows(part, clips), D), BF) for part in parts
        ]
        + [
            jax.ShapeDtypeStruct((owners * chunk, D), F32),
            jax.ShapeDtypeStruct((4, SHARE, D), BF),
            jax.ShapeDtypeStruct(vector_shape, F32),
        ],
        scratch_shapes=[
            vmem((rows, D), F32),
            vmem(mid_inputs[2].shape, BF),
            vmem((rows, D), F32),
            vmem((HEADS, rows, PAIR), BF),
            vmem((4, (D + 2 * FF) // 4, D), BF),
            vmem((8, D), F32),
        ]
        + [vmem(ref.shape, ref.dtype) for ref in back_inputs]
        + [
            vmem((rows, D), F32),
            vmem((block, D), F32),
            vmem((block, D), BF),
            vmem((2, HEADS, 1, PAIR), F32),
            vmem((4, block, D), BF),
            vmem((2, block, D), BF),
            vmem((rows, D), BF),
            vmem((2, rows, D), BF),
            vmem((rows, D), BF),
            vmem((rows, D), BF),
            dma((2, 2)),
            dma((2,)),
            dma((2, 2)),
            vmem((block, D), BF),
            vmem((owners, chunk, D), BF),
            vmem((clips, chunk, D), BF),
            vmem((owners, chunk, D), F32),
            vmem((chunk, D), BF),
            vmem((2, 400, D), BF),
            vmem((2, 400, D), BF),
            vmem(vector_shape, F32),
            vmem((4,) + vector_shape, F32),
            vmem(vector_shape, F32),
            vmem((clips,) + vector_shape, F32),
            vmem((4, SHARE, D), BF),
            dma((2,)),
            dma((2, clips)),
            dma((2, clips)),
            dma((5, clips)),
            dma((2, 2)),
            dma((2, 3)),
            dma((2, clips)),
            dma((2, 4)),
            dma((2, 4)),
            dma((17,)),
        ]
        + row_sums_scratch(parts[0], clips)
        + row_sums_scratch(parts[1], clips),
        compiler_params=pltpu.CompilerParams(
            collective_id=collective_id, has_side_effects=True, vmem_limit_bytes=63 * 2**20
        ),
        cost_estimate=pl.CostEstimate(
            flops=2**36, bytes_accessed=32 * 2**20, transcendentals=2**25
        ),
    )(*mid_inputs, *small, *back_inputs, *tail_inputs)


def adamw(param, mean_old, square_old, gradient, rate_value, decay):
    mean_new = 0.9 * mean_old + 0.1 * gradient
    square_new = 0.999 * square_old + 0.001 * gradient * gradient
    mean_hat = mean_new / (1.0 - 0.9**STEP)
    square_hat = square_new / (1.0 - 0.999**STEP)
    return (
        mean_new,
        square_new,
        param - rate_value * (mean_hat / (jnp.sqrt(square_hat) + 1e-08) + decay * param),
    )


RATES = (0.2 * math.sqrt(3.0), 0.12 * math.sqrt(CLIP_TOK), 0.2 * math.sqrt(FF / D), 0.2)


def update_kernel(*refs):
    refs = list(refs)

    def take(count):
        taken, refs[:count] = refs[:count], []
        return taken

    large_in, (vsum_ref,), vectors, taps, biases = take(13), take(1), take(3), take(3), take(3)
    large_out, new_vectors, new_taps, new_biases = take(10), take(3), take(3), take(3)
    large, made, in_sems, out_sems = take(13), take(9), *take(2)
    arriving = [
        pltpu.make_async_copy(src, dst, in_sems.at[k])
        for k, (src, dst) in enumerate(zip(large_in, large))
    ]
    block, late_ref, one_ref, two_ref = large[:4]
    moments, scaled_ref, weights, ingrad_ref = large[4:7], large[7], large[8:12], large[12]
    leaving = [
        pltpu.make_async_copy(src, dst, out_sems.at[k])
        for k, (src, dst) in enumerate(zip([block] + made, large_out))
    ]
    new_moments, new_weights, out_ref = made[0:4], made[4:8], made[8]
    for copy in arriving:
        copy.start()

    def arrive(*numbers):
        for number in numbers:
            arriving[number].wait()

    arrive(0)
    leaving[0].start()
    arrive(1)
    new_moments[0][...] = late_ref[0 : weights[0].shape[1], :].T
    leaving[1].start()
    arrive(2, 3)
    for which in (1, 2, 3):
        arrive(3 + which)
        rows = weights[which].shape[0]
        summed = one_ref[80:400, :] if which == 2 else (two_ref if which == 3 else one_ref)[0:rows, :]
        new_moments[which][...] = 0.95 * moments[which - 1][...] + summed.astype(F32)
        leaving[1 + which].start()
    arrive(7)
    for which in range(4):
        arrive(8 + which)
        rows = weights[which].shape[1 if which == 0 else 0]
        scaled = scaled_ref[which, 0:rows, :].astype(F32)
        if which == 0:
            scaled = scaled.T
        new_weights[which][...] = 0.999 * weights[which][...] - RATES[which] * scaled
        leaving[5 + which].start()
    arrive(12)
    for row in range(20):
        at = slice(20 * row, 20 * row + 20), slice(400 + 20 * row, 420 + 20 * row)
        out_ref[0, row] = jnp.stack([ingrad_ref[part, :] for part in at], axis=1)
    leaving[9].start()
    bias_sums = vsum_ref[9:13, :]

    def bias_part(part):
        row, column = divmod(part * HEAD_DIM, D)
        return bias_sums[row : row + 1, column : column + HEAD_DIM]

    bias_grad = jnp.concatenate(
        [
            jnp.concatenate([bias_part(2 * r), bias_part(2 * r + 1)], axis=1)
            for r in range(FF // 128)
        ],
        axis=0,
    )
    for (param, mean, square), outs, grad, rate, decay in (
        (vectors, new_vectors, vsum_ref[0:9, :], 0.2, 0.0),
        (taps, new_taps, vsum_ref[13:40, :], 0.05, 0.01),
        (biases, new_biases, bias_grad, 0.2, 0.0),
    ):
        for ref, value in zip(
            outs, adamw(param[...], mean[...], square[...], grad, rate, decay)
        ):
            ref[...] = value
    for copy in leaving:
        copy.wait()


def update(block, sums, weights, moments, vectors, taps, biases):
    ingrad, late, one, two, scaled, vector_sums = sums
    large = [block, late, one, two, *moments[1:], scaled, *weights, ingrad]
    small = [vector_sums, *vectors, *taps, *biases]
    hbm = pl.BlockSpec(memory_space=pl.ANY)
    made = [jax.ShapeDtypeStruct(x.shape, F32) for x in (*moments, *weights, block)]
    outs = [jax.ShapeDtypeStruct(block.shape, BF), *made]
    outs += [jax.ShapeDtypeStruct(x.shape, F32) for x in small[1:]]
    return pl.pallas_call(
        update_kernel,
        in_specs=[hbm] * len(large) + [VMEM_SPEC] * len(small),
        out_specs=[hbm] * 10 + [VMEM_SPEC] * 9,
        out_shape=outs,
        scratch_shapes=[pltpu.VMEM(x.shape, x.dtype) for x in large]
        + [pltpu.VMEM(x.shape, x.dtype) for x in made]
        + [pltpu.SemaphoreType.DMA((len(large),)), pltpu.SemaphoreType.DMA((10,))],
        compiler_params=pltpu.CompilerParams(vmem_limit_bytes=62 * 2**20),
        cost_estimate=pl.CostEstimate(
            flops=2**22, bytes_accessed=12 * 2**20, transcendentals=2**14
        ),
    )(*large, *small)


def frames_last(block):
    return jnp.transpose(block, (0, 2, 3, 1, 4))


def frames_second(block):
    return jnp.transpose(block, (0, 3, 1, 2, 4))


def per_device(
    clips_in,
    out_grad,
    clip_side,
    qkv_weight,
    proj_weight,
    up_weight,
    down_weight,
    qkv_moment,
    proj_moment,
    up_moment,
    down_moment,
    vectors,
    vector_mean,
    vector_square,
    up_bias,
    up_bias_mean,
    up_bias_square,
    conv_kernel,
    kernel_mean,
    kernel_square,
):
    clips = lax.axis_size("clip")
    clips_in, out_grad = frames_last(clips_in), frames_last(out_grad)
    weights = (qkv_weight, proj_weight, up_weight, down_weight)
    moments = (qkv_moment, proj_moment, up_moment, down_moment)
    (
        tokens,
        normed_home,
        normed_cross,
        heads_q,
        home,
        cross,
        kept,
        heads_out,
        query_weight,
        pair_weight,
        other_weights,
    ) = front(clips_in, clip_side, qkv_weight.T, *weights[1:], vectors, conv_kernel, clips, 0)
    block_out, ingrad, sums_one, sums_two, late_moment, scaled, vector_sums = rest(
        (heads_out, tokens, out_grad, other_weights),
        (clip_side, jnp.asarray(CELL_AT), vectors, up_bias.reshape(FF // 128, 128), conv_kernel),
        (
            heads_q,
            kept,
            cross,
            home,
            normed_home,
            normed_cross,
            query_weight,
            pair_weight,
        ),
        (clips_in, qkv_moment.T, *moments[1:]),
        clips,
        1,
    )
    as_rows = lambda vector: vector.reshape(FF // 128, 128)
    updated = update(
        block_out,
        (ingrad, late_moment, sums_one, sums_two, scaled, vector_sums),
        (qkv_weight.T, *weights[1:]),
        (qkv_moment.T, *moments[1:]),
        (vectors, vector_mean, vector_square),
        (conv_kernel, kernel_mean, kernel_square),
        tuple(as_rows(vector) for vector in (up_bias, up_bias_mean, up_bias_square)),
    )
    new_moments = (updated[1].T, *updated[2:5])
    new_weights = (updated[5].T, *updated[6:9])
    outs = [frames_second(updated[0]), frames_second(updated[9])]
    for moment, weight in zip(new_moments, new_weights):
        outs += [moment, weight]
    bias_new = [vector.reshape(FF) for vector in updated[16:19]]
    return (*outs, *updated[10:13], *bias_new, *updated[13:16])


def solution(mesh):
    big = P("clip", "frame", None, None, None)
    rows = P("frame", None)
    return jax.shard_map(
        per_device,
        mesh=mesh,
        in_specs=(big, big, P("clip")) + (rows,) * 8 + (P(),) * 9,
        out_specs=(big, big) + (rows,) * 8 + (P(),) * 9,
        check_vma=False,
    )
```

```python
import functools
import math

import jax
import jax.numpy as jnp
import numpy as np
from jax import lax
from jax.experimental import pallas as pl
from jax.experimental.pallas import tpu as pltpu
from jax.sharding import PartitionSpec as P

D = 320
HEADS = 5
HEAD_DIM = 64
PAIR = 2 * HEAD_DIM
WIDE = HEADS * PAIR
FF = 1280
NS_STEPS = 5
STEP = 10
CLIP_TOK = 3200
SHARE = 320

POLY_ONE = 3.4445
POLY_TWO = -4.775
POLY_THREE = 2.0315
LOG2E = math.log2(math.e)
SCORE_SCALE = HEAD_DIM**-0.5
MASKED = -1e30
MESH = pl.DeviceIdType.MESH
BF = jnp.bfloat16
F32 = jnp.float32
NT = (((1,), (1,)), ((), ()))
VMEM_SPEC = pl.BlockSpec(memory_space=pltpu.VMEM)


def dot_nt(left, right):
    return lax.dot_general(left, right, NT, preferred_element_type=F32)


def dot_nn(left, right):
    return jnp.dot(left, right, preferred_element_type=F32)


def lanes_of(rows):
    return lax.broadcasted_iota(jnp.int32, (rows, PAIR), 1)


CELL_AT = np.stack([np.arange(400) // 20, np.arange(400) % 20], axis=1).astype(np.float32)


def select_lanes(upper):
    row = lax.broadcasted_iota(jnp.int32, (D, WIDE), 0)
    col = lax.broadcasted_iota(jnp.int32, (D, WIDE), 1)
    source = lax.shift_left(lax.shift_right_logical(col, 7), 6) + (col & (HEAD_DIM - 1))
    half = col & HEAD_DIM
    return (source == row) & (half == (HEAD_DIM if upper else 0))


def flatten_frame(read_row, dst, base):
    for row in range(20):
        dst[base + 20 * row : base + 20 * row + 20, :] = read_row(row).astype(F32)


def build_slabs(center, edged, slot, flat, cells):
    blank = jnp.zeros((20, D), F32)
    edged[1, slot, 0:20, :] = blank
    edged[1, slot, 420:440, :] = blank
    edged[1, slot, 20:420, :] = flat
    center[1, slot] = flat
    col = cells[:, 1:2]
    for e, keep in ((0, col > 0.5), (2, col < 18.5)):
        moved = jnp.where(keep, edged[1, slot, 19 + e : 419 + e, :], 0.0)
        center[e, slot] = moved
        edged[e, slot, 0:20, :] = blank
        edged[e, slot, 420:440, :] = blank
        edged[e, slot, 20:420, :] = moved


def slab(center, edged, slot, b, e, start, size):
    if b == 1:
        return center[e, slot, pl.ds(start, size), :]
    return edged[e, slot, pl.ds(start + 20 * b, size), :]


def inside_of(side_ref, cells):
    side = side_ref[0].astype(F32) - 0.5
    return (cells[:, 0:1] < side) & (cells[:, 1:2] < side)


def norm_parts(rows):
    average = jnp.sum(rows, axis=-1, keepdims=True) * (1.0 / D)
    centered = rows - average
    variance = jnp.sum(centered * centered, axis=-1, keepdims=True) * (1.0 / D)
    scale = lax.rsqrt(variance + 1e-05)
    return centered * scale, scale


def frame_peers():
    f = lax.axis_index("frame")
    near = f + 1 - 2 * lax.rem(f, 2)
    across = lax.rem(f + 2, 4)
    return f, near, across, lax.rem(near + 2, 4)


def share_rows(rows, clips):
    return 16 * (-(-rows // (16 * clips)))


def greet_all(clips):
    barrier = pltpu.get_barrier_semaphore()
    for peer in frame_peers()[1:]:
        pl.semaphore_signal(barrier, inc=1, device_id={"frame": peer}, device_id_type=MESH)
    c = lax.axis_index("clip")

    def greet(step, carry):
        pl.semaphore_signal(
            barrier, inc=1, device_id={"clip": lax.rem(c + step, clips)}, device_id_type=MESH
        )
        return carry

    lax.fori_loop(1, clips, greet, 0)


def await_greetings(count):
    pl.semaphore_wait(pltpu.get_barrier_semaphore(), count)


def send(src, dst, send_sem, recv_sem, peer):
    return pltpu.make_async_remote_copy(
        src_ref=src,
        dst_ref=dst,
        send_sem=send_sem,
        recv_sem=recv_sem,
        device_id={"frame": peer},
        device_id_type=MESH,
    )


def halo_copies(first, last, halo, sems):
    f = lax.axis_index("frame")
    down = send(first, halo.at[1], sems.at[0, 0], sems.at[1, 0], jnp.maximum(f - 1, 0))
    up = send(last, halo.at[0], sems.at[0, 1], sems.at[1, 1], jnp.minimum(f + 1, 3))
    return down, up


def start_halos(down, up, halo):
    f = lax.axis_index("frame")

    @pl.when(f > 0)
    def _():
        down.start()

    @pl.when(f < 3)
    def _():
        up.start()

    @pl.when(f == 0)
    def _():
        halo[0] = jnp.zeros(halo.shape[1:], halo.dtype)

    @pl.when(f == 3)
    def _():
        halo[1] = jnp.zeros(halo.shape[1:], halo.dtype)


def wait_halos(down, up):
    f = lax.axis_index("frame")

    @pl.when(f > 0)
    def _():
        down.wait_send()
        up.wait_recv()

    @pl.when(f < 3)
    def _():
        up.wait_send()
        down.wait_recv()


EXP_SCALE = SCORE_SCALE * LOG2E


def tail_lanes(inside, copies):
    lane = lax.broadcasted_iota(jnp.int32, (inside.shape[0], PAIR), 1)
    tail = jnp.where(
        lane == HEAD_DIM,
        jnp.where(inside, 0.0, MASKED),
        jnp.where((lane > HEAD_DIM) & (lane < HEAD_DIM + 4), 1.0, 0.0),
    )
    return jnp.concatenate([tail] * copies, axis=0).astype(BF)


def front_kernel(
    clips,
    x_ref,
    side_ref,
    cells_ref,
    qkv_ref,
    proj_ref,
    up_ref,
    down_ref,
    vec_ref,
    taps_ref,
    tok_out,
    nhome_out,
    ncross_out,
    q_out,
    home_out,
    cross_out,
    kept_out,
    att_out,
    wq_out,
    wkv_out,
    others_out,
    tok_ref,
    nhome_ref,
    ncross_ref,
    q_ref,
    home_ref,
    cross_ref,
    kept_ref,
    att_ref,
    wq_ref,
    wkv_ref,
    others_ref,
    halo_ref,
    edge,
    raw,
    center,
    edged,
    qkv_full,
    tail,
    halo_sems,
    qkv_sems,
    other_sems,
    spread_sems,
    near_sems,
    cross_sems,
    out_sems,
):
    leaving = []

    def leave(src, dst):
        copy = pltpu.make_async_copy(src, dst, out_sems.at[len(leaving)])
        copy.start()
        leaving.append(copy)

    f, near, across, far = frame_peers()
    c = lax.axis_index("clip")
    greet_all(clips)
    part_rows = qkv_ref.shape[1]

    def qkv_rows(owner):
        return qkv_full.at[pl.ds(pl.multiple_of(owner * part_rows, 16), part_rows), :]

    qkv_full[pl.ds(pl.multiple_of(f * part_rows, 16), part_rows), :] = qkv_ref[...].T.astype(BF)
    start = 0
    for shard in (proj_ref, up_ref, down_ref):
        size = shard.shape[0]
        others_ref[f, start : start + size, :] = shard[...].astype(BF)
        start += size
    spare = others_ref.shape[1] - start
    if spare:
        others_ref[f, start : start + spare, :] = jnp.zeros((spare, D), BF)
    cells = cells_ref[...]
    inside = inside_of(side_ref, cells)
    for t in range(2):
        flatten_frame(lambda row, t=t: x_ref[0, row, :, t, :], raw, 400 * t)
        edge[t] = raw[400 * t : 400 * t + 400, :].astype(BF)

    await_greetings(3 + clips - 1)
    down, up = halo_copies(edge.at[0], edge.at[1], halo_ref, halo_sems)
    start_halos(down, up, halo_ref)
    qkv_cross = send(qkv_rows(f), qkv_rows(f), qkv_sems.at[0, 1], qkv_sems.at[1, 1], across)
    qkv_near = send(qkv_rows(f), qkv_rows(f), qkv_sems.at[0, 0], qkv_sems.at[1, 0], near)
    qkv_relay = send(
        qkv_rows(across), qkv_rows(across), qkv_sems.at[0, 2], qkv_sems.at[1, 2], near
    )
    qkv_near.start()

    part = others_ref.shape[1] // clips

    def part_of(owner, clip):
        return others_ref.at[owner, pl.ds(pl.multiple_of(clip * part, 16), part), :]

    other_near = send(
        others_ref.at[f], others_ref.at[f], other_sems.at[0, 0], other_sems.at[1, 0], near
    )
    other_cross = send(
        part_of(f, c), part_of(f, c), other_sems.at[0, 1], other_sems.at[1, 1], across
    )
    other_relay = send(
        others_ref.at[across],
        others_ref.at[across],
        other_sems.at[0, 2],
        other_sems.at[1, 2],
        near,
    )

    def spread(clip, landing):
        return pltpu.make_async_remote_copy(
            src_ref=part_of(across, c),
            dst_ref=part_of(across, landing),
            send_sem=spread_sems.at[0, clip],
            recv_sem=spread_sems.at[1, landing],
            device_id={"clip": clip},
            device_id_type=MESH,
        )

    def other_clips(act):
        def body(step, carry):
            act(lax.rem(c + step, clips))
            return carry

        lax.fori_loop(1, clips, body, 0)

    other_near.start()

    for t in range(2):
        build_slabs(
            center, edged, t + 1, jnp.where(inside, raw[400 * t : 400 * t + 400, :], 0.0), cells
        )

    def conv_part(t, depths, start, total):
        for a in depths:
            for b in range(3):
                for e in range(3):
                    offset = 9 * a + 3 * b + e
                    total = total + taps_ref[offset : offset + 1, :] * slab(
                        center, edged, t + a, b, e, start, 40
                    )
        return total

    for t, depths in ((0, (1, 2)), (1, (0, 1))):

        def own_part(step, carry, t=t, depths=depths):
            start = pl.multiple_of(step * 40, 8)
            at = pl.ds(pl.multiple_of(start + 400 * t, 8), 40)
            tok_ref[at, :] = conv_part(t, depths, start, raw[at, :] + vec_ref[4:5, :])
            return carry

        lax.fori_loop(0, 10, own_part, 0)
        if t == 0:
            qkv_cross.start()
            other_cross.start()
    wait_halos(down, up)
    for side, slot in ((0, 0), (1, 3)):
        rim = halo_ref[side].astype(F32)
        build_slabs(center, edged, slot, jnp.where(inside, rim, 0.0), cells)
    rows = tok_ref.shape[0]
    piece = rows // HEADS

    def cross_copy(k):
        at = pl.ds(pl.multiple_of(k * piece, 16), piece)
        return send(
            nhome_ref.at[at, :],
            ncross_ref.at[at, :],
            cross_sems.at[0, 0, k],
            cross_sems.at[1, 0, k],
            across,
        )

    def relay_copy(k):
        return send(
            ncross_ref.at[pl.ds(pl.multiple_of(k * piece, 16), piece), :],
            ncross_ref.at[pl.ds(pl.multiple_of(rows + k * piece, 16), piece), :],
            cross_sems.at[0, 1, k],
            cross_sems.at[1, 1, k],
            near,
        )

    near_copy = send(
        nhome_ref.at[pl.ds(0, rows), :],
        nhome_ref.at[pl.ds(rows, rows), :],
        near_sems.at[0],
        near_sems.at[1],
        near,
    )
    for t, depths, ready in ((0, (0,), (0, 1)), (1, (2,), (2,))):

        def rim_part(step, carry, t=t, depths=depths):
            start = pl.multiple_of(step * 40, 8)
            at = pl.ds(pl.multiple_of(start + 400 * t, 8), 40)
            rows = conv_part(t, depths, start, tok_ref[at, :])
            tok_ref[at, :] = rows
            raw[at, :] = norm_parts(rows)[0] * vec_ref[0:1, :] + vec_ref[1:2, :]
            return carry

        lax.fori_loop(0, 10, rim_part, 0)
        at = slice(400 * t, 400 * t + 400)
        nhome_ref[at, :] = raw[at, :].astype(BF)
        for k in ready:
            cross_copy(k).start()
    near_copy.start()
    qkv_cross.wait_recv()
    qkv_relay.start()
    other_cross.wait_recv()
    other_clips(lambda clip: spread(clip, c).start())

    blank = jnp.zeros((1, HEAD_DIM), F32)

    def head_bias(row, h):
        return vec_ref[row : row + 1, HEAD_DIM * h : HEAD_DIM * (h + 1)]

    qkv_near.wait_recv()
    qkv_relay.wait_recv()
    for h in range(HEADS):
        wq_ref[PAIR * h : PAIR * h + HEAD_DIM, :] = qkv_full[HEAD_DIM * h : HEAD_DIM * (h + 1), :]
        wq_ref[PAIR * h + HEAD_DIM : PAIR * (h + 1), :] = jnp.zeros((HEAD_DIM, D), BF)
        wkv_ref[PAIR * h : PAIR * h + HEAD_DIM, :] = qkv_full[
            D + HEAD_DIM * h : D + HEAD_DIM * (h + 1), :
        ]
        wkv_ref[PAIR * h + HEAD_DIM : PAIR * (h + 1), :] = qkv_full[
            2 * D + HEAD_DIM * h : 2 * D + HEAD_DIM * (h + 1), :
        ]
    leave(tok_ref, tok_out)
    leave(wq_ref, wq_out)
    leave(wkv_ref, wkv_out)
    wide_query = jnp.concatenate(
        [part for h in range(HEADS) for part in (head_bias(5, h), blank)], axis=1
    )
    wide_pair = jnp.concatenate(
        [part for h in range(HEADS) for part in (blank, head_bias(6, h))], axis=1
    )

    def project(normed, weight, bias, place):
        joined = (dot_nt(normed, weight[...]) + bias).astype(BF)
        for h in range(HEADS):
            place(h, joined[:, PAIR * h : PAIR * (h + 1)])

    def place_query(h, value):
        q_ref[h] = value

    def place_own(h, value):
        home_ref[h, 0:rows, :] = value

    def place_near(h, value):
        home_ref[h, rows : 2 * rows, :] = value

    def place_cross(h, value):
        cross_ref[h] = value

    project(nhome_ref[0:rows, :], wq_ref, wide_query, place_query)
    cross_copy(3).start()
    project(nhome_ref[0:rows, :], wkv_ref, wide_pair, place_own)
    leave(q_ref, q_out)
    tail[...] = tail_lanes(inside, 4)
    tile = rows // 2
    mask_lane = jnp.where(lanes_of(tile) == HEAD_DIM, 1.0, 0.0).astype(BF)

    def tile_pass(t, source, last):
        at = pl.ds(pl.multiple_of(t * tile, 16), tile)
        lane = lanes_of(tile)
        for h in range(HEADS):
            keys = jnp.concatenate([source[h], tail[...]], axis=1)
            score = dot_nt(jnp.concatenate([q_ref[h, at, :], mask_lane], axis=1), keys)
            peak = jnp.max(score, axis=-1, keepdims=True)
            if last:
                kept = kept_ref[h, at, :]
                old_peak = kept[:, 0:1]
                peak = jnp.maximum(peak, old_peak)
            terms = jnp.exp2((score - peak) * EXP_SCALE).astype(BF)
            mixed = dot_nn(terms, keys)
            total = mixed[:, PAIR + HEAD_DIM + 1 : PAIR + HEAD_DIM + 2]
            mixed = mixed[:, 0:PAIR]
            if last:
                fade = jnp.exp2((old_peak - peak) * EXP_SCALE)
                total = total + fade * kept[:, 32:33]
                mixed = (mixed + fade * kept) / total
                log_sum = peak + jnp.log2(total) * (1.0 / EXP_SCALE)
                kept_ref[h, at, :] = jnp.where(lane < HEAD_DIM, log_sum, mixed)
                att_ref[h, at, :] = jnp.where(lane < HEAD_DIM, 0.0, mixed).astype(BF)
            else:
                kept_ref[h, at, :] = jnp.where(
                    lane < 32, peak, jnp.where(lane < HEAD_DIM, total, mixed)
                )

    def pass_on(k):
        cross_copy(k).wait_recv()
        relay_copy(k).start()

    def first_pass(t, carry):
        tile_pass(t, home_ref, False)

        @pl.when(t == 0)
        def _():
            for k in (0, 1, 2):
                pass_on(k)

        return carry

    def second_pass(t, carry):
        tile_pass(t, cross_ref, True)

        @pl.when(t == 0)
        def _():
            other_relay.wait_recv()
            others_leave.start()

        return carry

    near_copy.wait_recv()
    other_near.wait()
    leave(nhome_ref, nhome_out)
    cross_copy(4).start()
    project(nhome_ref[rows : 2 * rows, :], wkv_ref, wide_pair, place_near)
    leave(home_ref, home_out)
    lax.fori_loop(0, 2, first_pass, 0)
    for k in (3, 4):
        pass_on(k)
    other_clips(lambda clip: spread(clip, clip).wait_recv())
    other_relay.start()
    others_leave = pltpu.make_async_copy(others_ref, others_out, out_sems.at[out_sems.shape[0] - 1])
    for k in range(HEADS):
        relay_copy(k).wait_recv()
    leave(ncross_ref, ncross_out)
    project(ncross_ref[...], wkv_ref, wide_pair, place_cross)
    leave(cross_ref, cross_out)
    lax.fori_loop(0, 2, second_pass, 0)
    leave(kept_ref, kept_out)
    leave(att_ref, att_out)
    other_relay.wait_send()
    other_clips(lambda clip: spread(clip, c).wait_send())
    for copy in (other_cross, near_copy, qkv_cross, qkv_near, qkv_relay):
        copy.wait_send()
    for k in range(HEADS):
        cross_copy(k).wait_send()
        relay_copy(k).wait_send()
    others_leave.wait()
    for copy in leaving:
        copy.wait()


def front(clips_in, clip_side, qkv, proj, up, down, vectors, taps, clips, collective_id):
    rows = 800
    other_rows = clips * share_rows(proj.shape[0] + up.shape[0] + down.shape[0], clips)
    outs = (
        ((rows, D), F32),
        ((2 * rows, D), BF),
        ((2 * rows, D), BF),
        ((HEADS, rows, PAIR), BF),
        ((HEADS, 2 * rows, PAIR), BF),
        ((HEADS, 2 * rows, PAIR), BF),
        ((HEADS, rows, PAIR), F32),
        ((HEADS, rows, PAIR), BF),
        ((WIDE, D), BF),
        ((WIDE, D), BF),
        ((4, other_rows, D), BF),
    )
    return pl.pallas_call(
        functools.partial(front_kernel, clips),
        in_specs=[VMEM_SPEC, pl.BlockSpec(memory_space=pltpu.SMEM)] + [VMEM_SPEC] * 7,
        out_specs=[pl.BlockSpec(memory_space=pl.ANY)] * len(outs),
        out_shape=[jax.ShapeDtypeStruct(*out) for out in outs],
        scratch_shapes=[pltpu.VMEM(*out) for out in outs]
        + [
            pltpu.VMEM((2, 400, D), BF),
            pltpu.VMEM((2, 400, D), BF),
            pltpu.VMEM((rows, D), F32),
            pltpu.VMEM((3, 4, 400, D), F32),
            pltpu.VMEM((3, 4, 440, D), F32),
            pltpu.VMEM((3 * D, D), BF),
            pltpu.VMEM((2 * rows, PAIR), BF),
            pltpu.SemaphoreType.DMA((2, 2)),
            pltpu.SemaphoreType.DMA((2, 3)),
            pltpu.SemaphoreType.DMA((2, 3)),
            pltpu.SemaphoreType.DMA((2, clips)),
            pltpu.SemaphoreType.DMA((2,)),
            pltpu.SemaphoreType.DMA((2, 2, HEADS)),
            pltpu.SemaphoreType.DMA((len(outs),)),
        ],
        compiler_params=pltpu.CompilerParams(
            collective_id=collective_id, has_side_effects=True, vmem_limit_bytes=60 * 2**20
        ),
        cost_estimate=pl.CostEstimate(
            flops=2**34, bytes_accessed=16 * 2**20, transcendentals=2**23
        ),
    )(clips_in, clip_side, jnp.asarray(CELL_AT), qkv, proj, up, down, vectors, taps)


INV_SQRT2 = math.sqrt(0.5)
INV_SQRT_2PI = 1.0 / math.sqrt(2.0 * math.pi)


def dot_tn(left, right):
    return lax.dot_general(left, right, (((0,), (0,)), ((), ())), preferred_element_type=F32)


def norm_back(upstream, unit, scale, gain):
    through = upstream * gain
    mean_one = jnp.sum(through, axis=-1, keepdims=True) * (1.0 / D)
    mean_two = jnp.sum(through * unit, axis=-1, keepdims=True) * (1.0 / D)
    return scale * (through - mean_one - unit * mean_two)


def column_sum(rows):
    return jnp.sum(rows, axis=0, keepdims=True)


def mid_phase(
    att_ref,
    tok_ref,
    og_ref,
    side_ref,
    cells_ref,
    vec_ref,
    ubias_ref,
    others_ref,
    out_ref,
    gsec_ref,
    dout_ref,
    grads_ref,
    vsum_ref,
    raw,
    first_out,
    wide,
    act,
    ghid,
    normed,
    top,
    branch_low,
    att_low,
    proj_ref,
    up_ref,
    down_ref,
):
    start = 0
    for full in (proj_ref, up_ref, down_ref):
        size = full.shape[0] // 4
        for owner in range(4):
            full[size * owner : size * (owner + 1), :] = others_ref[owner, start : start + size, :]
        start += size
    up_bias = jnp.concatenate([ubias_ref[r : r + 1, :] for r in range(FF // 128)], axis=1)
    inside = inside_of(side_ref, cells_ref[...])
    pick = select_lanes(True).astype(F32).astype(BF)
    wide[...] = dot_nn(proj_ref[...], pick).astype(BF)
    vsum_ref[...] = jnp.zeros(vsum_ref.shape, F32)
    for t in range(2):
        at = slice(400 * t, 400 * t + 400)
        heads = jnp.concatenate([att_ref[h, at, :] for h in range(HEADS)], axis=1)
        att_low[at, :] = dot_nt(heads, pick).astype(BF)
        second = tok_ref[at, :] + (dot_nt(heads, wide[...]) + vec_ref[7:8, :])
        unit, scale = norm_parts(second)
        normed_two = (unit * vec_ref[2:3, :] + vec_ref[3:4, :]).astype(BF)
        normed[at, :] = normed_two
        flatten_frame(lambda row, t=t: og_ref[0, row, :, t, :], raw, 0)
        grad_top = jnp.where(inside, raw[...], 0.0)
        top_low = grad_top.astype(BF)
        top[at, :] = top_low
        hidden = dot_nt(normed_two, up_ref[...]) + up_bias
        half = 0.5 + 0.5 * lax.erf(hidden * INV_SQRT2)
        activated = (hidden * half).astype(BF)
        act[at, :] = activated
        slope = half + hidden * (INV_SQRT_2PI * jnp.exp(-0.5 * hidden * hidden))
        grad_hidden = (dot_nt(top_low, down_ref[...]) * slope).astype(BF)
        ghid[at, :] = grad_hidden
        result = second + (dot_nn(activated, down_ref[...]) + vec_ref[8:9, :])
        if t == 0:
            first_out[...] = result
        else:
            raw[...] = result
            for row in range(20):
                part = slice(20 * row, 20 * row + 20)
                out_ref[0, row] = jnp.stack([first_out[part, :], raw[part, :]], axis=1).astype(BF)
        upstream = dot_nn(grad_hidden, up_ref[...])
        grad_second = grad_top + norm_back(upstream, unit, scale, vec_ref[2:3, :])
        gsec_ref[at, :] = grad_second
        low = grad_second.astype(BF)
        branch_low[at, :] = low
        dout = dot_nn(low, wide[...]).astype(BF)
        for h in range(HEADS):
            dout_ref[h, at, :] = dout[:, PAIR * h : PAIR * (h + 1)]
        vsum_ref[0:1, :] += column_sum(upstream * unit)
        vsum_ref[1:2, :] += column_sum(upstream)
        vsum_ref[2:3, :] += column_sum(low.astype(F32))
        vsum_ref[3:4, :] += column_sum(grad_top)
        bias_sum = column_sum(grad_hidden.astype(F32))
        for part in range(4):
            vsum_ref[4 + part : 5 + part, :] += bias_sum[:, D * part : D * (part + 1)]
    rows = up_ref.shape[0] // 4
    proj_rows = D // 4
    grad = dot_tn(branch_low[...], att_low[...]).astype(BF)
    for owner in range(4):
        grads_ref[owner, 0:proj_rows, :] = grad[proj_rows * owner : proj_rows * (owner + 1), :]
    for owner in range(4):
        at = slice(rows * owner, rows * (owner + 1))
        start = proj_rows
        grads_ref[owner, start : start + rows, :] = dot_tn(ghid[:, at], normed[...]).astype(BF)
        start = proj_rows + rows
        grads_ref[owner, start : start + rows, :] = dot_tn(act[:, at], top[...]).astype(BF)


class RowSums:
    def __init__(self, clips, g_ref, at, pair_in, cross_out, cross_in, shares, shares_in, sums,
                 frame_sems, part_sems, sum_sems):
        self.clips = clips
        self.g = g_ref
        self.at = at
        self.pair_in = pair_in
        self.cross_out = cross_out
        self.cross_in = cross_in
        self.shares = shares
        self.shares_in = shares_in
        self.sums = sums
        self.part_sems = part_sems
        self.sum_sems = sum_sems
        f, near, across, far = frame_peers()
        self.f, self.across = f, across
        self.c = lax.axis_index("clip")
        sem = frame_sems
        part = lambda owner: g_ref.at[owner, pl.ds(at.start, at.stop - at.start), :]
        self.first = send(part(far), pair_in.at[0], sem.at[0, 0], sem.at[1, 0], near)
        self.second = send(part(near), pair_in.at[1], sem.at[0, 1], sem.at[1, 1], near)
        self.cross = send(cross_out, cross_in, sem.at[0, 2], sem.at[1, 2], across)

    def peer(self, step):
        return lax.rem(self.c + step, self.clips)

    def part_copy(self, step):
        return pltpu.make_async_remote_copy(
            src_ref=self.shares.at[self.peer(step)],
            dst_ref=self.shares_in.at[step],
            send_sem=self.part_sems.at[0, step],
            recv_sem=self.part_sems.at[1, step],
            device_id={"clip": self.peer(step)},
            device_id_type=MESH,
        )

    def sum_copy(self, step):
        return pltpu.make_async_remote_copy(
            src_ref=self.sums.at[self.c],
            dst_ref=self.sums.at[self.c],
            send_sem=self.sum_sems.at[0, step],
            recv_sem=self.sum_sems.at[1, step],
            device_id={"clip": self.peer(step)},
            device_id_type=MESH,
        )

    def each(self, act):
        def body(step, carry):
            act(step)
            return carry

        lax.fori_loop(1, self.clips, body, 0)

    def pair_step(self):
        self.first.start()
        self.second.start()

    def cross_step(self):
        self.first.wait()
        self.cross_out[...] = (
            self.g[self.across, self.at, :].astype(F32) + self.pair_in[0].astype(F32)
        ).astype(BF)
        self.cross.start()

    def share_step(self):
        self.second.wait()
        self.cross.wait()
        mine = (
            self.g[self.f, self.at, :].astype(F32)
            + self.pair_in[1].astype(F32)
            + self.cross_in[...].astype(F32)
        ).astype(BF)
        rows, chunk = mine.shape[0], self.shares.shape[1]
        spare = self.clips * chunk - rows
        if spare:
            mine = jnp.concatenate([mine, jnp.zeros((spare, D), BF)], axis=0)
        self.shares[...] = mine.reshape(self.clips, chunk, D)
        self.each(lambda step: self.part_copy(step).start())

    def sum_step(self):
        self.each(lambda step: self.part_copy(step).wait())

        def add_part(step, total):
            return total + self.shares_in[step].astype(F32)

        total = lax.fori_loop(1, self.clips, add_part, self.shares[self.c].astype(F32))
        self.sums[self.c] = total.astype(BF)
        self.each(lambda step: self.sum_copy(step).start())

    def finish(self):
        self.each(lambda step: self.sum_copy(step).wait())


def row_sums_scratch(rows, clips):
    chunk = share_rows(rows, clips)
    return [
        pltpu.VMEM((2, rows, D), BF),
        pltpu.VMEM((rows, D), BF),
        pltpu.VMEM((rows, D), BF),
        pltpu.VMEM((clips, chunk, D), BF),
        pltpu.VMEM((clips, chunk, D), BF),
        pltpu.VMEM((clips, chunk, D), BF),
        pltpu.SemaphoreType.DMA((2, 3)),
        pltpu.SemaphoreType.DMA((2, clips)),
        pltpu.SemaphoreType.DMA((2, clips)),
    ]


EARLY_PARTS = (slice(0, 400), slice(400, 720))


def row_pieces(start, size, block):
    pieces, skip = [], 0
    while skip < size:
        owner, row = divmod(start + skip, block)
        step = min(size - skip, block - row)
        pieces.append((owner, row, skip, step))
        skip += step
    return pieces


def back_phase(
    one,
    two,
    arrived,
    q_ref,
    dout_ref,
    kept_ref,
    cross_ref,
    home_ref,
    nhome_ref,
    ncross_ref,
    wq_ref,
    wkv_ref,
    side_ref,
    cells_ref,
    gnorm_ref,
    own_ref,
    out_ref,
    bsum_ref,
    grads_ref,
    grads_in,
    pair_out,
    pair_in,
    cross_out,
    cross_in,
    pair_sems,
    cross_sems,
    grad_sems,
    extra,
    qd_t,
    tail,
    low_one,
    low_two,
    low_three,
    dq_sum,
    turned_pairs,
    pair_grad,
):
    f, near, across, far = frame_peers()
    rows = q_ref.shape[1]
    dnormed = gnorm_ref
    dq_low = q_ref
    tail[...] = tail_lanes(inside_of(side_ref, cells_ref[...]), 4)
    arrived(0, 3)
    lower = lax.broadcasted_iota(jnp.int32, (PAIR, 1), 0) < HEAD_DIM
    scale_of = jnp.where(lower, SCORE_SCALE, 1.0)
    chunks = ((0, 512, low_one), (512, 512, low_two), (1024, 576, low_three))

    def minus_parts(column, lane):
        high = column.astype(BF).astype(F32)
        mid = (column - high).astype(BF).astype(F32)
        rest = column - high - mid
        return jnp.where(
            lane == HEAD_DIM + 1,
            -high,
            jnp.where(lane == HEAD_DIM + 2, -mid, jnp.where(lane == HEAD_DIM + 3, -rest, 0.0)),
        )

    def prepare(h):
        lane = lanes_of(rows)
        kept = kept_ref[h]
        queries, douts = q_ref[h].astype(F32), dout_ref[h].astype(F32)
        log_sum = kept[:, 0:1]
        row_dot = jnp.sum(douts * kept, axis=-1, keepdims=True)
        of_queries = jnp.where(lane == HEAD_DIM, 1.0, minus_parts(log_sum, lane))
        extra[h, 0:rows, :] = of_queries.astype(BF)
        extra[h, rows : 2 * rows, :] = minus_parts(row_dot, lane).astype(BF)
        qd_t[h] = jnp.concatenate([queries, douts], axis=0).T.astype(BF)
        bsum_ref[1, h] = column_sum(douts)

    def head_pass(h, source, add):
        pairs = source[h]
        both = jnp.concatenate([q_ref[h], dout_ref[h]], axis=0)
        both = jnp.concatenate([both, extra[h]], axis=1)
        products = [
            dot_nt(
                both,
                jnp.concatenate(
                    [pairs[start : start + size, :], tail[start : start + size, :]], axis=1
                ),
            )
            for start, size, low in chunks
        ]
        total = dq_sum[h] if add else None
        at = pl.ds(pl.multiple_of(h * PAIR, PAIR), PAIR)
        for (start, size, low), product in zip(chunks, products):
            probs = jnp.exp2(product[0:rows, :] * EXP_SCALE)
            low[0:rows, :] = (probs * product[rows : 2 * rows, :]).astype(BF)
            low[rows : 2 * rows, :] = probs.astype(BF)
            part = dot_nn(low[0:rows, :], pairs[start : start + size, :])
            total = part if total is None else total + part
            turned = dot_nn(qd_t[h], low[...]) * scale_of
            turned_pairs[at, start : start + size] = turned.astype(BF)
        if add:
            total = jnp.where(lanes_of(rows) < HEAD_DIM, total * SCORE_SCALE, 0.0)
            dq_low[h] = total.astype(BF)
            bsum_ref[0, h] = column_sum(total)
        else:
            dq_sum[h] = total

    def of_normed(normed, add):
        grad = dot_nn(turned_pairs[...], normed[...])
        pair_grad[...] = pair_grad[...] + grad if add else grad
        total = dot_nn(wkv_ref[...].astype(F32).T.astype(BF), turned_pairs[...]).T
        dnormed[...] = total[0:rows, :]
        pair_out[...] = total[rows : 2 * rows, :].astype(BF)

    def pair_copy(phase):
        return send(
            pair_out, pair_in.at[phase], pair_sems.at[0, phase], pair_sems.at[1, phase], near
        )

    to_across = send(cross_out, cross_in, cross_sems.at[0], cross_sems.at[1], across)

    def cross_pass(h, carry):
        prepare(h)
        head_pass(h, cross_ref, False)

        @pl.when(h == 0)
        def _():
            one.cross_step()

        @pl.when(h == 2)
        def _():
            two.cross_step()

        @pl.when(h == 3)
        def _():
            one.share_step()

        return carry

    def home_pass(h, carry):
        head_pass(h, home_ref, True)

        @pl.when(h == 0)
        def _():
            pair_copy(0).wait()
            cross_out[...] = (dnormed[...] + pair_in[0].astype(F32)).astype(BF)
            to_across.start()
            two.share_step()

        @pl.when(h == 1)
        def _():
            one.sum_step()

        @pl.when(h == 3)
        def _():
            two.sum_step()

        return carry

    lax.fori_loop(0, HEADS, cross_pass, 0)
    arrived(3, 8)
    of_normed(ncross_ref, False)
    pair_copy(0).start()
    lax.fori_loop(0, HEADS, home_pass, 0)
    of_normed(nhome_ref, True)
    pair_copy(1).start()

    block = grads_ref.shape[1]

    def place(start, values):
        for owner, row, skip, size in row_pieces(start, values.shape[0], block):
            grads_ref[owner, row : row + size, :] = values[skip : skip + size, :]

    dq = jnp.concatenate([dq_low[h] for h in range(HEADS)], axis=1)
    of_queries = dot_tn(dq, nhome_ref[0:rows, :]).astype(BF)
    for h in range(HEADS):
        of_pairs = pair_grad[PAIR * h : PAIR * (h + 1), :].astype(BF)
        place(HEAD_DIM * h, of_queries[PAIR * h : PAIR * h + HEAD_DIM, :])
        place(D + HEAD_DIM * h, of_pairs[0:HEAD_DIM, :])
        place(2 * D + HEAD_DIM * h, of_pairs[HEAD_DIM:PAIR, :])
    to_pair = [
        send(grads_ref.at[peer], grads_in.at[k], grad_sems.at[0, k], grad_sems.at[1, k], near)
        for k, peer in enumerate((far, near))
    ]
    for copy in to_pair:
        copy.start()
    total = dnormed[...] + dot_nn(dq, wq_ref[...])
    to_across.wait()
    pair_copy(1).wait()
    gnorm_ref[...] = total + pair_in[1].astype(F32) + cross_in[...].astype(F32)
    for copy in to_pair:
        copy.wait()
    out_ref[...] = (grads_ref[across].astype(F32) + grads_in[0].astype(F32)).astype(BF)
    own_ref[...] = grads_ref[f].astype(F32) + grads_in[1].astype(F32)


def newton_schulz(whole):
    wide = whole.astype(F32)
    norm = jnp.sqrt(jnp.sum(wide * wide)) + 1e-07
    eye = (
        lax.broadcasted_iota(jnp.int32, (D, D), 0) == lax.broadcasted_iota(jnp.int32, (D, D), 1)
    ).astype(F32)
    turned = dot_nt(eye.astype(BF), whole) / norm

    def iterate(step, current):
        held = current.astype(BF)
        gram = dot_nt(held, held)
        gram_low = gram.astype(BF)
        poly = POLY_TWO * gram + POLY_THREE * dot_nn(gram_low, gram_low)
        return POLY_ONE * current + dot_nn(poly.astype(BF), held)

    return lax.fori_loop(0, NS_STEPS, iterate, turned)


OWNER_OF = (3, 1, 0, 2)
QKV_AT = OWNER_OF[0]


def tail_phase(
    clips,
    one,
    two,
    arrived,
    copy_out,
    gnorm_ref,
    own_ref,
    across_ref,
    bsum_ref,
    tok_ref,
    gsec_ref,
    x_ref,
    side_ref,
    cells_ref,
    taps_ref,
    vec_ref,
    mid_sums_ref,
    one_ref,
    two_ref,
    qkv_m_ref,
    proj_m_ref,
    up_m_ref,
    down_m_ref,
    late_ref,
    scaled_ref,
    vsum_ref,
    cross_in,
    shares,
    shares_in,
    new_rows,
    new_low,
    first_low,
    rim,
    v_mine,
    v_frames,
    v_total,
    v_clips,
    gathered,
    old_rows,
    center,
    edged,
    low,
    grad_sems,
    part_sems,
    row_sems,
    spread_sems,
    rim_sems,
    vf_sems,
    vc_sems,
    there_sems,
    back_sems,
):
    first, ingrad_ref, outer = gnorm_ref, gsec_ref, tok_ref
    f, near, across, far = frame_peers()
    c = lax.axis_index("clip")
    block = own_ref.shape[0]
    owners, chunk = shares.shape[0], shares.shape[1]

    def each(count, act):
        def body(step, carry):
            act(step)
            return carry

        lax.fori_loop(0, count, body, 0)

    def other_clips(act):
        each(clips - 1, lambda step: act(lax.rem(c + 1 + step, clips)))

    down, up = halo_copies(first_low.at[0], first_low.at[1], rim, rim_sems)

    to_across = send(across_ref, cross_in, grad_sems.at[0], grad_sems.at[1], across)
    to_across.start()

    upstream = gnorm_ref[...]
    unit, scale = norm_parts(tok_ref[...])
    grad_first = gsec_ref[...] + norm_back(upstream, unit, scale, vec_ref[0:1, :])
    first[...] = grad_first
    first_low[...] = grad_first.astype(BF).reshape(first_low.shape)
    one.finish()
    two.finish()
    one_ref[...] = one.sums[...].reshape(one_ref.shape)
    two_ref[...] = two.sums[...].reshape(two_ref.shape)
    arrived(0, 5)
    old_rows[0:block, :] = qkv_m_ref[...].T
    if owners * chunk > block:
        old_rows[block : owners * chunk, :] = jnp.zeros((owners * chunk - block, D), F32)

    v_mine[0:1, :] = column_sum(upstream * unit)
    v_mine[1:2, :] = column_sum(upstream)
    v_mine[2:4, :] = mid_sums_ref[0:2, :]
    v_mine[4:5, :] = column_sum(grad_first)
    v_mine[5:6, :] = jnp.concatenate(
        [bsum_ref[0, h, :, 0:HEAD_DIM] for h in range(HEADS)], axis=1
    )
    v_mine[6:7, :] = jnp.concatenate(
        [bsum_ref[1, h, :, HEAD_DIM:PAIR] for h in range(HEADS)], axis=1
    )
    v_mine[7:9, :] = mid_sums_ref[2:4, :]
    v_mine[9:13, :] = mid_sums_ref[4:8, :]

    cells = cells_ref[...]
    inside = inside_of(side_ref, cells)
    for t in range(2):
        build_slabs(center, edged, t + 1, first[400 * t : 400 * t + 400, :], cells)

    def part_copy(owner):
        return pltpu.make_async_remote_copy(
            src_ref=shares.at[owner],
            dst_ref=shares_in.at[c],
            send_sem=part_sems.at[0, owner],
            recv_sem=part_sems.at[1, c],
            device_id={"clip": owner},
            device_id_type=MESH,
        )

    def other_owners(act):
        def step(owner):
            @pl.when(owner != c)
            def _():
                act(owner)

        each(owners, step)

    to_across.wait()
    mine = (own_ref[...] + cross_in[...].astype(F32)).astype(BF)
    if owners * chunk > block:
        mine = jnp.concatenate([mine, jnp.zeros((owners * chunk - block, D), BF)], axis=0)
    shares[...] = mine.reshape(owners, chunk, D)
    other_owners(lambda owner: part_copy(owner).start())
    start_halos(down, up, rim)

    def row_copy(clip):
        return pltpu.make_async_remote_copy(
            src_ref=new_rows.at[c],
            dst_ref=new_rows.at[c],
            send_sem=row_sems.at[0, clip],
            recv_sem=row_sems.at[1, c],
            device_id={"clip": clip},
            device_id_type=MESH,
        )

    def spread_copy(clip):
        return pltpu.make_async_remote_copy(
            src_ref=new_low,
            dst_ref=gathered.at[f, pl.ds(pl.multiple_of(c * chunk, 16), chunk), :],
            send_sem=spread_sems.at[4, clip],
            recv_sem=spread_sems.at[f, c],
            device_id={"clip": clip, "frame": QKV_AT},
            device_id_type=MESH,
        )

    def share_sum():
        @pl.when(c < owners)
        def _():
            shares_in[c] = shares[c]

            def arrive(clip):
                pltpu.make_async_remote_copy(
                    src_ref=shares.at[0],
                    dst_ref=shares_in.at[clip],
                    send_sem=part_sems.at[0, 0],
                    recv_sem=part_sems.at[1, clip],
                    device_id={"clip": clip},
                    device_id_type=MESH,
                ).wait_recv()

            other_clips(arrive)

            def add_part(clip, total):
                return total + shares_in[clip].astype(F32)

            total = lax.fori_loop(0, clips, add_part, jnp.zeros((chunk, D), F32))
            at = pl.ds(pl.multiple_of(c * chunk, 16), chunk)
            fresh = 0.95 * old_rows[at, :] + total
            new_rows[c] = fresh
            new_low[...] = fresh.astype(BF)
            other_clips(lambda clip: spread_copy(clip).start())

            @pl.when(f != QKV_AT)
            def _():
                spread_copy(c).start()

            @pl.when(f == QKV_AT)
            def _():
                gathered[QKV_AT, at, :] = new_low[...]

            other_clips(lambda clip: row_copy(clip).start())

    for t in range(2):
        at = slice(400 * t, 400 * t + 400)
        flatten_frame(lambda row, t=t: x_ref[0, row, :, t, :], outer, 400 * t)
        outer[at, :] = jnp.where(inside, outer[at, :], 0.0)

    def plane(t, a, add_rows, add_taps):
        def step(number, totals):
            start = pl.multiple_of(number * 16, 16)
            at = pl.ds(pl.multiple_of(start + 400 * t, 16), 16)
            masked = outer[at, :]
            total = jnp.zeros((16, D), F32)
            sums_out = []
            for b in range(3):
                for e in range(3):
                    offset = 9 * a + 3 * b + e
                    piece = slab(center, edged, t + 2 - a, 2 - b, 2 - e, start, 16)
                    total = total + taps_ref[offset : offset + 1, :] * piece
                    product = masked * piece
                    sums_out.append(totals[3 * b + e] + (product[0:8, :] + product[8:16, :]))
            if add_rows:
                ingrad_ref[at, :] += total
            else:
                ingrad_ref[at, :] = total
            return tuple(sums_out)

        totals = lax.fori_loop(0, 25, step, tuple(jnp.zeros((8, D), F32) for _ in range(9)))
        for which, total in enumerate(totals):
            at = slice(13 + 9 * a + which, 14 + 9 * a + which)
            if add_taps:
                v_mine[at, :] += column_sum(total)
            else:
                v_mine[at, :] = column_sum(total)

    plane(0, 0, False, False)

    moments = (None, proj_m_ref, up_m_ref, down_m_ref)

    def to_owner(which):
        at = pl.ds(0, moments[which].shape[0])
        return send(
            low.at[which, at, :],
            gathered.at[f, at, :],
            there_sems.at[0, which],
            there_sems.at[1, f],
            OWNER_OF[which],
        )

    for which in (3, 2, 1):
        rows = moments[which].shape[0]
        summed = one_ref[80:400, :] if which == 2 else (two_ref if which == 3 else one_ref)[0:rows, :]
        low[which, 0:rows, :] = (0.95 * moments[which][...] + summed.astype(F32)).astype(BF)

        @pl.when(f != OWNER_OF[which])
        def _(which=which):
            to_owner(which).start()

    plane(0, 1, True, False)
    share_sum()
    plane(1, 1, False, True)
    plane(1, 2, True, False)
    wait_halos(down, up)
    for side, slot in ((0, 0), (1, 3)):
        build_slabs(center, edged, slot, rim[side].astype(F32), cells)
    plane(0, 2, True, True)
    plane(1, 0, True, True)
    for t in range(2):
        at = slice(400 * t, 400 * t + 400)
        ingrad_ref[at, :] = first[at, :] + jnp.where(inside, ingrad_ref[at, :], 0.0)
    copy_out()

    v_copies = []
    for which, peer in enumerate((near, across, far)):
        copy = send(v_mine, v_frames.at[f], vf_sems.at[0, which], vf_sems.at[1, which], peer)
        copy.start()
        v_copies.append(copy)
    v_frames[f] = v_mine[...]

    @pl.when(f == QKV_AT)
    def _():
        def rows_arrive(frame, clip):
            pltpu.make_async_remote_copy(
                src_ref=new_low,
                dst_ref=gathered.at[frame, pl.ds(pl.multiple_of(clip * chunk, 16), chunk), :],
                send_sem=spread_sems.at[4, clip],
                recv_sem=spread_sems.at[frame, clip],
                device_id={"clip": clip, "frame": frame},
                device_id_type=MESH,
            ).wait_recv()

        other_owners(lambda clip: rows_arrive(QKV_AT, clip))
        for step in (1, 2, 3):
            frame = (QKV_AT + step) % 4
            each(owners, lambda clip, frame=frame: rows_arrive(frame, clip))

    for which in (1, 2, 3):

        @pl.when(f != OWNER_OF[which])
        def _(which=which):
            to_owner(which).wait_send()

        @pl.when(f == OWNER_OF[which])
        def _(which=which):
            at = pl.ds(0, moments[which].shape[0])
            gathered[OWNER_OF[which], at, :] = low[which, at, :]
            for other in range(4):
                if other != OWNER_OF[which]:
                    send(
                        low.at[0, at, :],
                        gathered.at[other, at, :],
                        there_sems.at[0, 0],
                        there_sems.at[1, other],
                        other,
                    ).wait_recv()

    turned = newton_schulz(gathered[...].reshape(4 * SHARE, D))
    low[:, 0:SHARE, :] = turned.T.astype(BF).reshape(4, SHARE, D)
    row_counts = (block, *(ref.shape[0] for ref in moments[1:]))

    def back_copy(which, step):
        at = pl.ds(0, row_counts[which])
        to = (OWNER_OF[which] + step) % 4
        return send(
            low.at[to, at, :],
            scaled_ref.at[which, at, :],
            back_sems.at[0, step],
            back_sems.at[1, which],
            to,
        )

    for which in range(4):

        @pl.when(f == OWNER_OF[which])
        def _(which=which):
            for step in (2, 1, 3):
                back_copy(which, step).start()
            at = pl.ds(0, row_counts[which])
            scaled_ref[which, at, :] = low[OWNER_OF[which], at, :]

    for copy in v_copies:
        copy.wait()
    v_total[...] = v_frames[0] + v_frames[1] + v_frames[2] + v_frames[3]

    def v_copy(clip):
        return pltpu.make_async_remote_copy(
            src_ref=v_total,
            dst_ref=v_clips.at[c],
            send_sem=vc_sems.at[0, clip],
            recv_sem=vc_sems.at[1, c],
            device_id={"clip": clip},
            device_id_type=MESH,
        )

    other_clips(lambda clip: v_copy(clip).start())
    v_clips[c] = v_total[...]

    other_owners(lambda owner: part_copy(owner).wait_send())

    @pl.when(c < owners)
    def _():
        other_clips(lambda clip: spread_copy(clip).wait_send())

        @pl.when(f != QKV_AT)
        def _():
            spread_copy(c).wait_send()

        other_clips(lambda clip: row_copy(clip).wait_send())

    def new_rows_arrive(clip):
        pltpu.make_async_remote_copy(
            src_ref=new_rows.at[0],
            dst_ref=new_rows.at[clip],
            send_sem=row_sems.at[0, 0],
            recv_sem=row_sems.at[1, clip],
            device_id={"clip": clip},
            device_id_type=MESH,
        ).wait_recv()

    other_owners(new_rows_arrive)
    late_ref[...] = new_rows[...].reshape(late_ref.shape)

    def v_arrives(clip):
        v_copy(clip).wait_send()
        pltpu.make_async_remote_copy(
            src_ref=v_total,
            dst_ref=v_clips.at[clip],
            send_sem=vc_sems.at[0, clip],
            recv_sem=vc_sems.at[1, clip],
            device_id={"clip": clip},
            device_id_type=MESH,
        ).wait_recv()

    other_clips(v_arrives)

    def add_v(step, total):
        return total + v_clips[step]

    vsum_ref[...] = lax.fori_loop(0, clips, add_v, jnp.zeros(vsum_ref.shape, F32))
    for which in range(4):

        @pl.when(f == OWNER_OF[which])
        def _(which=which):
            for step in (2, 1, 3):
                back_copy(which, step).wait_send()

        @pl.when(f != OWNER_OF[which])
        def _(which=which):
            back_copy(which, 1).wait_recv()


def rest_kernel(
    clips,
    att_in,
    tok_in,
    og_in,
    others_in,
    side_ref,
    cells_ref,
    vec_ref,
    ubias_ref,
    taps_ref,
    *refs,
):
    refs = list(refs)

    def take(count):
        taken, refs[:count] = refs[:count], []
        return taken

    back_sources = take(8)
    tail_sources = take(5)
    block_out, ingrad_out, one_ref, two_ref, late_ref, scaled_ref, vsum_ref = take(7)
    tok, out, gsec, dout, early, mid_sums = take(6)
    back_inputs = take(8)
    gnorm, own, across_rows, bsum = take(4)
    back_buffers = take(6)
    back_sems = take(3)
    tail_landing = take(12)
    tail_sems = take(9)
    (copy_sems,) = take(1)
    half = len(refs) // 2
    f, near, across, far = frame_peers()
    c = lax.axis_index("clip")
    gathered = tail_landing[-1]
    block, proj_rows = own.shape[0], D // 4
    chunk = share_rows(block, clips)
    owned = -(-block // chunk) * chunk

    @pl.when(f == QKV_AT)
    def _():
        gathered[:, owned:SHARE, :] = jnp.zeros((4, SHARE - owned, D), BF)

    @pl.when(f == OWNER_OF[1])
    def _():
        gathered[:, proj_rows:SHARE, :] = jnp.zeros((4, SHARE - proj_rows, D), BF)

    greet_all(clips)
    barrier = pltpu.get_barrier_semaphore()

    def greet(frame):
        def body(step, carry):
            pl.semaphore_signal(
                barrier,
                inc=1,
                device_id={"clip": lax.rem(c + step, clips), "frame": frame},
                device_id_type=MESH,
            )
            return carry

        lax.fori_loop(1, clips, body, 0)

    @pl.when(f == QKV_AT)
    def _():
        for step in (1, 2, 3):
            greet((QKV_AT + step) % 4)

    @pl.when(f != QKV_AT)
    def _():
        greet(QKV_AT)

    def copies(sources, targets, first):
        return [
            pltpu.make_async_copy(src, dst, copy_sems.at[first + k])
            for k, (src, dst) in enumerate(zip(sources, targets))
        ]

    def arrival(waiting):
        def arrived(start, stop):
            for copy in waiting[start:stop]:
                copy.wait()

        return arrived

    for_back = copies(back_sources, back_inputs, 4)

    def middle(att, og, others, *scratch):
        for_mid = copies((others_in, att_in, tok_in, og_in), (others, att, tok, og), 0)
        for copy in for_mid:
            copy.start()
        for copy in for_mid:
            copy.wait()
        for copy in for_back:
            copy.start()
        mid_phase(
            att, tok, og, side_ref, cells_ref, vec_ref, ubias_ref, others, out, gsec, dout, early,
            mid_sums, *scratch,
        )

    rows = tok.shape[0]
    vmem = pltpu.VMEM
    pl.run_scoped(
        middle,
        vmem(att_in.shape, BF),
        vmem(og_in.shape, BF),
        vmem(others_in.shape, BF),
        vmem((400, D), F32),
        vmem((400, D), F32),
        vmem((D, WIDE), BF),
        vmem((rows, FF), BF),
        vmem((rows, FF), BF),
        vmem((rows, D), BF),
        vmem((rows, D), BF),
        vmem((rows, D), BF),
        vmem((rows, D), BF),
        vmem((D, D), BF),
        vmem((FF, D), BF),
        vmem((FF, D), BF),
    )
    out_copy = pltpu.make_async_copy(out, block_out, copy_sems.at[0])
    out_copy.start()

    @pl.when(f == QKV_AT)
    def _():
        await_greetings(3 + 4 * (clips - 1))

    @pl.when(f != QKV_AT)
    def _():
        await_greetings(3 + 2 * (clips - 1))

    one = RowSums(clips, early, EARLY_PARTS[0], *refs[:half])
    two = RowSums(clips, early, EARLY_PARTS[1], *refs[half:])
    one.pair_step()
    two.pair_step()

    def backward(*scratch):
        back_phase(
            one, two, arrival(for_back), back_inputs[0], dout, *back_inputs[1:], side_ref,
            cells_ref, gnorm, own, across_rows, bsum, *back_buffers, *back_sems, *scratch,
        )

    pl.run_scoped(
        backward,
        vmem((HEADS, 2 * rows, PAIR), BF),
        vmem((HEADS, PAIR, 2 * rows), BF),
        vmem((2 * rows, PAIR), BF),
        vmem((2 * rows, 512), BF),
        vmem((2 * rows, 512), BF),
        vmem((2 * rows, 576), BF),
        vmem((HEADS, rows, PAIR), F32),
        vmem((WIDE, 2 * rows), BF),
        vmem((WIDE, D), F32),
    )

    def finish(x, qkv_m, proj_m, up_m, down_m, *scratch):
        for_tail = copies(tail_sources, (x, qkv_m, proj_m, up_m, down_m), 12)
        for copy in for_tail:
            copy.start()
        leave = pltpu.make_async_copy(gsec, ingrad_out, copy_sems.at[1])
        tail_phase(
            clips, one, two, arrival(for_tail), leave.start, gnorm, own, across_rows, bsum, tok,
            gsec, x, side_ref, cells_ref, taps_ref, vec_ref, mid_sums, one_ref, two_ref, qkv_m,
            proj_m, up_m, down_m, late_ref, scaled_ref, vsum_ref, *tail_landing, *scratch, early,
            *tail_sems,
        )
        leave.wait()

    pl.run_scoped(
        finish,
        *(vmem(ref.shape, ref.dtype) for ref in tail_sources),
        vmem((owned, D), F32),
        vmem((3, 4, 400, D), F32),
        vmem((3, 4, 440, D), F32),
    )
    out_copy.wait()


def rest(mid_inputs, small, back_inputs, tail_inputs, clips, collective_id):
    rows, block = 800, 3 * D // 4
    chunk = share_rows(block, clips)
    owners = -(-block // chunk)
    vector_shape = (40, D)
    vmem = pltpu.VMEM
    dma = pltpu.SemaphoreType.DMA
    parts = [part.stop - part.start for part in EARLY_PARTS]
    hbm = pl.BlockSpec(memory_space=pl.ANY)
    return pl.pallas_call(
        functools.partial(rest_kernel, clips),
        in_specs=[hbm] * 4
        + [pl.BlockSpec(memory_space=pltpu.SMEM)]
        + [VMEM_SPEC] * 4
        + [hbm] * (len(back_inputs) + len(tail_inputs)),
        out_specs=[hbm] * 2 + [VMEM_SPEC] * 5,
        out_shape=[
            jax.ShapeDtypeStruct(mid_inputs[2].shape, BF),
            jax.ShapeDtypeStruct((rows, D), F32),
        ]
        + [
            jax.ShapeDtypeStruct((clips * share_rows(part, clips), D), BF) for part in parts
        ]
        + [
            jax.ShapeDtypeStruct((owners * chunk, D), F32),
            jax.ShapeDtypeStruct((4, SHARE, D), BF),
            jax.ShapeDtypeStruct(vector_shape, F32),
        ],
        scratch_shapes=[
            vmem((rows, D), F32),
            vmem(mid_inputs[2].shape, BF),
            vmem((rows, D), F32),
            vmem((HEADS, rows, PAIR), BF),
            vmem((4, (D + 2 * FF) // 4, D), BF),
            vmem((8, D), F32),
        ]
        + [vmem(ref.shape, ref.dtype) for ref in back_inputs]
        + [
            vmem((rows, D), F32),
            vmem((block, D), F32),
            vmem((block, D), BF),
            vmem((2, HEADS, 1, PAIR), F32),
            vmem((4, block, D), BF),
            vmem((2, block, D), BF),
            vmem((rows, D), BF),
            vmem((2, rows, D), BF),
            vmem((rows, D), BF),
            vmem((rows, D), BF),
            dma((2, 2)),
            dma((2,)),
            dma((2, 2)),
            vmem((block, D), BF),
            vmem((owners, chunk, D), BF),
            vmem((clips, chunk, D), BF),
            vmem((owners, chunk, D), F32),
            vmem((chunk, D), BF),
            vmem((2, 400, D), BF),
            vmem((2, 400, D), BF),
            vmem(vector_shape, F32),
            vmem((4,) + vector_shape, F32),
            vmem(vector_shape, F32),
            vmem((clips,) + vector_shape, F32),
            vmem((4, SHARE, D), BF),
            dma((2,)),
            dma((2, clips)),
            dma((2, clips)),
            dma((5, clips)),
            dma((2, 2)),
            dma((2, 3)),
            dma((2, clips)),
            dma((2, 4)),
            dma((2, 4)),
            dma((17,)),
        ]
        + row_sums_scratch(parts[0], clips)
        + row_sums_scratch(parts[1], clips),
        compiler_params=pltpu.CompilerParams(
            collective_id=collective_id, has_side_effects=True, vmem_limit_bytes=63 * 2**20
        ),
        cost_estimate=pl.CostEstimate(
            flops=2**36, bytes_accessed=32 * 2**20, transcendentals=2**25
        ),
    )(*mid_inputs, *small, *back_inputs, *tail_inputs)


def adamw(param, mean_old, square_old, gradient, rate_value, decay):
    mean_new = 0.9 * mean_old + 0.1 * gradient
    square_new = 0.999 * square_old + 0.001 * gradient * gradient
    mean_hat = mean_new / (1.0 - 0.9**STEP)
    square_hat = square_new / (1.0 - 0.999**STEP)
    return (
        mean_new,
        square_new,
        param - rate_value * (mean_hat / (jnp.sqrt(square_hat) + 1e-08) + decay * param),
    )


RATES = (0.2 * math.sqrt(3.0), 0.12 * math.sqrt(CLIP_TOK), 0.2 * math.sqrt(FF / D), 0.2)


def update_kernel(*refs):
    refs = list(refs)

    def take(count):
        taken, refs[:count] = refs[:count], []
        return taken

    block_in, ingrad_ref, late_ref, one_ref, two_ref, scaled_ref, vsum_ref = take(7)
    weights, moments, vectors, taps, biases = take(4), take(3), take(3), take(3), take(3)
    block_out, out_ref = take(2)
    new_moments, new_weights = take(4), take(4)
    new_vectors, new_taps, new_biases = take(3), take(3), take(3)
    block, sem = take(2)
    into = pltpu.make_async_copy(block_in, block, sem)
    into.start()
    for row in range(20):
        at = slice(20 * row, 20 * row + 20), slice(400 + 20 * row, 420 + 20 * row)
        out_ref[0, row] = jnp.stack([ingrad_ref[part, :] for part in at], axis=1)
    into.wait()
    through = pltpu.make_async_copy(block, block_out, sem)
    through.start()
    rows = weights[0].shape[1]
    new_moments[0][...] = late_ref[0:rows, :].T
    new_weights[0][...] = 0.999 * weights[0][...] - RATES[0] * (
        scaled_ref[0, 0:rows, :].astype(F32).T
    )
    for which in (1, 2, 3):
        rows = weights[which].shape[0]
        summed = one_ref[80:400, :] if which == 2 else (two_ref if which == 3 else one_ref)[0:rows, :]
        new_moments[which][...] = 0.95 * moments[which - 1][...] + summed.astype(F32)
        new_weights[which][...] = 0.999 * weights[which][...] - RATES[which] * scaled_ref[
            which, 0:rows, :
        ].astype(F32)
    bias_sums = vsum_ref[9:13, :]

    def bias_part(part):
        row, column = divmod(part * HEAD_DIM, D)
        return bias_sums[row : row + 1, column : column + HEAD_DIM]

    bias_grad = jnp.concatenate(
        [
            jnp.concatenate([bias_part(2 * r), bias_part(2 * r + 1)], axis=1)
            for r in range(FF // 128)
        ],
        axis=0,
    )
    for (param, mean, square), outs, grad, rate, decay in (
        (vectors, new_vectors, vsum_ref[0:9, :], 0.2, 0.0),
        (taps, new_taps, vsum_ref[13:40, :], 0.05, 0.01),
        (biases, new_biases, bias_grad, 0.2, 0.0),
    ):
        for ref, value in zip(
            outs, adamw(param[...], mean[...], square[...], grad, rate, decay)
        ):
            ref[...] = value
    through.wait()


def update(block, sums, weights, moments, vectors, taps, biases):
    operands = [block, *sums, *weights, *moments[1:], *vectors, *taps, *biases]
    hbm = pl.BlockSpec(memory_space=pl.ANY)
    outs = [jax.ShapeDtypeStruct(block.shape, dtype) for dtype in (BF, F32)]
    outs += [
        jax.ShapeDtypeStruct(x.shape, F32)
        for x in (*moments, *weights, *vectors, *taps, *biases)
    ]
    return pl.pallas_call(
        update_kernel,
        in_specs=[hbm] + [VMEM_SPEC] * (len(operands) - 1),
        out_specs=[hbm] + [VMEM_SPEC] * (len(outs) - 1),
        out_shape=outs,
        scratch_shapes=[pltpu.VMEM(block.shape, BF), pltpu.SemaphoreType.DMA],
        compiler_params=pltpu.CompilerParams(vmem_limit_bytes=62 * 2**20),
        cost_estimate=pl.CostEstimate(
            flops=2**22, bytes_accessed=12 * 2**20, transcendentals=2**14
        ),
    )(*operands)


def frames_last(block):
    return jnp.transpose(block, (0, 2, 3, 1, 4))


def frames_second(block):
    return jnp.transpose(block, (0, 3, 1, 2, 4))


def per_device(
    clips_in,
    out_grad,
    clip_side,
    qkv_weight,
    proj_weight,
    up_weight,
    down_weight,
    qkv_moment,
    proj_moment,
    up_moment,
    down_moment,
    vectors,
    vector_mean,
    vector_square,
    up_bias,
    up_bias_mean,
    up_bias_square,
    conv_kernel,
    kernel_mean,
    kernel_square,
):
    clips = lax.axis_size("clip")
    clips_in, out_grad = frames_last(clips_in), frames_last(out_grad)
    weights = (qkv_weight, proj_weight, up_weight, down_weight)
    moments = (qkv_moment, proj_moment, up_moment, down_moment)
    (
        tokens,
        normed_home,
        normed_cross,
        heads_q,
        home,
        cross,
        kept,
        heads_out,
        query_weight,
        pair_weight,
        other_weights,
    ) = front(clips_in, clip_side, qkv_weight.T, *weights[1:], vectors, conv_kernel, clips, 0)
    block_out, ingrad, sums_one, sums_two, late_moment, scaled, vector_sums = rest(
        (heads_out, tokens, out_grad, other_weights),
        (clip_side, jnp.asarray(CELL_AT), vectors, up_bias.reshape(FF // 128, 128), conv_kernel),
        (
            heads_q,
            kept,
            cross,
            home,
            normed_home,
            normed_cross,
            query_weight,
            pair_weight,
        ),
        (clips_in, qkv_moment.T, *moments[1:]),
        clips,
        1,
    )
    as_rows = lambda vector: vector.reshape(FF // 128, 128)
    updated = update(
        block_out,
        (ingrad, late_moment, sums_one, sums_two, scaled, vector_sums),
        (qkv_weight.T, *weights[1:]),
        (qkv_moment.T, *moments[1:]),
        (vectors, vector_mean, vector_square),
        (conv_kernel, kernel_mean, kernel_square),
        tuple(as_rows(vector) for vector in (up_bias, up_bias_mean, up_bias_square)),
    )
    new_moments = (updated[2].T, *updated[3:6])
    new_weights = (updated[6].T, *updated[7:10])
    outs = [frames_second(updated[0]), frames_second(updated[1])]
    for moment, weight in zip(new_moments, new_weights):
        outs += [moment, weight]
    bias_new = [vector.reshape(FF) for vector in updated[16:19]]
    return (*outs, *updated[10:13], *bias_new, *updated[13:16])


def solution(mesh):
    big = P("clip", "frame", None, None, None)
    rows = P("frame", None)
    return jax.shard_map(
        per_device,
        mesh=mesh,
        in_specs=(big, big, P("clip")) + (rows,) * 8 + (P(),) * 9,
        out_specs=(big, big) + (rows,) * 8 + (P(),) * 9,
        check_vma=False,
    )
```

```python
import functools
import math

import jax
import jax.numpy as jnp
import numpy as np
from jax import lax
from jax.experimental import pallas as pl
from jax.experimental.pallas import tpu as pltpu
from jax.sharding import PartitionSpec as P

D = 320
HEADS = 5
HEAD_DIM = 64
PAIR = 2 * HEAD_DIM
WIDE = HEADS * PAIR
FF = 1280
NS_STEPS = 5
STEP = 10
CLIP_TOK = 3200
SHARE = 320

POLY_ONE = 3.4445
POLY_TWO = -4.775
POLY_THREE = 2.0315
LOG2E = math.log2(math.e)
SCORE_SCALE = HEAD_DIM**-0.5
MASKED = -1e30
MESH = pl.DeviceIdType.MESH
BF = jnp.bfloat16
F32 = jnp.float32
NT = (((1,), (1,)), ((), ()))
VMEM_SPEC = pl.BlockSpec(memory_space=pltpu.VMEM)


def dot_nt(left, right):
    return lax.dot_general(left, right, NT, preferred_element_type=F32)


def dot_nn(left, right):
    return jnp.dot(left, right, preferred_element_type=F32)


def lanes_of(rows):
    return lax.broadcasted_iota(jnp.int32, (rows, PAIR), 1)


CELL_AT = np.stack([np.arange(400) // 20, np.arange(400) % 20], axis=1).astype(np.float32)


def select_lanes(upper):
    row = lax.broadcasted_iota(jnp.int32, (D, WIDE), 0)
    col = lax.broadcasted_iota(jnp.int32, (D, WIDE), 1)
    source = lax.shift_left(lax.shift_right_logical(col, 7), 6) + (col & (HEAD_DIM - 1))
    half = col & HEAD_DIM
    return (source == row) & (half == (HEAD_DIM if upper else 0))


def flatten_frame(read_row, dst, base):
    for row in range(20):
        dst[base + 20 * row : base + 20 * row + 20, :] = read_row(row).astype(F32)


def build_slabs(center, edged, slot, flat, cells):
    blank = jnp.zeros((20, D), F32)
    edged[1, slot, 0:20, :] = blank
    edged[1, slot, 420:440, :] = blank
    edged[1, slot, 20:420, :] = flat
    center[1, slot] = flat
    col = cells[:, 1:2]
    for e, keep in ((0, col > 0.5), (2, col < 18.5)):
        moved = jnp.where(keep, edged[1, slot, 19 + e : 419 + e, :], 0.0)
        center[e, slot] = moved
        edged[e, slot, 0:20, :] = blank
        edged[e, slot, 420:440, :] = blank
        edged[e, slot, 20:420, :] = moved


def slab(center, edged, slot, b, e, start, size):
    if b == 1:
        return center[e, slot, pl.ds(start, size), :]
    return edged[e, slot, pl.ds(start + 20 * b, size), :]


def inside_of(side_ref, cells):
    side = side_ref[0].astype(F32) - 0.5
    return (cells[:, 0:1] < side) & (cells[:, 1:2] < side)


def norm_parts(rows):
    average = jnp.sum(rows, axis=-1, keepdims=True) * (1.0 / D)
    centered = rows - average
    variance = jnp.sum(centered * centered, axis=-1, keepdims=True) * (1.0 / D)
    scale = lax.rsqrt(variance + 1e-05)
    return centered * scale, scale


def frame_peers():
    f = lax.axis_index("frame")
    near = f + 1 - 2 * lax.rem(f, 2)
    across = lax.rem(f + 2, 4)
    return f, near, across, lax.rem(near + 2, 4)


def share_rows(rows, clips):
    return 16 * (-(-rows // (16 * clips)))


def greet_all(clips):
    barrier = pltpu.get_barrier_semaphore()
    for peer in frame_peers()[1:]:
        pl.semaphore_signal(barrier, inc=1, device_id={"frame": peer}, device_id_type=MESH)
    c = lax.axis_index("clip")

    def greet(step, carry):
        pl.semaphore_signal(
            barrier, inc=1, device_id={"clip": lax.rem(c + step, clips)}, device_id_type=MESH
        )
        return carry

    lax.fori_loop(1, clips, greet, 0)


def await_greetings(count):
    pl.semaphore_wait(pltpu.get_barrier_semaphore(), count)


def send(src, dst, send_sem, recv_sem, peer):
    return pltpu.make_async_remote_copy(
        src_ref=src,
        dst_ref=dst,
        send_sem=send_sem,
        recv_sem=recv_sem,
        device_id={"frame": peer},
        device_id_type=MESH,
    )


def halo_copies(first, last, halo, sems):
    f = lax.axis_index("frame")
    down = send(first, halo.at[1], sems.at[0, 0], sems.at[1, 0], jnp.maximum(f - 1, 0))
    up = send(last, halo.at[0], sems.at[0, 1], sems.at[1, 1], jnp.minimum(f + 1, 3))
    return down, up


def start_halos(down, up, halo):
    f = lax.axis_index("frame")

    @pl.when(f > 0)
    def _():
        down.start()

    @pl.when(f < 3)
    def _():
        up.start()

    @pl.when(f == 0)
    def _():
        halo[0] = jnp.zeros(halo.shape[1:], halo.dtype)

    @pl.when(f == 3)
    def _():
        halo[1] = jnp.zeros(halo.shape[1:], halo.dtype)


def wait_halos(down, up):
    f = lax.axis_index("frame")

    @pl.when(f > 0)
    def _():
        down.wait_send()
        up.wait_recv()

    @pl.when(f < 3)
    def _():
        up.wait_send()
        down.wait_recv()


EXP_SCALE = SCORE_SCALE * LOG2E


def tail_lanes(inside, copies):
    lane = lax.broadcasted_iota(jnp.int32, (inside.shape[0], PAIR), 1)
    tail = jnp.where(
        lane == HEAD_DIM,
        jnp.where(inside, 0.0, MASKED),
        jnp.where((lane > HEAD_DIM) & (lane < HEAD_DIM + 4), 1.0, 0.0),
    )
    return jnp.concatenate([tail] * copies, axis=0).astype(BF)


def front_kernel(
    clips,
    x_ref,
    side_ref,
    cells_ref,
    qkv_ref,
    proj_ref,
    up_ref,
    down_ref,
    vec_ref,
    taps_ref,
    tok_out,
    nhome_out,
    ncross_out,
    q_out,
    home_out,
    cross_out,
    kept_out,
    att_out,
    wq_out,
    wkv_out,
    others_out,
    tok_ref,
    nhome_ref,
    ncross_ref,
    q_ref,
    home_ref,
    cross_ref,
    kept_ref,
    att_ref,
    wq_ref,
    wkv_ref,
    others_ref,
    halo_ref,
    edge,
    raw,
    center,
    edged,
    qkv_full,
    tail,
    halo_sems,
    qkv_sems,
    other_sems,
    spread_sems,
    near_sems,
    cross_sems,
    out_sems,
):
    leaving = []

    def leave(src, dst):
        copy = pltpu.make_async_copy(src, dst, out_sems.at[len(leaving)])
        copy.start()
        leaving.append(copy)

    f, near, across, far = frame_peers()
    c = lax.axis_index("clip")
    greet_all(clips)
    part_rows = qkv_ref.shape[1]

    def qkv_rows(owner):
        return qkv_full.at[pl.ds(pl.multiple_of(owner * part_rows, 16), part_rows), :]

    qkv_full[pl.ds(pl.multiple_of(f * part_rows, 16), part_rows), :] = qkv_ref[...].T.astype(BF)
    start = 0
    for shard in (proj_ref, up_ref, down_ref):
        size = shard.shape[0]
        others_ref[f, start : start + size, :] = shard[...].astype(BF)
        start += size
    spare = others_ref.shape[1] - start
    if spare:
        others_ref[f, start : start + spare, :] = jnp.zeros((spare, D), BF)
    cells = cells_ref[...]
    inside = inside_of(side_ref, cells)
    for t in range(2):
        flatten_frame(lambda row, t=t: x_ref[0, row, :, t, :], raw, 400 * t)
        edge[t] = raw[400 * t : 400 * t + 400, :].astype(BF)

    await_greetings(3 + clips - 1)
    down, up = halo_copies(edge.at[0], edge.at[1], halo_ref, halo_sems)
    start_halos(down, up, halo_ref)
    qkv_cross = send(qkv_rows(f), qkv_rows(f), qkv_sems.at[0, 1], qkv_sems.at[1, 1], across)
    qkv_near = send(qkv_rows(f), qkv_rows(f), qkv_sems.at[0, 0], qkv_sems.at[1, 0], near)
    qkv_relay = send(
        qkv_rows(across), qkv_rows(across), qkv_sems.at[0, 2], qkv_sems.at[1, 2], near
    )
    qkv_near.start()

    part = others_ref.shape[1] // clips

    def part_of(owner, clip):
        return others_ref.at[owner, pl.ds(pl.multiple_of(clip * part, 16), part), :]

    other_near = send(
        others_ref.at[f], others_ref.at[f], other_sems.at[0, 0], other_sems.at[1, 0], near
    )
    other_cross = send(
        part_of(f, c), part_of(f, c), other_sems.at[0, 1], other_sems.at[1, 1], across
    )
    other_relay = send(
        others_ref.at[across],
        others_ref.at[across],
        other_sems.at[0, 2],
        other_sems.at[1, 2],
        near,
    )

    def spread(clip, landing):
        return pltpu.make_async_remote_copy(
            src_ref=part_of(across, c),
            dst_ref=part_of(across, landing),
            send_sem=spread_sems.at[0, clip],
            recv_sem=spread_sems.at[1, landing],
            device_id={"clip": clip},
            device_id_type=MESH,
        )

    def other_clips(act):
        def body(step, carry):
            act(lax.rem(c + step, clips))
            return carry

        lax.fori_loop(1, clips, body, 0)

    other_near.start()

    for t in range(2):
        build_slabs(
            center, edged, t + 1, jnp.where(inside, raw[400 * t : 400 * t + 400, :], 0.0), cells
        )

    def conv_part(t, depths, start, total):
        for a in depths:
            for b in range(3):
                for e in range(3):
                    offset = 9 * a + 3 * b + e
                    total = total + taps_ref[offset : offset + 1, :] * slab(
                        center, edged, t + a, b, e, start, 40
                    )
        return total

    for t, depths in ((0, (1, 2)), (1, (0, 1))):

        def own_part(step, carry, t=t, depths=depths):
            start = pl.multiple_of(step * 40, 8)
            at = pl.ds(pl.multiple_of(start + 400 * t, 8), 40)
            tok_ref[at, :] = conv_part(t, depths, start, raw[at, :] + vec_ref[4:5, :])
            return carry

        lax.fori_loop(0, 10, own_part, 0)
        if t == 0:
            qkv_cross.start()
            other_cross.start()
    wait_halos(down, up)
    for side, slot in ((0, 0), (1, 3)):
        rim = halo_ref[side].astype(F32)
        build_slabs(center, edged, slot, jnp.where(inside, rim, 0.0), cells)
    rows = tok_ref.shape[0]
    piece = rows // HEADS

    def cross_copy(k):
        at = pl.ds(pl.multiple_of(k * piece, 16), piece)
        return send(
            nhome_ref.at[at, :],
            ncross_ref.at[at, :],
            cross_sems.at[0, 0, k],
            cross_sems.at[1, 0, k],
            across,
        )

    def relay_copy(k):
        return send(
            ncross_ref.at[pl.ds(pl.multiple_of(k * piece, 16), piece), :],
            ncross_ref.at[pl.ds(pl.multiple_of(rows + k * piece, 16), piece), :],
            cross_sems.at[0, 1, k],
            cross_sems.at[1, 1, k],
            near,
        )

    near_copy = send(
        nhome_ref.at[pl.ds(0, rows), :],
        nhome_ref.at[pl.ds(rows, rows), :],
        near_sems.at[0],
        near_sems.at[1],
        near,
    )
    for t, depths, ready in ((0, (0,), (0, 1)), (1, (2,), (2,))):

        def rim_part(step, carry, t=t, depths=depths):
            start = pl.multiple_of(step * 40, 8)
            at = pl.ds(pl.multiple_of(start + 400 * t, 8), 40)
            rows = conv_part(t, depths, start, tok_ref[at, :])
            tok_ref[at, :] = rows
            raw[at, :] = norm_parts(rows)[0] * vec_ref[0:1, :] + vec_ref[1:2, :]
            return carry

        lax.fori_loop(0, 10, rim_part, 0)
        at = slice(400 * t, 400 * t + 400)
        nhome_ref[at, :] = raw[at, :].astype(BF)
        for k in ready:
            cross_copy(k).start()
    near_copy.start()
    qkv_cross.wait_recv()
    qkv_relay.start()
    other_cross.wait_recv()
    other_clips(lambda clip: spread(clip, c).start())

    blank = jnp.zeros((1, HEAD_DIM), F32)

    def head_bias(row, h):
        return vec_ref[row : row + 1, HEAD_DIM * h : HEAD_DIM * (h + 1)]

    qkv_near.wait_recv()
    qkv_relay.wait_recv()
    for h in range(HEADS):
        wq_ref[PAIR * h : PAIR * h + HEAD_DIM, :] = qkv_full[HEAD_DIM * h : HEAD_DIM * (h + 1), :]
        wq_ref[PAIR * h + HEAD_DIM : PAIR * (h + 1), :] = jnp.zeros((HEAD_DIM, D), BF)
        wkv_ref[PAIR * h : PAIR * h + HEAD_DIM, :] = qkv_full[
            D + HEAD_DIM * h : D + HEAD_DIM * (h + 1), :
        ]
        wkv_ref[PAIR * h + HEAD_DIM : PAIR * (h + 1), :] = qkv_full[
            2 * D + HEAD_DIM * h : 2 * D + HEAD_DIM * (h + 1), :
        ]
    leave(tok_ref, tok_out)
    leave(wq_ref, wq_out)
    leave(wkv_ref, wkv_out)
    wide_query = jnp.concatenate(
        [part for h in range(HEADS) for part in (head_bias(5, h), blank)], axis=1
    )
    wide_pair = jnp.concatenate(
        [part for h in range(HEADS) for part in (blank, head_bias(6, h))], axis=1
    )

    def project(normed, weight, bias, place):
        joined = (dot_nt(normed, weight[...]) + bias).astype(BF)
        for h in range(HEADS):
            place(h, joined[:, PAIR * h : PAIR * (h + 1)])

    def place_query(h, value):
        q_ref[h] = value

    def place_own(h, value):
        home_ref[h, 0:rows, :] = value

    def place_near(h, value):
        home_ref[h, rows : 2 * rows, :] = value

    def place_cross(h, value):
        cross_ref[h] = value

    project(nhome_ref[0:rows, :], wq_ref, wide_query, place_query)
    cross_copy(3).start()
    project(nhome_ref[0:rows, :], wkv_ref, wide_pair, place_own)
    leave(q_ref, q_out)
    tail[...] = tail_lanes(inside, 4)
    tile = rows // 2
    mask_lane = jnp.where(lanes_of(tile) == HEAD_DIM, 1.0, 0.0).astype(BF)

    def tile_pass(t, source, last):
        at = pl.ds(pl.multiple_of(t * tile, 16), tile)
        lane = lanes_of(tile)
        for h in range(HEADS):
            keys = jnp.concatenate([source[h], tail[...]], axis=1)
            score = dot_nt(jnp.concatenate([q_ref[h, at, :], mask_lane], axis=1), keys)
            peak = jnp.max(score, axis=-1, keepdims=True)
            if last:
                kept = kept_ref[h, at, :]
                old_peak = kept[:, 0:1]
                peak = jnp.maximum(peak, old_peak)
            terms = jnp.exp2((score - peak) * EXP_SCALE).astype(BF)
            mixed = dot_nn(terms, keys)
            total = mixed[:, PAIR + HEAD_DIM + 1 : PAIR + HEAD_DIM + 2]
            mixed = mixed[:, 0:PAIR]
            if last:
                fade = jnp.exp2((old_peak - peak) * EXP_SCALE)
                total = total + fade * kept[:, 32:33]
                mixed = (mixed + fade * kept) / total
                log_sum = peak + jnp.log2(total) * (1.0 / EXP_SCALE)
                kept_ref[h, at, :] = jnp.where(lane < HEAD_DIM, log_sum, mixed)
                att_ref[h, at, :] = jnp.where(lane < HEAD_DIM, 0.0, mixed).astype(BF)
            else:
                kept_ref[h, at, :] = jnp.where(
                    lane < 32, peak, jnp.where(lane < HEAD_DIM, total, mixed)
                )

    def pass_on(k):
        cross_copy(k).wait_recv()
        relay_copy(k).start()

    def first_pass(t, carry):
        tile_pass(t, home_ref, False)

        @pl.when(t == 0)
        def _():
            for k in (0, 1, 2):
                pass_on(k)

        return carry

    def second_pass(t, carry):
        tile_pass(t, cross_ref, True)

        @pl.when(t == 0)
        def _():
            other_relay.wait_recv()
            others_leave.start()

        return carry

    near_copy.wait_recv()
    other_near.wait()
    leave(nhome_ref, nhome_out)
    cross_copy(4).start()
    project(nhome_ref[rows : 2 * rows, :], wkv_ref, wide_pair, place_near)
    leave(home_ref, home_out)
    lax.fori_loop(0, 2, first_pass, 0)
    for k in (3, 4):
        pass_on(k)
    other_clips(lambda clip: spread(clip, clip).wait_recv())
    other_relay.start()
    others_leave = pltpu.make_async_copy(others_ref, others_out, out_sems.at[out_sems.shape[0] - 1])
    for k in range(HEADS):
        relay_copy(k).wait_recv()
    leave(ncross_ref, ncross_out)
    project(ncross_ref[...], wkv_ref, wide_pair, place_cross)
    leave(cross_ref, cross_out)
    lax.fori_loop(0, 2, second_pass, 0)
    leave(kept_ref, kept_out)
    leave(att_ref, att_out)
    other_relay.wait_send()
    other_clips(lambda clip: spread(clip, c).wait_send())
    for copy in (other_cross, near_copy, qkv_cross, qkv_near, qkv_relay):
        copy.wait_send()
    for k in range(HEADS):
        cross_copy(k).wait_send()
        relay_copy(k).wait_send()
    others_leave.wait()
    for copy in leaving:
        copy.wait()


def front(clips_in, clip_side, qkv, proj, up, down, vectors, taps, clips, collective_id):
    rows = 800
    other_rows = clips * share_rows(proj.shape[0] + up.shape[0] + down.shape[0], clips)
    outs = (
        ((rows, D), F32),
        ((2 * rows, D), BF),
        ((2 * rows, D), BF),
        ((HEADS, rows, PAIR), BF),
        ((HEADS, 2 * rows, PAIR), BF),
        ((HEADS, 2 * rows, PAIR), BF),
        ((HEADS, rows, PAIR), F32),
        ((HEADS, rows, PAIR), BF),
        ((WIDE, D), BF),
        ((WIDE, D), BF),
        ((4, other_rows, D), BF),
    )
    return pl.pallas_call(
        functools.partial(front_kernel, clips),
        in_specs=[VMEM_SPEC, pl.BlockSpec(memory_space=pltpu.SMEM)] + [VMEM_SPEC] * 7,
        out_specs=[pl.BlockSpec(memory_space=pl.ANY)] * len(outs),
        out_shape=[jax.ShapeDtypeStruct(*out) for out in outs],
        scratch_shapes=[pltpu.VMEM(*out) for out in outs]
        + [
            pltpu.VMEM((2, 400, D), BF),
            pltpu.VMEM((2, 400, D), BF),
            pltpu.VMEM((rows, D), F32),
            pltpu.VMEM((3, 4, 400, D), F32),
            pltpu.VMEM((3, 4, 440, D), F32),
            pltpu.VMEM((3 * D, D), BF),
            pltpu.VMEM((2 * rows, PAIR), BF),
            pltpu.SemaphoreType.DMA((2, 2)),
            pltpu.SemaphoreType.DMA((2, 3)),
            pltpu.SemaphoreType.DMA((2, 3)),
            pltpu.SemaphoreType.DMA((2, clips)),
            pltpu.SemaphoreType.DMA((2,)),
            pltpu.SemaphoreType.DMA((2, 2, HEADS)),
            pltpu.SemaphoreType.DMA((len(outs),)),
        ],
        compiler_params=pltpu.CompilerParams(
            collective_id=collective_id, has_side_effects=True, vmem_limit_bytes=60 * 2**20
        ),
        cost_estimate=pl.CostEstimate(
            flops=2**34, bytes_accessed=16 * 2**20, transcendentals=2**23
        ),
    )(clips_in, clip_side, jnp.asarray(CELL_AT), qkv, proj, up, down, vectors, taps)


INV_SQRT2 = math.sqrt(0.5)
INV_SQRT_2PI = 1.0 / math.sqrt(2.0 * math.pi)


def dot_tn(left, right):
    return lax.dot_general(left, right, (((0,), (0,)), ((), ())), preferred_element_type=F32)


def norm_back(upstream, unit, scale, gain):
    through = upstream * gain
    mean_one = jnp.sum(through, axis=-1, keepdims=True) * (1.0 / D)
    mean_two = jnp.sum(through * unit, axis=-1, keepdims=True) * (1.0 / D)
    return scale * (through - mean_one - unit * mean_two)


def column_sum(rows):
    return jnp.sum(rows, axis=0, keepdims=True)


def mid_phase(
    arrived,
    att_ref,
    tok_ref,
    og_ref,
    side_ref,
    cells_ref,
    vec_ref,
    ubias_ref,
    others_ref,
    out_ref,
    gsec_ref,
    dout_ref,
    grads_ref,
    vsum_ref,
    raw,
    first_out,
    wide,
    act,
    ghid,
    normed,
    top,
    branch_low,
    att_low,
    proj_ref,
    up_ref,
    down_ref,
):
    start = 0
    for full in (proj_ref, up_ref, down_ref):
        size = full.shape[0] // 4
        for owner in range(4):
            full[size * owner : size * (owner + 1), :] = others_ref[owner, start : start + size, :]
        start += size
    up_bias = jnp.concatenate([ubias_ref[r : r + 1, :] for r in range(FF // 128)], axis=1)
    inside = inside_of(side_ref, cells_ref[...])
    pick = select_lanes(True).astype(F32).astype(BF)
    wide[...] = dot_nn(proj_ref[...], pick).astype(BF)
    vsum_ref[...] = jnp.zeros(vsum_ref.shape, F32)
    arrived()
    for t in range(2):
        at = slice(400 * t, 400 * t + 400)
        heads = jnp.concatenate([att_ref[h, at, :] for h in range(HEADS)], axis=1)
        att_low[at, :] = dot_nt(heads, pick).astype(BF)
        second = tok_ref[at, :] + (dot_nt(heads, wide[...]) + vec_ref[7:8, :])
        unit, scale = norm_parts(second)
        normed_two = (unit * vec_ref[2:3, :] + vec_ref[3:4, :]).astype(BF)
        normed[at, :] = normed_two
        flatten_frame(lambda row, t=t: og_ref[0, row, :, t, :], raw, 0)
        grad_top = jnp.where(inside, raw[...], 0.0)
        top_low = grad_top.astype(BF)
        top[at, :] = top_low
        hidden = dot_nt(normed_two, up_ref[...]) + up_bias
        half = 0.5 + 0.5 * lax.erf(hidden * INV_SQRT2)
        activated = (hidden * half).astype(BF)
        act[at, :] = activated
        slope = half + hidden * (INV_SQRT_2PI * jnp.exp(-0.5 * hidden * hidden))
        grad_hidden = (dot_nt(top_low, down_ref[...]) * slope).astype(BF)
        ghid[at, :] = grad_hidden
        result = second + (dot_nn(activated, down_ref[...]) + vec_ref[8:9, :])
        if t == 0:
            first_out[...] = result
        else:
            raw[...] = result
            for row in range(20):
                part = slice(20 * row, 20 * row + 20)
                out_ref[0, row] = jnp.stack([first_out[part, :], raw[part, :]], axis=1).astype(BF)
        upstream = dot_nn(grad_hidden, up_ref[...])
        grad_second = grad_top + norm_back(upstream, unit, scale, vec_ref[2:3, :])
        gsec_ref[at, :] = grad_second
        low = grad_second.astype(BF)
        branch_low[at, :] = low
        dout = dot_nn(low, wide[...]).astype(BF)
        for h in range(HEADS):
            dout_ref[h, at, :] = dout[:, PAIR * h : PAIR * (h + 1)]
        vsum_ref[0:1, :] += column_sum(upstream * unit)
        vsum_ref[1:2, :] += column_sum(upstream)
        vsum_ref[2:3, :] += column_sum(low.astype(F32))
        vsum_ref[3:4, :] += column_sum(grad_top)
        bias_sum = column_sum(grad_hidden.astype(F32))
        for part in range(4):
            vsum_ref[4 + part : 5 + part, :] += bias_sum[:, D * part : D * (part + 1)]
    rows = up_ref.shape[0] // 4
    proj_rows = D // 4
    grad = dot_tn(branch_low[...], att_low[...]).astype(BF)
    for owner in range(4):
        grads_ref[owner, 0:proj_rows, :] = grad[proj_rows * owner : proj_rows * (owner + 1), :]
    for owner in range(4):
        at = slice(rows * owner, rows * (owner + 1))
        start = proj_rows
        grads_ref[owner, start : start + rows, :] = dot_tn(ghid[:, at], normed[...]).astype(BF)
        start = proj_rows + rows
        grads_ref[owner, start : start + rows, :] = dot_tn(act[:, at], top[...]).astype(BF)


class RowSums:
    def __init__(self, clips, g_ref, at, pair_in, cross_out, cross_in, shares, shares_in, sums,
                 frame_sems, part_sems, sum_sems):
        self.clips = clips
        self.g = g_ref
        self.at = at
        self.pair_in = pair_in
        self.cross_out = cross_out
        self.cross_in = cross_in
        self.shares = shares
        self.shares_in = shares_in
        self.sums = sums
        self.part_sems = part_sems
        self.sum_sems = sum_sems
        f, near, across, far = frame_peers()
        self.f, self.across = f, across
        self.c = lax.axis_index("clip")
        sem = frame_sems
        part = lambda owner: g_ref.at[owner, pl.ds(at.start, at.stop - at.start), :]
        self.first = send(part(far), pair_in.at[0], sem.at[0, 0], sem.at[1, 0], near)
        self.second = send(part(near), pair_in.at[1], sem.at[0, 1], sem.at[1, 1], near)
        self.cross = send(cross_out, cross_in, sem.at[0, 2], sem.at[1, 2], across)

    def peer(self, step):
        return lax.rem(self.c + step, self.clips)

    def part_copy(self, step):
        return pltpu.make_async_remote_copy(
            src_ref=self.shares.at[self.peer(step)],
            dst_ref=self.shares_in.at[step],
            send_sem=self.part_sems.at[0, step],
            recv_sem=self.part_sems.at[1, step],
            device_id={"clip": self.peer(step)},
            device_id_type=MESH,
        )

    def sum_copy(self, step):
        return pltpu.make_async_remote_copy(
            src_ref=self.sums.at[self.c],
            dst_ref=self.sums.at[self.c],
            send_sem=self.sum_sems.at[0, step],
            recv_sem=self.sum_sems.at[1, step],
            device_id={"clip": self.peer(step)},
            device_id_type=MESH,
        )

    def each(self, act):
        def body(step, carry):
            act(step)
            return carry

        lax.fori_loop(1, self.clips, body, 0)

    def pair_step(self):
        self.first.start()
        self.second.start()

    def cross_step(self):
        self.first.wait()
        self.cross_out[...] = (
            self.g[self.across, self.at, :].astype(F32) + self.pair_in[0].astype(F32)
        ).astype(BF)
        self.cross.start()

    def share_step(self):
        self.second.wait()
        self.cross.wait()
        mine = (
            self.g[self.f, self.at, :].astype(F32)
            + self.pair_in[1].astype(F32)
            + self.cross_in[...].astype(F32)
        ).astype(BF)
        rows, chunk = mine.shape[0], self.shares.shape[1]
        spare = self.clips * chunk - rows
        if spare:
            mine = jnp.concatenate([mine, jnp.zeros((spare, D), BF)], axis=0)
        self.shares[...] = mine.reshape(self.clips, chunk, D)
        self.each(lambda step: self.part_copy(step).start())

    def sum_step(self):
        self.each(lambda step: self.part_copy(step).wait())

        def add_part(step, total):
            return total + self.shares_in[step].astype(F32)

        total = lax.fori_loop(1, self.clips, add_part, self.shares[self.c].astype(F32))
        self.sums[self.c] = total.astype(BF)
        self.each(lambda step: self.sum_copy(step).start())

    def finish(self):
        self.each(lambda step: self.sum_copy(step).wait())


def row_sums_scratch(rows, clips):
    chunk = share_rows(rows, clips)
    return [
        pltpu.VMEM((2, rows, D), BF),
        pltpu.VMEM((rows, D), BF),
        pltpu.VMEM((rows, D), BF),
        pltpu.VMEM((clips, chunk, D), BF),
        pltpu.VMEM((clips, chunk, D), BF),
        pltpu.VMEM((clips, chunk, D), BF),
        pltpu.SemaphoreType.DMA((2, 3)),
        pltpu.SemaphoreType.DMA((2, clips)),
        pltpu.SemaphoreType.DMA((2, clips)),
    ]


EARLY_PARTS = (slice(0, 400), slice(400, 720))


def row_pieces(start, size, block):
    pieces, skip = [], 0
    while skip < size:
        owner, row = divmod(start + skip, block)
        step = min(size - skip, block - row)
        pieces.append((owner, row, skip, step))
        skip += step
    return pieces


def back_phase(
    one,
    two,
    arrived,
    q_ref,
    dout_ref,
    kept_ref,
    cross_ref,
    home_ref,
    nhome_ref,
    ncross_ref,
    wq_ref,
    wkv_ref,
    side_ref,
    cells_ref,
    gnorm_ref,
    own_ref,
    out_ref,
    bsum_ref,
    grads_ref,
    grads_in,
    pair_out,
    pair_in,
    cross_out,
    cross_in,
    pair_sems,
    cross_sems,
    grad_sems,
    extra,
    qd_t,
    tail,
    low_one,
    low_two,
    low_three,
    dq_sum,
    turned_pairs,
    pair_grad,
):
    f, near, across, far = frame_peers()
    rows = q_ref.shape[1]
    dnormed = gnorm_ref
    dq_low = q_ref
    tail[...] = tail_lanes(inside_of(side_ref, cells_ref[...]), 4)
    arrived(0, 3)
    lower = lax.broadcasted_iota(jnp.int32, (PAIR, 1), 0) < HEAD_DIM
    scale_of = jnp.where(lower, SCORE_SCALE, 1.0)
    chunks = ((0, 512, low_one), (512, 512, low_two), (1024, 576, low_three))

    def minus_parts(column, lane):
        high = column.astype(BF).astype(F32)
        mid = (column - high).astype(BF).astype(F32)
        rest = column - high - mid
        return jnp.where(
            lane == HEAD_DIM + 1,
            -high,
            jnp.where(lane == HEAD_DIM + 2, -mid, jnp.where(lane == HEAD_DIM + 3, -rest, 0.0)),
        )

    def prepare(h):
        lane = lanes_of(rows)
        kept = kept_ref[h]
        queries, douts = q_ref[h].astype(F32), dout_ref[h].astype(F32)
        log_sum = kept[:, 0:1]
        row_dot = jnp.sum(douts * kept, axis=-1, keepdims=True)
        of_queries = jnp.where(lane == HEAD_DIM, 1.0, minus_parts(log_sum, lane))
        extra[h, 0:rows, :] = of_queries.astype(BF)
        extra[h, rows : 2 * rows, :] = minus_parts(row_dot, lane).astype(BF)
        qd_t[h] = jnp.concatenate([queries, douts], axis=0).T.astype(BF)
        bsum_ref[1, h] = column_sum(douts)

    def head_pass(h, source, add):
        pairs = source[h]
        both = jnp.concatenate([q_ref[h], dout_ref[h]], axis=0)
        both = jnp.concatenate([both, extra[h]], axis=1)
        products = [
            dot_nt(
                both,
                jnp.concatenate(
                    [pairs[start : start + size, :], tail[start : start + size, :]], axis=1
                ),
            )
            for start, size, low in chunks
        ]
        total = dq_sum[h] if add else None
        at = pl.ds(pl.multiple_of(h * PAIR, PAIR), PAIR)
        for (start, size, low), product in zip(chunks, products):
            probs = jnp.exp2(product[0:rows, :] * EXP_SCALE)
            low[0:rows, :] = (probs * product[rows : 2 * rows, :]).astype(BF)
            low[rows : 2 * rows, :] = probs.astype(BF)
            part = dot_nn(low[0:rows, :], pairs[start : start + size, :])
            total = part if total is None else total + part
            turned = dot_nn(qd_t[h], low[...]) * scale_of
            turned_pairs[at, start : start + size] = turned.astype(BF)
        if add:
            total = jnp.where(lanes_of(rows) < HEAD_DIM, total * SCORE_SCALE, 0.0)
            dq_low[h] = total.astype(BF)
            bsum_ref[0, h] = column_sum(total)
        else:
            dq_sum[h] = total

    def of_normed(normed, add):
        grad = dot_nn(turned_pairs[...], normed[...])
        pair_grad[...] = pair_grad[...] + grad if add else grad
        total = dot_nn(wkv_ref[...].astype(F32).T.astype(BF), turned_pairs[...]).T
        dnormed[...] = total[0:rows, :]
        pair_out[...] = total[rows : 2 * rows, :].astype(BF)

    def pair_copy(phase):
        return send(
            pair_out, pair_in.at[phase], pair_sems.at[0, phase], pair_sems.at[1, phase], near
        )

    to_across = send(cross_out, cross_in, cross_sems.at[0], cross_sems.at[1], across)

    def cross_pass(h, carry):
        prepare(h)
        head_pass(h, cross_ref, False)

        @pl.when(h == 0)
        def _():
            one.cross_step()

        @pl.when(h == 2)
        def _():
            two.cross_step()

        @pl.when(h == 3)
        def _():
            one.share_step()

        return carry

    def home_pass(h, carry):
        head_pass(h, home_ref, True)

        @pl.when(h == 0)
        def _():
            pair_copy(0).wait()
            cross_out[...] = (dnormed[...] + pair_in[0].astype(F32)).astype(BF)
            to_across.start()
            two.share_step()

        @pl.when(h == 1)
        def _():
            one.sum_step()

        @pl.when(h == 3)
        def _():
            two.sum_step()

        return carry

    lax.fori_loop(0, HEADS, cross_pass, 0)
    arrived(3, 8)
    of_normed(ncross_ref, False)
    pair_copy(0).start()
    lax.fori_loop(0, HEADS, home_pass, 0)
    of_normed(nhome_ref, True)
    pair_copy(1).start()

    block = grads_ref.shape[1]

    def place(start, values):
        for owner, row, skip, size in row_pieces(start, values.shape[0], block):
            grads_ref[owner, row : row + size, :] = values[skip : skip + size, :]

    dq = jnp.concatenate([dq_low[h] for h in range(HEADS)], axis=1)
    of_queries = dot_tn(dq, nhome_ref[0:rows, :]).astype(BF)
    for h in range(HEADS):
        of_pairs = pair_grad[PAIR * h : PAIR * (h + 1), :].astype(BF)
        place(HEAD_DIM * h, of_queries[PAIR * h : PAIR * h + HEAD_DIM, :])
        place(D + HEAD_DIM * h, of_pairs[0:HEAD_DIM, :])
        place(2 * D + HEAD_DIM * h, of_pairs[HEAD_DIM:PAIR, :])
    to_pair = [
        send(grads_ref.at[peer], grads_in.at[k], grad_sems.at[0, k], grad_sems.at[1, k], near)
        for k, peer in enumerate((far, near))
    ]
    for copy in to_pair:
        copy.start()
    total = dnormed[...] + dot_nn(dq, wq_ref[...])
    to_across.wait()
    pair_copy(1).wait()
    gnorm_ref[...] = total + pair_in[1].astype(F32) + cross_in[...].astype(F32)
    for copy in to_pair:
        copy.wait()
    out_ref[...] = (grads_ref[across].astype(F32) + grads_in[0].astype(F32)).astype(BF)
    own_ref[...] = grads_ref[f].astype(F32) + grads_in[1].astype(F32)


def newton_schulz(whole):
    wide = whole.astype(F32)
    norm = jnp.sqrt(jnp.sum(wide * wide)) + 1e-07
    eye = (
        lax.broadcasted_iota(jnp.int32, (D, D), 0) == lax.broadcasted_iota(jnp.int32, (D, D), 1)
    ).astype(F32)
    turned = dot_nt(eye.astype(BF), whole) / norm

    def iterate(step, current):
        held = current.astype(BF)
        gram = dot_nt(held, held)
        gram_low = gram.astype(BF)
        poly = POLY_TWO * gram + POLY_THREE * dot_nn(gram_low, gram_low)
        return POLY_ONE * current + dot_nn(poly.astype(BF), held)

    for step in range(NS_STEPS):
        turned = iterate(step, turned)
    return turned


OWNER_OF = (3, 1, 0, 2)
QKV_AT = OWNER_OF[0]


def tail_phase(
    clips,
    one,
    two,
    arrived,
    copy_out,
    gnorm_ref,
    own_ref,
    across_ref,
    bsum_ref,
    tok_ref,
    gsec_ref,
    x_ref,
    side_ref,
    cells_ref,
    taps_ref,
    vec_ref,
    mid_sums_ref,
    one_ref,
    two_ref,
    qkv_m_ref,
    proj_m_ref,
    up_m_ref,
    down_m_ref,
    late_ref,
    scaled_ref,
    vsum_ref,
    cross_in,
    shares,
    shares_in,
    new_rows,
    new_low,
    first_low,
    rim,
    v_mine,
    v_frames,
    v_total,
    v_clips,
    gathered,
    old_rows,
    center,
    edged,
    low,
    grad_sems,
    part_sems,
    row_sems,
    spread_sems,
    rim_sems,
    vf_sems,
    vc_sems,
    there_sems,
    back_sems,
):
    first, ingrad_ref, outer = gnorm_ref, gsec_ref, tok_ref
    f, near, across, far = frame_peers()
    c = lax.axis_index("clip")
    block = own_ref.shape[0]
    owners, chunk = shares.shape[0], shares.shape[1]

    def each(count, act):
        def body(step, carry):
            act(step)
            return carry

        lax.fori_loop(0, count, body, 0)

    def other_clips(act):
        each(clips - 1, lambda step: act(lax.rem(c + 1 + step, clips)))

    down, up = halo_copies(first_low.at[0], first_low.at[1], rim, rim_sems)

    to_across = send(across_ref, cross_in, grad_sems.at[0], grad_sems.at[1], across)
    to_across.start()

    upstream = gnorm_ref[...]
    unit, scale = norm_parts(tok_ref[...])
    grad_first = gsec_ref[...] + norm_back(upstream, unit, scale, vec_ref[0:1, :])
    first[...] = grad_first
    first_low[...] = grad_first.astype(BF).reshape(first_low.shape)
    one.finish()
    two.finish()
    one_ref[...] = one.sums[...].reshape(one_ref.shape)
    two_ref[...] = two.sums[...].reshape(two_ref.shape)
    arrived(0, 5)
    old_rows[0:block, :] = qkv_m_ref[...].T
    if owners * chunk > block:
        old_rows[block : owners * chunk, :] = jnp.zeros((owners * chunk - block, D), F32)

    v_mine[0:1, :] = column_sum(upstream * unit)
    v_mine[1:2, :] = column_sum(upstream)
    v_mine[2:4, :] = mid_sums_ref[0:2, :]
    v_mine[4:5, :] = column_sum(grad_first)
    v_mine[5:6, :] = jnp.concatenate(
        [bsum_ref[0, h, :, 0:HEAD_DIM] for h in range(HEADS)], axis=1
    )
    v_mine[6:7, :] = jnp.concatenate(
        [bsum_ref[1, h, :, HEAD_DIM:PAIR] for h in range(HEADS)], axis=1
    )
    v_mine[7:9, :] = mid_sums_ref[2:4, :]
    v_mine[9:13, :] = mid_sums_ref[4:8, :]

    cells = cells_ref[...]
    inside = inside_of(side_ref, cells)
    for t in range(2):
        build_slabs(center, edged, t + 1, first[400 * t : 400 * t + 400, :], cells)

    def part_copy(owner):
        return pltpu.make_async_remote_copy(
            src_ref=shares.at[owner],
            dst_ref=shares_in.at[c],
            send_sem=part_sems.at[0, owner],
            recv_sem=part_sems.at[1, c],
            device_id={"clip": owner},
            device_id_type=MESH,
        )

    def other_owners(act):
        def step(owner):
            @pl.when(owner != c)
            def _():
                act(owner)

        each(owners, step)

    to_across.wait()
    mine = (own_ref[...] + cross_in[...].astype(F32)).astype(BF)
    if owners * chunk > block:
        mine = jnp.concatenate([mine, jnp.zeros((owners * chunk - block, D), BF)], axis=0)
    shares[...] = mine.reshape(owners, chunk, D)
    other_owners(lambda owner: part_copy(owner).start())
    start_halos(down, up, rim)

    def row_copy(clip):
        return pltpu.make_async_remote_copy(
            src_ref=new_rows.at[c],
            dst_ref=new_rows.at[c],
            send_sem=row_sems.at[0, clip],
            recv_sem=row_sems.at[1, c],
            device_id={"clip": clip},
            device_id_type=MESH,
        )

    def spread_copy(clip):
        return pltpu.make_async_remote_copy(
            src_ref=new_low,
            dst_ref=gathered.at[f, pl.ds(pl.multiple_of(c * chunk, 16), chunk), :],
            send_sem=spread_sems.at[4, clip],
            recv_sem=spread_sems.at[f, c],
            device_id={"clip": clip, "frame": QKV_AT},
            device_id_type=MESH,
        )

    def share_sum():
        @pl.when(c < owners)
        def _():
            shares_in[c] = shares[c]

            def arrive(clip):
                pltpu.make_async_remote_copy(
                    src_ref=shares.at[0],
                    dst_ref=shares_in.at[clip],
                    send_sem=part_sems.at[0, 0],
                    recv_sem=part_sems.at[1, clip],
                    device_id={"clip": clip},
                    device_id_type=MESH,
                ).wait_recv()

            other_clips(arrive)

            def add_part(clip, total):
                return total + shares_in[clip].astype(F32)

            total = lax.fori_loop(0, clips, add_part, jnp.zeros((chunk, D), F32))
            at = pl.ds(pl.multiple_of(c * chunk, 16), chunk)
            fresh = 0.95 * old_rows[at, :] + total
            new_rows[c] = fresh
            new_low[...] = fresh.astype(BF)
            other_clips(lambda clip: spread_copy(clip).start())

            @pl.when(f != QKV_AT)
            def _():
                spread_copy(c).start()

            @pl.when(f == QKV_AT)
            def _():
                gathered[QKV_AT, at, :] = new_low[...]

            other_clips(lambda clip: row_copy(clip).start())

    for t in range(2):
        at = slice(400 * t, 400 * t + 400)
        flatten_frame(lambda row, t=t: x_ref[0, row, :, t, :], outer, 400 * t)
        outer[at, :] = jnp.where(inside, outer[at, :], 0.0)

    def plane(t, a, add_rows, add_taps):
        def step(number, totals):
            start = pl.multiple_of(number * 16, 16)
            at = pl.ds(pl.multiple_of(start + 400 * t, 16), 16)
            masked = outer[at, :]
            total = jnp.zeros((16, D), F32)
            sums_out = []
            for b in range(3):
                for e in range(3):
                    offset = 9 * a + 3 * b + e
                    piece = slab(center, edged, t + 2 - a, 2 - b, 2 - e, start, 16)
                    total = total + taps_ref[offset : offset + 1, :] * piece
                    product = masked * piece
                    sums_out.append(totals[3 * b + e] + (product[0:8, :] + product[8:16, :]))
            if add_rows:
                ingrad_ref[at, :] += total
            else:
                ingrad_ref[at, :] = total
            return tuple(sums_out)

        totals = lax.fori_loop(0, 25, step, tuple(jnp.zeros((8, D), F32) for _ in range(9)))
        for which, total in enumerate(totals):
            at = slice(13 + 9 * a + which, 14 + 9 * a + which)
            if add_taps:
                v_mine[at, :] += column_sum(total)
            else:
                v_mine[at, :] = column_sum(total)

    plane(0, 0, False, False)

    moments = (None, proj_m_ref, up_m_ref, down_m_ref)

    def to_owner(which):
        at = pl.ds(0, moments[which].shape[0])
        return send(
            low.at[which, at, :],
            gathered.at[f, at, :],
            there_sems.at[0, which],
            there_sems.at[1, f],
            OWNER_OF[which],
        )

    for which in (3, 2, 1):
        rows = moments[which].shape[0]
        summed = one_ref[80:400, :] if which == 2 else (two_ref if which == 3 else one_ref)[0:rows, :]
        low[which, 0:rows, :] = (0.95 * moments[which][...] + summed.astype(F32)).astype(BF)

        @pl.when(f != OWNER_OF[which])
        def _(which=which):
            to_owner(which).start()

    plane(0, 1, True, False)
    share_sum()
    plane(1, 1, False, True)
    plane(1, 2, True, False)
    wait_halos(down, up)
    for side, slot in ((0, 0), (1, 3)):
        build_slabs(center, edged, slot, rim[side].astype(F32), cells)
    plane(0, 2, True, True)
    plane(1, 0, True, True)
    for t in range(2):
        at = slice(400 * t, 400 * t + 400)
        ingrad_ref[at, :] = first[at, :] + jnp.where(inside, ingrad_ref[at, :], 0.0)
    copy_out()

    v_copies = []
    for which, peer in enumerate((near, across, far)):
        copy = send(v_mine, v_frames.at[f], vf_sems.at[0, which], vf_sems.at[1, which], peer)
        copy.start()
        v_copies.append(copy)
    v_frames[f] = v_mine[...]

    @pl.when(f == QKV_AT)
    def _():
        def rows_arrive(frame, clip):
            pltpu.make_async_remote_copy(
                src_ref=new_low,
                dst_ref=gathered.at[frame, pl.ds(pl.multiple_of(clip * chunk, 16), chunk), :],
                send_sem=spread_sems.at[4, clip],
                recv_sem=spread_sems.at[frame, clip],
                device_id={"clip": clip, "frame": frame},
                device_id_type=MESH,
            ).wait_recv()

        other_owners(lambda clip: rows_arrive(QKV_AT, clip))
        for step in (1, 2, 3):
            frame = (QKV_AT + step) % 4
            each(owners, lambda clip, frame=frame: rows_arrive(frame, clip))

    for which in (1, 2, 3):

        @pl.when(f != OWNER_OF[which])
        def _(which=which):
            to_owner(which).wait_send()

        @pl.when(f == OWNER_OF[which])
        def _(which=which):
            at = pl.ds(0, moments[which].shape[0])
            gathered[OWNER_OF[which], at, :] = low[which, at, :]
            for other in range(4):
                if other != OWNER_OF[which]:
                    send(
                        low.at[0, at, :],
                        gathered.at[other, at, :],
                        there_sems.at[0, 0],
                        there_sems.at[1, other],
                        other,
                    ).wait_recv()

    turned = newton_schulz(gathered[...].reshape(4 * SHARE, D))
    low[:, 0:SHARE, :] = turned.T.astype(BF).reshape(4, SHARE, D)
    row_counts = (block, *(ref.shape[0] for ref in moments[1:]))

    def back_copy(which, step):
        at = pl.ds(0, row_counts[which])
        to = (OWNER_OF[which] + step) % 4
        return send(
            low.at[to, at, :],
            scaled_ref.at[which, at, :],
            back_sems.at[0, step],
            back_sems.at[1, which],
            to,
        )

    for which in range(4):

        @pl.when(f == OWNER_OF[which])
        def _(which=which):
            for step in (2, 1, 3):
                back_copy(which, step).start()
            at = pl.ds(0, row_counts[which])
            scaled_ref[which, at, :] = low[OWNER_OF[which], at, :]

    for copy in v_copies:
        copy.wait()
    v_total[...] = v_frames[0] + v_frames[1] + v_frames[2] + v_frames[3]

    def v_copy(clip):
        return pltpu.make_async_remote_copy(
            src_ref=v_total,
            dst_ref=v_clips.at[c],
            send_sem=vc_sems.at[0, clip],
            recv_sem=vc_sems.at[1, c],
            device_id={"clip": clip},
            device_id_type=MESH,
        )

    other_clips(lambda clip: v_copy(clip).start())
    v_clips[c] = v_total[...]

    other_owners(lambda owner: part_copy(owner).wait_send())

    @pl.when(c < owners)
    def _():
        other_clips(lambda clip: spread_copy(clip).wait_send())

        @pl.when(f != QKV_AT)
        def _():
            spread_copy(c).wait_send()

        other_clips(lambda clip: row_copy(clip).wait_send())

    def new_rows_arrive(clip):
        pltpu.make_async_remote_copy(
            src_ref=new_rows.at[0],
            dst_ref=new_rows.at[clip],
            send_sem=row_sems.at[0, 0],
            recv_sem=row_sems.at[1, clip],
            device_id={"clip": clip},
            device_id_type=MESH,
        ).wait_recv()

    other_owners(new_rows_arrive)
    late_ref[...] = new_rows[...].reshape(late_ref.shape)

    def v_arrives(clip):
        v_copy(clip).wait_send()
        pltpu.make_async_remote_copy(
            src_ref=v_total,
            dst_ref=v_clips.at[clip],
            send_sem=vc_sems.at[0, clip],
            recv_sem=vc_sems.at[1, clip],
            device_id={"clip": clip},
            device_id_type=MESH,
        ).wait_recv()

    other_clips(v_arrives)

    def add_v(step, total):
        return total + v_clips[step]

    vsum_ref[...] = lax.fori_loop(0, clips, add_v, jnp.zeros(vsum_ref.shape, F32))
    for which in range(4):

        @pl.when(f == OWNER_OF[which])
        def _(which=which):
            for step in (2, 1, 3):
                back_copy(which, step).wait_send()

        @pl.when(f != OWNER_OF[which])
        def _(which=which):
            back_copy(which, 1).wait_recv()


def rest_kernel(
    clips,
    att_in,
    tok_in,
    og_in,
    others_in,
    side_ref,
    cells_ref,
    vec_ref,
    ubias_ref,
    taps_ref,
    *refs,
):
    refs = list(refs)

    def take(count):
        taken, refs[:count] = refs[:count], []
        return taken

    back_sources = take(8)
    tail_sources = take(5)
    block_out, ingrad_out, one_ref, two_ref, late_ref, scaled_ref, vsum_ref = take(7)
    tok, out, gsec, dout, early, mid_sums = take(6)
    back_inputs = take(8)
    gnorm, own, across_rows, bsum = take(4)
    back_buffers = take(6)
    back_sems = take(3)
    tail_landing = take(12)
    tail_sems = take(9)
    (copy_sems,) = take(1)
    half = len(refs) // 2
    f, near, across, far = frame_peers()
    c = lax.axis_index("clip")
    gathered = tail_landing[-1]
    block, proj_rows = own.shape[0], D // 4
    chunk = share_rows(block, clips)
    owned = -(-block // chunk) * chunk

    @pl.when(f == QKV_AT)
    def _():
        gathered[:, owned:SHARE, :] = jnp.zeros((4, SHARE - owned, D), BF)

    @pl.when(f == OWNER_OF[1])
    def _():
        gathered[:, proj_rows:SHARE, :] = jnp.zeros((4, SHARE - proj_rows, D), BF)

    greet_all(clips)
    barrier = pltpu.get_barrier_semaphore()

    def greet(frame):
        def body(step, carry):
            pl.semaphore_signal(
                barrier,
                inc=1,
                device_id={"clip": lax.rem(c + step, clips), "frame": frame},
                device_id_type=MESH,
            )
            return carry

        lax.fori_loop(1, clips, body, 0)

    @pl.when(f == QKV_AT)
    def _():
        for step in (1, 2, 3):
            greet((QKV_AT + step) % 4)

    @pl.when(f != QKV_AT)
    def _():
        greet(QKV_AT)

    def copies(sources, targets, first):
        return [
            pltpu.make_async_copy(src, dst, copy_sems.at[first + k])
            for k, (src, dst) in enumerate(zip(sources, targets))
        ]

    def arrival(waiting):
        def arrived(start, stop):
            for copy in waiting[start:stop]:
                copy.wait()

        return arrived

    for_back = copies(back_sources, back_inputs, 4)

    def middle(att, og, others, *scratch):
        for_mid = copies((others_in, att_in, tok_in, og_in), (others, att, tok, og), 0)
        for copy in for_mid:
            copy.start()
        for_mid[0].wait()

        def arrived():
            for copy in for_mid[1:]:
                copy.wait()
            for copy in for_back:
                copy.start()

        mid_phase(
            arrived, att, tok, og, side_ref, cells_ref, vec_ref, ubias_ref, others, out, gsec, dout, early,
            mid_sums, *scratch,
        )

    rows = tok.shape[0]
    vmem = pltpu.VMEM
    pl.run_scoped(
        middle,
        vmem(att_in.shape, BF),
        vmem(og_in.shape, BF),
        vmem(others_in.shape, BF),
        vmem((400, D), F32),
        vmem((400, D), F32),
        vmem((D, WIDE), BF),
        vmem((rows, FF), BF),
        vmem((rows, FF), BF),
        vmem((rows, D), BF),
        vmem((rows, D), BF),
        vmem((rows, D), BF),
        vmem((rows, D), BF),
        vmem((D, D), BF),
        vmem((FF, D), BF),
        vmem((FF, D), BF),
    )
    out_copy = pltpu.make_async_copy(out, block_out, copy_sems.at[0])
    out_copy.start()

    @pl.when(f == QKV_AT)
    def _():
        await_greetings(3 + 4 * (clips - 1))

    @pl.when(f != QKV_AT)
    def _():
        await_greetings(3 + 2 * (clips - 1))

    one = RowSums(clips, early, EARLY_PARTS[0], *refs[:half])
    two = RowSums(clips, early, EARLY_PARTS[1], *refs[half:])
    one.pair_step()
    two.pair_step()

    def backward(*scratch):
        back_phase(
            one, two, arrival(for_back), back_inputs[0], dout, *back_inputs[1:], side_ref,
            cells_ref, gnorm, own, across_rows, bsum, *back_buffers, *back_sems, *scratch,
        )

    pl.run_scoped(
        backward,
        vmem((HEADS, 2 * rows, PAIR), BF),
        vmem((HEADS, PAIR, 2 * rows), BF),
        vmem((2 * rows, PAIR), BF),
        vmem((2 * rows, 512), BF),
        vmem((2 * rows, 512), BF),
        vmem((2 * rows, 576), BF),
        vmem((HEADS, rows, PAIR), F32),
        vmem((WIDE, 2 * rows), BF),
        vmem((WIDE, D), F32),
    )

    def finish(x, qkv_m, proj_m, up_m, down_m, *scratch):
        for_tail = copies(tail_sources, (x, qkv_m, proj_m, up_m, down_m), 12)
        for copy in for_tail:
            copy.start()
        leave = pltpu.make_async_copy(gsec, ingrad_out, copy_sems.at[1])
        tail_phase(
            clips, one, two, arrival(for_tail), leave.start, gnorm, own, across_rows, bsum, tok,
            gsec, x, side_ref, cells_ref, taps_ref, vec_ref, mid_sums, one_ref, two_ref, qkv_m,
            proj_m, up_m, down_m, late_ref, scaled_ref, vsum_ref, *tail_landing, *scratch, early,
            *tail_sems,
        )
        leave.wait()

    pl.run_scoped(
        finish,
        *(vmem(ref.shape, ref.dtype) for ref in tail_sources),
        vmem((owned, D), F32),
        vmem((3, 4, 400, D), F32),
        vmem((3, 4, 440, D), F32),
    )
    out_copy.wait()


def rest(mid_inputs, small, back_inputs, tail_inputs, clips, collective_id):
    rows, block = 800, 3 * D // 4
    chunk = share_rows(block, clips)
    owners = -(-block // chunk)
    vector_shape = (40, D)
    vmem = pltpu.VMEM
    dma = pltpu.SemaphoreType.DMA
    parts = [part.stop - part.start for part in EARLY_PARTS]
    hbm = pl.BlockSpec(memory_space=pl.ANY)
    return pl.pallas_call(
        functools.partial(rest_kernel, clips),
        in_specs=[hbm] * 4
        + [pl.BlockSpec(memory_space=pltpu.SMEM)]
        + [VMEM_SPEC] * 4
        + [hbm] * (len(back_inputs) + len(tail_inputs)),
        out_specs=[hbm] * 2 + [VMEM_SPEC] * 5,
        out_shape=[
            jax.ShapeDtypeStruct(mid_inputs[2].shape, BF),
            jax.ShapeDtypeStruct((rows, D), F32),
        ]
        + [
            jax.ShapeDtypeStruct((clips * share_rows(part, clips), D), BF) for part in parts
        ]
        + [
            jax.ShapeDtypeStruct((owners * chunk, D), F32),
            jax.ShapeDtypeStruct((4, SHARE, D), BF),
            jax.ShapeDtypeStruct(vector_shape, F32),
        ],
        scratch_shapes=[
            vmem((rows, D), F32),
            vmem(mid_inputs[2].shape, BF),
            vmem((rows, D), F32),
            vmem((HEADS, rows, PAIR), BF),
            vmem((4, (D + 2 * FF) // 4, D), BF),
            vmem((8, D), F32),
        ]
        + [vmem(ref.shape, ref.dtype) for ref in back_inputs]
        + [
            vmem((rows, D), F32),
            vmem((block, D), F32),
            vmem((block, D), BF),
            vmem((2, HEADS, 1, PAIR), F32),
            vmem((4, block, D), BF),
            vmem((2, block, D), BF),
            vmem((rows, D), BF),
            vmem((2, rows, D), BF),
            vmem((rows, D), BF),
            vmem((rows, D), BF),
            dma((2, 2)),
            dma((2,)),
            dma((2, 2)),
            vmem((block, D), BF),
            vmem((owners, chunk, D), BF),
            vmem((clips, chunk, D), BF),
            vmem((owners, chunk, D), F32),
            vmem((chunk, D), BF),
            vmem((2, 400, D), BF),
            vmem((2, 400, D), BF),
            vmem(vector_shape, F32),
            vmem((4,) + vector_shape, F32),
            vmem(vector_shape, F32),
            vmem((clips,) + vector_shape, F32),
            vmem((4, SHARE, D), BF),
            dma((2,)),
            dma((2, clips)),
            dma((2, clips)),
            dma((5, clips)),
            dma((2, 2)),
            dma((2, 3)),
            dma((2, clips)),
            dma((2, 4)),
            dma((2, 4)),
            dma((17,)),
        ]
        + row_sums_scratch(parts[0], clips)
        + row_sums_scratch(parts[1], clips),
        compiler_params=pltpu.CompilerParams(
            collective_id=collective_id, has_side_effects=True, vmem_limit_bytes=63 * 2**20
        ),
        cost_estimate=pl.CostEstimate(
            flops=2**36, bytes_accessed=32 * 2**20, transcendentals=2**25
        ),
    )(*mid_inputs, *small, *back_inputs, *tail_inputs)


def adamw(param, mean_old, square_old, gradient, rate_value, decay):
    mean_new = 0.9 * mean_old + 0.1 * gradient
    square_new = 0.999 * square_old + 0.001 * gradient * gradient
    mean_hat = mean_new / (1.0 - 0.9**STEP)
    square_hat = square_new / (1.0 - 0.999**STEP)
    return (
        mean_new,
        square_new,
        param - rate_value * (mean_hat / (jnp.sqrt(square_hat) + 1e-08) + decay * param),
    )


RATES = (0.2 * math.sqrt(3.0), 0.12 * math.sqrt(CLIP_TOK), 0.2 * math.sqrt(FF / D), 0.2)


def update_kernel(*refs):
    refs = list(refs)

    def take(count):
        taken, refs[:count] = refs[:count], []
        return taken

    block_in, ingrad_ref, late_ref, one_ref, two_ref, scaled_ref, vsum_ref = take(7)
    weights, moments, vectors, taps, biases = take(4), take(3), take(3), take(3), take(3)
    block_out, out_ref = take(2)
    new_moments, new_weights = take(4), take(4)
    new_vectors, new_taps, new_biases = take(3), take(3), take(3)
    block, sem = take(2)
    into = pltpu.make_async_copy(block_in, block, sem)
    into.start()
    for row in range(20):
        at = slice(20 * row, 20 * row + 20), slice(400 + 20 * row, 420 + 20 * row)
        out_ref[0, row] = jnp.stack([ingrad_ref[part, :] for part in at], axis=1)
    into.wait()
    through = pltpu.make_async_copy(block, block_out, sem)
    through.start()
    rows = weights[0].shape[1]
    new_moments[0][...] = late_ref[0:rows, :].T
    new_weights[0][...] = 0.999 * weights[0][...] - RATES[0] * (
        scaled_ref[0, 0:rows, :].astype(F32).T
    )
    for which in (1, 2, 3):
        rows = weights[which].shape[0]
        summed = one_ref[80:400, :] if which == 2 else (two_ref if which == 3 else one_ref)[0:rows, :]
        new_moments[which][...] = 0.95 * moments[which - 1][...] + summed.astype(F32)
        new_weights[which][...] = 0.999 * weights[which][...] - RATES[which] * scaled_ref[
            which, 0:rows, :
        ].astype(F32)
    bias_sums = vsum_ref[9:13, :]

    def bias_part(part):
        row, column = divmod(part * HEAD_DIM, D)
        return bias_sums[row : row + 1, column : column + HEAD_DIM]

    bias_grad = jnp.concatenate(
        [
            jnp.concatenate([bias_part(2 * r), bias_part(2 * r + 1)], axis=1)
            for r in range(FF // 128)
        ],
        axis=0,
    )
    for (param, mean, square), outs, grad, rate, decay in (
        (vectors, new_vectors, vsum_ref[0:9, :], 0.2, 0.0),
        (taps, new_taps, vsum_ref[13:40, :], 0.05, 0.01),
        (biases, new_biases, bias_grad, 0.2, 0.0),
    ):
        for ref, value in zip(
            outs, adamw(param[...], mean[...], square[...], grad, rate, decay)
        ):
            ref[...] = value
    through.wait()


def update(block, sums, weights, moments, vectors, taps, biases):
    operands = [block, *sums, *weights, *moments[1:], *vectors, *taps, *biases]
    hbm = pl.BlockSpec(memory_space=pl.ANY)
    outs = [jax.ShapeDtypeStruct(block.shape, dtype) for dtype in (BF, F32)]
    outs += [
        jax.ShapeDtypeStruct(x.shape, F32)
        for x in (*moments, *weights, *vectors, *taps, *biases)
    ]
    return pl.pallas_call(
        update_kernel,
        in_specs=[hbm] + [VMEM_SPEC] * (len(operands) - 1),
        out_specs=[hbm] + [VMEM_SPEC] * (len(outs) - 1),
        out_shape=outs,
        scratch_shapes=[pltpu.VMEM(block.shape, BF), pltpu.SemaphoreType.DMA],
        compiler_params=pltpu.CompilerParams(vmem_limit_bytes=62 * 2**20),
        cost_estimate=pl.CostEstimate(
            flops=2**22, bytes_accessed=12 * 2**20, transcendentals=2**14
        ),
    )(*operands)


def frames_last(block):
    return jnp.transpose(block, (0, 2, 3, 1, 4))


def frames_second(block):
    return jnp.transpose(block, (0, 3, 1, 2, 4))


def per_device(
    clips_in,
    out_grad,
    clip_side,
    qkv_weight,
    proj_weight,
    up_weight,
    down_weight,
    qkv_moment,
    proj_moment,
    up_moment,
    down_moment,
    vectors,
    vector_mean,
    vector_square,
    up_bias,
    up_bias_mean,
    up_bias_square,
    conv_kernel,
    kernel_mean,
    kernel_square,
):
    clips = lax.axis_size("clip")
    clips_in, out_grad = frames_last(clips_in), frames_last(out_grad)
    weights = (qkv_weight, proj_weight, up_weight, down_weight)
    moments = (qkv_moment, proj_moment, up_moment, down_moment)
    (
        tokens,
        normed_home,
        normed_cross,
        heads_q,
        home,
        cross,
        kept,
        heads_out,
        query_weight,
        pair_weight,
        other_weights,
    ) = front(clips_in, clip_side, qkv_weight.T, *weights[1:], vectors, conv_kernel, clips, 0)
    block_out, ingrad, sums_one, sums_two, late_moment, scaled, vector_sums = rest(
        (heads_out, tokens, out_grad, other_weights),
        (clip_side, jnp.asarray(CELL_AT), vectors, up_bias.reshape(FF // 128, 128), conv_kernel),
        (
            heads_q,
            kept,
            cross,
            home,
            normed_home,
            normed_cross,
            query_weight,
            pair_weight,
        ),
        (clips_in, qkv_moment.T, *moments[1:]),
        clips,
        1,
    )
    as_rows = lambda vector: vector.reshape(FF // 128, 128)
    updated = update(
        block_out,
        (ingrad, late_moment, sums_one, sums_two, scaled, vector_sums),
        (qkv_weight.T, *weights[1:]),
        (qkv_moment.T, *moments[1:]),
        (vectors, vector_mean, vector_square),
        (conv_kernel, kernel_mean, kernel_square),
        tuple(as_rows(vector) for vector in (up_bias, up_bias_mean, up_bias_square)),
    )
    new_moments = (updated[2].T, *updated[3:6])
    new_weights = (updated[6].T, *updated[7:10])
    outs = [frames_second(updated[0]), frames_second(updated[1])]
    for moment, weight in zip(new_moments, new_weights):
        outs += [moment, weight]
    bias_new = [vector.reshape(FF) for vector in updated[16:19]]
    return (*outs, *updated[10:13], *bias_new, *updated[13:16])


def solution(mesh):
    big = P("clip", "frame", None, None, None)
    rows = P("frame", None)
    return jax.shard_map(
        per_device,
        mesh=mesh,
        in_specs=(big, big, P("clip")) + (rows,) * 8 + (P(),) * 9,
        out_specs=(big, big) + (rows,) * 8 + (P(),) * 9,
        check_vma=False,
    )
```
